32 devices in a mesh: dp: 32 (over z, y, x, core).
Axes of the slice: x: 2, y: 2, z: 4, core: 2. Of those that a mesh axis runs over, the one named last changes fastest.
Arguments:
- hidden_in: bfloat16 [32768, 768], P('dp'), may hold values from -6 to 6
- lengths: int32 [64], P('dp'), may hold values from 128 to 512, as said below
- cotangent: bfloat16 [32768, 768], P('dp'), may hold values from -6 to 6
- proj_qkv: float32 [768, 2304], P('dp'), may hold values from -0.21875 to 0.21875
- proj_attn: float32 [768, 768], P('dp'), may hold values from -1.75 to 1.75
- proj_up: float32 [768, 3072], P('dp'), may hold values from -0.21875 to 0.21875
- proj_down: float32 [3072, 768], P('dp'), may hold values from -0.21875 to 0.21875
- vectors: float32 [9216], P('dp'), may hold values from -1 to 2
- first_qkv: float32 [768, 2304], P('dp'), may hold values from -6 to 6
- first_attn: float32 [768, 768], P('dp'), may hold values from -40 to 40
- first_up: float32 [768, 3072], P('dp'), may hold values from -40 to 40
- first_down: float32 [3072, 768], P('dp'), may hold values from -40 to 40
- first_vectors: float32 [9216], P('dp'), may hold values from -40 to 40
- second_qkv: float32 [768, 2304], P('dp'), may hold values from 0.128 to 2.048
- second_attn: float32 [768, 768], P('dp'), may hold values from 0.16384 to 2.62144
- second_up: float32 [768, 3072], P('dp'), may hold values from 2.048 to 32.768
- second_down: float32 [3072, 768], P('dp'), may hold values from 2.048 to 32.768
- second_vectors: float32 [9216], P('dp'), may hold values from 2.048 to 32.768
Outputs:
- layer_output: bfloat16 [32768, 768], P('dp')
- input_grad: bfloat16 [32768, 768], P('dp')
- next_first_qkv: float32 [768, 2304], P('dp')
- next_second_qkv: float32 [768, 2304], P('dp')
- next_qkv: float32 [768, 2304], P('dp')
- next_first_attn: float32 [768, 768], P('dp')
- next_second_attn: float32 [768, 768], P('dp')
- next_attn: float32 [768, 768], P('dp')
- next_first_up: float32 [768, 3072], P('dp')
- next_second_up: float32 [768, 3072], P('dp')
- next_up: float32 [768, 3072], P('dp')
- next_first_down: float32 [3072, 768], P('dp')
- next_second_down: float32 [3072, 768], P('dp')
- next_down: float32 [3072, 768], P('dp')
- next_first_vectors: float32 [9216], P('dp')
- next_second_vectors: float32 [9216], P('dp')
- next_vectors: float32 [9216], P('dp')
The draws below stay inside these ranges and needn't reach their ends.
Inputs may be any that keep to these rules, and one draw needn't show every extreme that they name: Slot s of a device's 2 * 1 sequences belongs to micro-batch s // 1 of that device. Some sequence has length 512 in every draw; a device's lengths are at least half of a per-device ceiling between 256 and 512.
All inputs are finite; a program needn't handle non-finite values.
Results may differ from the reference program's by a relative error of at most 0.019.
The reference program's roundings to bfloat16 on the way count: a program that leaves them out, or rounds other values in their place, can miss the bound.
Values may be sent and summed in bfloat16 or wider, within the bound.
No kernel may reach another device: no remote copies, remote signals or barrier semaphores. Data moves between devices by JAX's collectives and lax.ppermute only.
A program may use at most 192 MiB of HBM per device.

```python
import math
import jax
import jax.numpy as jnp
from jax import lax

D = 768
HEAD = 64
FF = 3072
SEQ_LEN = 512
BATCH = 1
MICRO = 2
STEP = 10
VEC = 9216
SEQS = 64
TOKENS = 32768


def draw_lengths(key, part):
    key = jax.random.fold_in(key, 11)
    key_cap, key_len, key_pick = jax.random.split(key, 3)
    per_device = MICRO * BATCH
    holders = SEQS // per_device
    ceiling = jax.random.randint(key_cap, (holders, 1), SEQ_LEN // 2, SEQ_LEN + 1)
    lowest = ceiling // 2
    spread = jax.random.randint(key_len, (holders, per_device), 0, 1 << 20)
    drawn = (lowest + spread % (ceiling - lowest + 1)).reshape(-1)
    chosen = jax.random.randint(key_pick, (), 0, SEQS)
    return jnp.where(jnp.arange(SEQS) == chosen, SEQ_LEN, drawn).astype(jnp.int32)


def draw_vectors(key, part):
    key = jax.random.fold_in(key, 23)
    noise = jnp.clip(jax.random.normal(key, (VEC,), jnp.float32), -3.0, 3.0)
    places = jnp.arange(VEC)
    base = 4 * D + FF
    is_gain = (places >= base) & (places < base + D) | (places >= base + 2 * D) & (places < base + 3 * D)
    return jnp.where(is_gain, 1.0 + 0.2 * noise, 0.3 * noise).astype(jnp.float32)


def levels(stream_key, dims, pieces, low, top_value):
    factor_of, own = 1.0, jax.random.fold_in(stream_key, 6)
    for axis_at, blocks in pieces:
        heights = jnp.exp(jax.random.uniform(jax.random.fold_in(own, axis_at), (blocks,), jnp.float32, low / len(pieces), top_value / len(pieces)))
        factor_of = factor_of * jnp.repeat(heights, dims[axis_at] // blocks).reshape([-1 if axis == axis_at else 1 for axis in range(len(dims))])
    return factor_of


def scatter_about(key, shape, scale, limit, shards=(), kind=jnp.bfloat16):
    array = scale * jax.random.normal(key, shape, jnp.float32)
    if shards:
        array = array * levels(key, shape, shards, -0.22, 0.18)
    return jnp.clip(array, -limit, limit).astype(kind)


def setup_inputs(seed: int = 0) -> dict:
    splits = jax.random.split(jax.random.key(seed), 19)
    hidden_in = scatter_about(splits[0], (TOKENS, D), 1.0, 6.0, ((0, 32),))
    lengths = draw_lengths(jax.random.fold_in(splits[18], 71), 0)
    cotangent = scatter_about(splits[2], (TOKENS, D), 1.0, 6.0, ((0, 32),))
    proj_qkv = scatter_about(splits[3], (D, 3 * D), D ** -0.5, 0.21875, ((0, 32),), jnp.float32)
    proj_attn = scatter_about(splits[4], (D, D), (D // 64) ** -0.5, 1.75, ((0, 32),), jnp.float32)
    proj_up = scatter_about(splits[5], (D, FF), D ** -0.5, 0.21875, ((0, 32),), jnp.float32)
    proj_down = scatter_about(splits[6], (FF, D), (FF // 4) ** -0.5, 0.21875, ((0, 32),), jnp.float32)
    vectors = draw_vectors(jax.random.fold_in(splits[18], 71), 0)
    first_qkv = scatter_about(splits[8], (D, 3 * D), (0.03 * (SEQS * SEQ_LEN / 8) ** 0.5), 6.0, ((0, 32),), jnp.float32)
    first_attn = scatter_about(splits[9], (D, D), (0.11 * (SEQS * SEQ_LEN / 8) ** 0.5), 40.0, ((0, 32),), jnp.float32)
    first_up = scatter_about(splits[10], (D, FF), (0.11 * (SEQS * SEQ_LEN / 8) ** 0.5), 40.0, ((0, 32),), jnp.float32)
    first_down = scatter_about(splits[11], (FF, D), (0.11 * (SEQS * SEQ_LEN / 8) ** 0.5), 40.0, ((0, 32),), jnp.float32)
    first_vectors = scatter_about(splits[12], (VEC,), (0.11 * (SEQS * SEQ_LEN / 8) ** 0.5), 40.0, ((0, 32),), jnp.float32)
    second_qkv = jnp.clip(jnp.exp(math.log(2.048) - 2.7725887 * jax.random.uniform(splits[13], (D, 3 * D), jnp.float32) ** levels(splits[13], (D, 3 * D), ((0, 32),), -0.2, 0.2)), 0.128, 2.048)
    second_attn = jnp.clip(jnp.exp(math.log(2.62144) - 2.7725887 * jax.random.uniform(splits[14], (D, D), jnp.float32) ** levels(splits[14], (D, D), ((0, 32),), -0.2, 0.2)), 0.16384, 2.62144)
    second_up = jnp.clip(jnp.exp(math.log(32.768) - 2.7725887 * jax.random.uniform(splits[15], (D, FF), jnp.float32) ** levels(splits[15], (D, FF), ((0, 32),), -0.2, 0.2)), 2.048, 32.768)
    second_down = jnp.clip(jnp.exp(math.log(32.768) - 2.7725887 * jax.random.uniform(splits[16], (FF, D), jnp.float32) ** levels(splits[16], (FF, D), ((0, 32),), -0.2, 0.2)), 2.048, 32.768)
    second_vectors = jnp.clip(jnp.exp(math.log(32.768) - 2.7725887 * jax.random.uniform(splits[17], (VEC,), jnp.float32) ** levels(splits[17], (VEC,), ((0, 32),), -0.2, 0.2)), 2.048, 32.768)
    return {"hidden_in": hidden_in, "lengths": lengths, "cotangent": cotangent, "proj_qkv": proj_qkv, "proj_attn": proj_attn, "proj_up": proj_up, "proj_down": proj_down, "vectors": vectors, "first_qkv": first_qkv, "first_attn": first_attn, "first_up": first_up, "first_down": first_down, "first_vectors": first_vectors, "second_qkv": second_qkv, "second_attn": second_attn, "second_up": second_up, "second_down": second_down, "second_vectors": second_vectors}


@jax.custom_vjp
def low(v):
    return lax.optimization_barrier(v.astype(jnp.bfloat16)).astype(jnp.float32)

@jax.custom_vjp
def low_back(v):
    return v

def low_keep(v):
    return (low(v), None)

def low_pass(kept, grad):
    return (grad,)

def back_keep(v):
    return (v, None)

def back_low(kept, grad):
    return (low(grad),)
low.defvjp(low_keep, low_pass)
low_back.defvjp(back_keep, back_low)
EPSILON_NORM = 1e-05
BETA_ONE = 0.9
BETA_TWO = 0.999
LEARN_RATE = 0.1
LEARN_RATE_VECTOR = 0.4
WEIGHT_DECAY = 0.01
EPSILON_ADAM = 1e-08
HIGHEST = lax.Precision.HIGHEST

def matmul(left_arr, right_arr):
    return jnp.dot(left_arr, right_arr, precision=HIGHEST, preferred_element_type=jnp.float32)

def gelu_exact(upper):
    return 0.5 * upper * (1.0 + jax.scipy.special.erf(upper * (1.0 / math.sqrt(2.0))))

def normalize(resid, gain, shift):
    centred = resid - lax.optimization_barrier(jnp.mean(resid, axis=-1, keepdims=True))
    scaled = centred * lax.rsqrt(lax.optimization_barrier(jnp.mean(centred * centred, axis=-1, keepdims=True)) + EPSILON_NORM)
    return scaled * gain + shift

def attend(packed, length):
    width = packed.shape[1] // 3
    seq_len = packed.shape[0]
    query = packed[:, :width].reshape(seq_len, width // HEAD, HEAD)
    keyset = packed[:, width:2 * width].reshape(seq_len, width // HEAD, HEAD)
    valset = packed[:, 2 * width:].reshape(seq_len, width // HEAD, HEAD)
    scores = low_back(jnp.einsum('qhd,khd->hqk', query, keyset, precision=HIGHEST) * (1.0 / math.sqrt(HEAD)))
    alive = jnp.arange(seq_len) < length
    scores = jnp.where(alive[None, None, :], scores, -1e+30)
    highest = lax.optimization_barrier(jnp.max(scores, axis=-1, keepdims=True))
    expo = jnp.exp(scores - highest)
    probs = expo / lax.optimization_barrier(jnp.sum(expo, axis=-1, keepdims=True))
    mixed = jnp.einsum('hqk,khd->qhd', low(probs), valset, precision=HIGHEST)
    return mixed.reshape(seq_len, width)

def layer(params, hidden, seq_lengths):
    w_qkv, w_attn, w_up, w_down, vector = [low(param_arr) for param_arr in params]
    width = hidden.shape[1]
    inner = w_up.shape[1]
    base = 3 * width + inner
    q_bias = vector[:width]
    v_bias = vector[width:2 * width]
    attn_bias = vector[2 * width:3 * width]
    up_bias = vector[3 * width:base]
    down_bias = vector[base:base + width]
    gain_one = vector[base + width:base + 2 * width]
    shift_one = vector[base + 2 * width:base + 3 * width]
    gain_two = vector[base + 3 * width:base + 4 * width]
    shift_two = vector[base + 4 * width:base + 5 * width]
    packed = low(low_back(matmul(hidden, w_qkv) + jnp.concatenate([q_bias, jnp.zeros_like(q_bias), v_bias])))
    groups = seq_lengths.shape[0]
    seq_len = hidden.shape[0] // groups
    mixed = lax.map(jax.checkpoint(lambda paired: attend(paired[0], paired[1])), (packed.reshape(groups, seq_len, 3 * width), seq_lengths))
    mixed = low(low_back(mixed.reshape(groups * seq_len, width)))
    resid_one = hidden + low_back(matmul(mixed, w_attn) + attn_bias)
    first = normalize(resid_one, gain_one, shift_one)
    upper = low_back(matmul(low(first), w_up) + up_bias)
    active = low(gelu_exact(upper))
    resid_two = first + low_back(matmul(active, w_down) + down_bias)
    return normalize(resid_two, gain_two, shift_two)

def adamw(weight, grad, first, second, decay, rate):
    new_first = BETA_ONE * first + (1.0 - BETA_ONE) * grad
    new_second = BETA_TWO * second + (1.0 - BETA_TWO) * grad * grad
    corrected = new_first / (1.0 - BETA_ONE ** STEP)
    scale_sq = new_second / (1.0 - BETA_TWO ** STEP)
    new_weight = weight - rate * (corrected / (jnp.sqrt(scale_sq) + EPSILON_ADAM) + decay * weight)
    return (new_first, new_second, new_weight)

def reference(hidden_in, lengths, cotangent, proj_qkv, proj_attn, proj_up, proj_down, vectors, first_qkv, first_attn, first_up, first_down, first_vectors, second_qkv, second_attn, second_up, second_down, second_vectors):
    per_group = MICRO * BATCH
    groups = SEQS // per_group
    width = hidden_in.shape[1]
    rows_group = per_group * SEQ_LEN
    inputs = hidden_in.astype(jnp.float32).reshape(groups, rows_group, width)
    backs = cotangent.astype(jnp.float32).reshape(groups, rows_group, width)
    spans = lengths.reshape(groups, per_group)
    params = (proj_qkv, proj_attn, proj_up, proj_down, vectors)

    def one_group(running, group_item):
        hidden, seq_lengths, cot_rows = group_item
        alive = (jnp.arange(SEQ_LEN)[None, :] < seq_lengths[:, None]).reshape(-1)
        output, pull = jax.vjp(lambda values, rows: layer(values, rows, seq_lengths), params, hidden)
        gradients, grad_rows = pull(cot_rows * alive[:, None].astype(cot_rows.dtype))
        running = tuple((accum_arr + update for accum_arr, update in zip(running, gradients)))
        return (running, (output.astype(jnp.bfloat16), grad_rows.astype(jnp.bfloat16)))
    start = tuple((jnp.zeros_like(param_arr) for param_arr in params))
    totals, (outputs, grad_rows) = lax.scan(one_group, start, (inputs, spans, backs))
    m_qkv, v_qkv, w_qkv = adamw(proj_qkv, totals[0], first_qkv, second_qkv, WEIGHT_DECAY, LEARN_RATE)
    m_attn, v_attn, w_attn = adamw(proj_attn, totals[1], first_attn, second_attn, WEIGHT_DECAY, LEARN_RATE)
    m_up, v_up, w_up = adamw(proj_up, totals[2], first_up, second_up, WEIGHT_DECAY, LEARN_RATE)
    m_down, v_down, w_down = adamw(proj_down, totals[3], first_down, second_down, WEIGHT_DECAY, LEARN_RATE)
    m_vec, v_vec, w_vec = adamw(vectors, totals[4], first_vectors, second_vectors, 0.0, LEARN_RATE_VECTOR)
    return (outputs.reshape(-1, width), grad_rows.reshape(-1, width), m_qkv, v_qkv, w_qkv, m_attn, v_attn, w_attn, m_up, v_up, w_up, m_down, v_down, w_down, m_vec, v_vec, w_vec)
```

```python
import functools
import math

import jax
import jax.numpy as jnp
from jax import lax
from jax.experimental import pallas as pl
from jax.experimental.pallas import tpu as pltpu
from jax.sharding import PartitionSpec as P

HEAD = 64
STEP = 10

EPSILON_NORM = 1e-05
BETA_ONE = 0.9
BETA_TWO = 0.999
LEARN_RATE = 0.1
LEARN_RATE_VECTOR = 0.4
WEIGHT_DECAY = 0.01
EPSILON_ADAM = 1e-08

LANES = 128
ROWS = 256
GROUPS = 2
VMEM_BYTES = 56 * 1024 * 1024
BF = jnp.bfloat16
F32 = jnp.float32

NN = (((1,), (0,)), ((), ()))
NT = (((1,), (1,)), ((), ()))
TN = (((0,), (0,)), ((), ()))


def dot(left, right, dims=NN):
    return lax.dot_general(left, right, dims, preferred_element_type=F32)


def params(grid_rank):
    return pltpu.CompilerParams(
        dimension_semantics=("arbitrary",) * grid_rank, vmem_limit_bytes=VMEM_BYTES
    )


def cost(flops, moved, exps=0):
    return pl.CostEstimate(flops=int(flops), bytes_accessed=int(moved), transcendentals=int(exps))


def qkv_kernel(x_ref, w_ref, vec_ref, out_ref):
    width = x_ref.shape[1]
    x = x_ref[...]
    for part in range(3):
        cols = pl.ds(part * width, width)
        value = dot(x, w_ref[:, cols])
        if part == 0:
            value = value + vec_ref[0:1, :]
        if part == 2:
            value = value + vec_ref[1:2, :]
        out_ref[:, cols] = value.astype(BF)


def project_qkv(x, gathered, vec):
    rows, width = x.shape
    return pl.pallas_call(
        qkv_kernel,
        grid=(rows // ROWS,),
        in_specs=[
            pl.BlockSpec((ROWS, width), lambda i: (i, 0)),
            pl.BlockSpec((width, 3 * width), lambda i: (0, 0), pipeline_mode=pl.Buffered(1)),
            pl.BlockSpec(vec.shape, lambda i: (0, 0)),
        ],
        out_specs=pl.BlockSpec((ROWS, 3 * width), lambda i: (i, 0)),
        out_shape=jax.ShapeDtypeStruct((rows, 3 * width), BF),
        compiler_params=params(1),
        cost_estimate=cost(6 * rows * width * width, 2 * (4 * rows * width + 3 * width * width)),
        name="project_qkv",
    )(x, gathered, vec)


def attend_kernel(len_ref, q_ref, k_ref, v_ref, out_ref, lse_ref):
    length = len_ref[pl.program_id(0)]
    seq = q_ref.shape[0]
    query = q_ref[...] * jnp.asarray(1.0 / math.sqrt(HEAD), BF)
    keyset = k_ref[...]
    val_t = v_ref[...].T
    lane = lax.broadcasted_iota(jnp.int32, (seq, LANES), 1)
    alive = lax.broadcasted_iota(jnp.int32, (seq, seq), 0) < length
    mixed = []
    for head in range(2):
        mine = (lane < HEAD) if head == 0 else (lane >= HEAD)
        scores = dot(keyset, jnp.where(mine, query, jnp.zeros_like(query)), NT)
        scores = jnp.where(alive, scores, -1e30)
        highest = jnp.max(scores, axis=0, keepdims=True)
        expo = jnp.exp(scores - highest)
        summed = jnp.sum(expo, axis=0, keepdims=True)
        probs = (expo * (1.0 / summed)).astype(BF)
        mixed.append(dot(val_t[head * HEAD : (head + 1) * HEAD], probs))
        lse_ref[0, head : head + 1, :] = highest + jnp.log(summed)
    out_ref[...] = jnp.concatenate(mixed, axis=0).T.astype(BF)


def attend_forward(packed, lengths, width):
    rows = packed.shape[0]
    batch = lengths.shape[0]
    seq = rows // batch
    pairs = width // LANES
    grid_spec = pltpu.PrefetchScalarGridSpec(
        num_scalar_prefetch=1,
        grid=(batch, pairs),
        in_specs=[
            pl.BlockSpec((seq, LANES), lambda b, h, ln: (b, h)),
            pl.BlockSpec((seq, LANES), lambda b, h, ln: (b, pairs + h)),
            pl.BlockSpec((seq, LANES), lambda b, h, ln: (b, 2 * pairs + h)),
        ],
        out_specs=[
            pl.BlockSpec((seq, LANES), lambda b, h, ln: (b, h)),
            pl.BlockSpec((1, 2, seq), lambda b, h, ln: (b * pairs + h, 0, 0)),
        ],
    )
    return pl.pallas_call(
        attend_kernel,
        grid_spec=grid_spec,
        out_shape=[
            jax.ShapeDtypeStruct((rows, width), BF),
            jax.ShapeDtypeStruct((batch * pairs, 2, seq), F32),
        ],
        compiler_params=params(2),
        cost_estimate=cost(16 * rows * seq * width, 8 * rows * width, rows * seq * width // HEAD),
        name="attend_forward",
    )(lengths, packed, packed, packed)


def attend_back_kernel(len_ref, q_ref, k_ref, v_ref, g_ref, lse_ref, out_ref):
    length = len_ref[pl.program_id(0)]
    seq = q_ref.shape[0]
    factor = 1.0 / math.sqrt(HEAD)
    query = q_ref[...] * jnp.asarray(factor, BF)
    keyset = k_ref[...]
    valset = v_ref[...]
    grad = g_ref[...]
    key_t = keyset.T
    lane = lax.broadcasted_iota(jnp.int32, (seq, LANES), 1)
    alive = lax.broadcasted_iota(jnp.int32, (seq, seq), 0) < length
    grad_q = []
    grad_k = 0.0
    grad_v = 0.0
    for head in range(2):
        mine = (lane < HEAD) if head == 0 else (lane >= HEAD)
        query_h = jnp.where(mine, query, jnp.zeros_like(query))
        grad_h = jnp.where(mine, grad, jnp.zeros_like(grad))
        scores = jnp.where(alive, dot(keyset, query_h, NT), -1e30)
        probs = jnp.exp(scores - lse_ref[0, head : head + 1, :])
        grad_probs = dot(valset, grad_h, NT)
        total = jnp.sum(probs * grad_probs, axis=0, keepdims=True)
        grad_scores = (probs * (grad_probs - total)).astype(BF)
        grad_v = grad_v + dot(probs.astype(BF), grad_h)
        grad_k = grad_k + dot(grad_scores, query_h)
        grad_q.append(dot(key_t[head * HEAD : (head + 1) * HEAD], grad_scores))
    out_ref[0] = (jnp.concatenate(grad_q, axis=0).T * factor).astype(BF)
    out_ref[1] = grad_k.astype(BF)
    out_ref[2] = grad_v.astype(BF)


def attend_backward(packed, lengths, lse, grad_mixed, group):
    rows, width = grad_mixed.shape
    batch = lengths.shape[0]
    seq = rows // batch
    pairs = width // LANES
    here = pairs // GROUPS
    base = group * here
    grid_spec = pltpu.PrefetchScalarGridSpec(
        num_scalar_prefetch=1,
        grid=(batch, here),
        in_specs=[
            pl.BlockSpec((seq, LANES), lambda b, h, ln: (b, base + h)),
            pl.BlockSpec((seq, LANES), lambda b, h, ln: (b, pairs + base + h)),
            pl.BlockSpec((seq, LANES), lambda b, h, ln: (b, 2 * pairs + base + h)),
            pl.BlockSpec((seq, LANES), lambda b, h, ln: (b, base + h)),
            pl.BlockSpec((1, 2, seq), lambda b, h, ln: (b * pairs + base + h, 0, 0)),
        ],
        out_specs=pl.BlockSpec((3, seq, LANES), lambda b, h, ln: (0, b, h)),
    )
    return pl.pallas_call(
        attend_back_kernel,
        grid_spec=grid_spec,
        out_shape=jax.ShapeDtypeStruct((3, rows, here * LANES), BF),
        compiler_params=params(2),
        cost_estimate=cost(
            40 * rows * seq * here * LANES,
            14 * rows * here * LANES,
            rows * seq * here * 2,
        ),
        name="attend_backward",
    )(lengths, packed, packed, packed, grad_mixed, lse)


def norm_forward(resid, gain, shift):
    centred = resid - jnp.mean(resid, axis=-1, keepdims=True)
    inverse = lax.rsqrt(jnp.mean(centred * centred, axis=-1, keepdims=True) + EPSILON_NORM)
    scaled = centred * inverse
    return (scaled * gain + shift, scaled, inverse)


def norm_backward(grad, scaled, inverse, gain):
    grad_scaled = grad * gain
    return inverse * (
        grad_scaled
        - jnp.mean(grad_scaled, axis=-1, keepdims=True)
        - scaled * jnp.mean(grad_scaled * scaled, axis=-1, keepdims=True)
    )


def column_sum(value):
    return jnp.sum(value, axis=0, keepdims=True)


def middle_kernel(
    len_ref,
    x_ref,
    mixed_ref,
    cot_ref,
    w_attn,
    w_up,
    w_down,
    vec_ref,
    out_ref,
    first_ref,
    active_ref,
    upper_ref,
    branch_ref,
    attn_ref,
    gmix_ref,
    resid_ref,
    sum_ref,
    slope_ref,
    *,
    seq,
):
    step = pl.program_id(0)
    rows, width = x_ref.shape
    chunks = w_up.shape[1] // width
    start = (step * rows) % seq
    length = len_ref[(step * rows) // seq]

    def vec(index):
        return vec_ref[index : index + 1, :]

    gain_one, shift_one, gain_two, shift_two = vec(8), vec(9), vec(10), vec(11)

    @pl.when(step == 0)
    def _():
        sum_ref[...] = jnp.zeros_like(sum_ref)

    resid_one = x_ref[...].astype(F32) + dot(mixed_ref[...], w_attn[...]) + vec(2)
    first, scaled_one, inverse_one = norm_forward(resid_one, gain_one, shift_one)
    first_low = first.astype(BF)
    first_ref[...] = first_low
    total = first + vec(7)
    for j in range(chunks):
        cols = pl.ds(j * width, width)
        upper = dot(first_low, w_up[:, cols]) + vec(3 + j)
        half = 0.5 + 0.5 * lax.erf(upper * (1.0 / math.sqrt(2.0)))
        active = (upper * half).astype(BF)
        active_ref[:, cols] = active
        slope_ref[:, cols] = half + upper * jnp.exp(-0.5 * upper * upper) * (
            1.0 / math.sqrt(2.0 * math.pi)
        )
        total = total + dot(active, w_down[cols, :])
    output, scaled_two, inverse_two = norm_forward(total, gain_two, shift_two)
    out_ref[...] = output.astype(BF)

    @pl.when(start < length)
    def _():
        alive = lax.broadcasted_iota(jnp.int32, (rows, 1), 0) + start < length
        grad_out = jnp.where(alive, cot_ref[...].astype(F32), 0.0)
        grad_two = norm_backward(grad_out, scaled_two, inverse_two, gain_two)
        branch = grad_two.astype(BF)
        branch_ref[...] = branch
        grad_first = grad_two
        for j in range(chunks):
            cols = pl.ds(j * width, width)
            grad_upper = (dot(branch, w_down[cols, :], NT) * slope_ref[:, cols]).astype(BF)
            upper_ref[:, cols] = grad_upper
            sum_ref[3 + j : 4 + j, :] += column_sum(grad_upper.astype(F32))
            grad_first = grad_first + dot(grad_upper, w_up[:, cols], NT)
        grad_one = norm_backward(grad_first, scaled_one, inverse_one, gain_one)
        resid_ref[...] = grad_one
        grad_attn = grad_one.astype(BF)
        attn_ref[...] = grad_attn
        gmix_ref[...] = dot(grad_attn, w_attn[...], NT).astype(BF)
        sum_ref[2:3, :] += column_sum(grad_attn.astype(F32))
        sum_ref[7:8, :] += column_sum(branch.astype(F32))
        sum_ref[8:9, :] += column_sum(grad_first * scaled_one)
        sum_ref[9:10, :] += column_sum(grad_first)
        sum_ref[10:11, :] += column_sum(grad_out * scaled_two)
        sum_ref[11:12, :] += column_sum(grad_out)

    @pl.when(start >= length)
    def _():
        upper_ref[...] = jnp.zeros_like(upper_ref)
        branch_ref[...] = jnp.zeros_like(branch_ref)
        attn_ref[...] = jnp.zeros_like(attn_ref)
        gmix_ref[...] = jnp.zeros_like(gmix_ref)
        resid_ref[...] = jnp.zeros_like(resid_ref)


def middle(x, mixed, cotangent, lengths, gathered, w_down, vec):
    rows, width = x.shape
    inner = w_down.shape[0]
    seq = rows // lengths.shape[0]
    once = pl.Buffered(1)
    thin = pl.BlockSpec((ROWS, width), lambda i, ln: (i, 0))
    wide = pl.BlockSpec((ROWS, inner), lambda i, ln: (i, 0))
    grid_spec = pltpu.PrefetchScalarGridSpec(
        num_scalar_prefetch=1,
        grid=(rows // ROWS,),
        in_specs=[
            thin,
            thin,
            thin,
            pl.BlockSpec((width, width), lambda i, ln: (0, 3), pipeline_mode=once),
            pl.BlockSpec((width, inner), lambda i, ln: (0, 1), pipeline_mode=once),
            pl.BlockSpec((inner, width), lambda i, ln: (0, 0), pipeline_mode=once),
            pl.BlockSpec(vec.shape, lambda i, ln: (0, 0)),
        ],
        out_specs=[
            thin,
            thin,
            wide,
            wide,
            thin,
            thin,
            thin,
            thin,
            pl.BlockSpec(vec.shape, lambda i, ln: (0, 0)),
        ],
        scratch_shapes=[pltpu.VMEM((ROWS, inner), F32)],
    )
    low = jax.ShapeDtypeStruct((rows, width), BF)
    low_wide = jax.ShapeDtypeStruct((rows, inner), BF)
    return pl.pallas_call(
        functools.partial(middle_kernel, seq=seq),
        grid_spec=grid_spec,
        out_shape=[
            low,
            low,
            low_wide,
            low_wide,
            low,
            low,
            low,
            jax.ShapeDtypeStruct((rows, width), F32),
            jax.ShapeDtypeStruct(vec.shape, F32),
        ],
        compiler_params=params(1),
        cost_estimate=cost(
            8 * rows * width * inner + 4 * rows * width * width,
            rows * (4 * inner + 20 * width) + 4 * width * inner,
            2 * rows * inner,
        ),
        name="middle",
    )(lengths, x, mixed, cotangent, gathered, gathered, w_down, vec)


def weight_kernel(src_ref, left_ref, right_ref, *refs, sums):
    keep_ref, send_ref, acc_ref = refs[0], refs[1], refs[-1]
    half, piece, _ = keep_ref.shape
    right = right_ref[0] if len(right_ref.shape) == 3 else right_ref[...]
    acc_ref[...] = dot(left_ref[...], right, TN)
    if sums:
        refs[2][0] = jnp.broadcast_to(column_sum(right.astype(F32)), refs[2].shape[1:])
    for slot in range(half):
        for ref, offset in ((keep_ref, 0), (send_ref, half)):
            begin = pl.multiple_of(src_ref[offset + slot] * piece, 8)
            ref[slot] = acc_ref[pl.ds(begin, piece), :].astype(BF)


def plain_weight_kernel(left_ref, right_ref, out_ref, *refs):
    right = right_ref[0] if len(right_ref.shape) == 3 else right_ref[...]
    out_ref[...] = dot(left_ref[...], right, TN).astype(BF)
    if refs:
        refs[0][0] = jnp.broadcast_to(column_sum(right.astype(F32)), refs[0].shape[1:])


def weight_gradient(left, right, source, sums=False):
    rows, tall = left.shape
    devices = source.shape[0]
    piece = tall // devices
    if right.ndim == 3:
        steps, _, tile = right.shape
        right_block = pl.BlockSpec((1, rows, tile), lambda j, *s: (j, 0, 0))
    else:
        tile = min(right.shape[1], 768)
        steps = right.shape[1] // tile
        right_block = pl.BlockSpec((rows, tile), lambda j, *s: (0, j))
    left_block = pl.BlockSpec((rows, tall), lambda j, *s: (0, 0))
    extra_specs = [pl.BlockSpec((1, 8, tile), lambda j, *s: (j, 0, 0))] if sums else []
    extra_shapes = [jax.ShapeDtypeStruct((steps, 8, tile), F32)] if sums else []
    estimate = cost(2 * rows * tall * tile * steps, 2 * tall * tile * steps + 2 * rows * (tall + tile * steps))
    if piece % 8:
        whole, *rest = pl.pallas_call(
            plain_weight_kernel,
            grid=(steps,),
            in_specs=[left_block, right_block],
            out_specs=[pl.BlockSpec((tall, tile), lambda j: (0, j))] + extra_specs,
            out_shape=[jax.ShapeDtypeStruct((tall, steps * tile), BF)] + extra_shapes,
            compiler_params=params(1),
            cost_estimate=estimate,
            name="weight_gradient",
        )(left, right)
        ordered = jnp.take(whole.reshape(devices, piece, steps * tile), source, axis=0)
        return (ordered[: devices // 2], ordered[devices // 2 :], *rest)
    block = pl.BlockSpec((devices // 2, piece, tile), lambda j, s: (0, 0, j))
    shape = jax.ShapeDtypeStruct((devices // 2, piece, steps * tile), BF)
    grid_spec = pltpu.PrefetchScalarGridSpec(
        num_scalar_prefetch=1,
        grid=(steps,),
        in_specs=[left_block, right_block],
        out_specs=[block, block] + extra_specs,
        scratch_shapes=[pltpu.VMEM((tall, tile), F32)],
    )
    return pl.pallas_call(
        functools.partial(weight_kernel, sums=sums),
        grid_spec=grid_spec,
        out_shape=[shape, shape] + extra_shapes,
        compiler_params=params(1),
        cost_estimate=estimate,
        name="weight_gradient",
    )(source, left, right)


def tall_kernel(slot_ref, left_ref, right_ref, keep_ref, send_ref, acc_ref):
    step = pl.program_id(0)
    half, piece, _ = keep_ref.shape
    here = left_ref.shape[1] // piece
    acc_ref[...] = dot(left_ref[...], right_ref[...], TN)
    for index in range(here):
        slot = slot_ref[step * here + index]
        part = acc_ref[index * piece : (index + 1) * piece, :].astype(BF)

        @pl.when(slot < half)
        def _():
            keep_ref[jnp.minimum(slot, half - 1)] = part

        @pl.when(slot >= half)
        def _():
            send_ref[jnp.maximum(slot - half, 0)] = part


def plain_tall_kernel(left_ref, right_ref, out_ref):
    out_ref[...] = dot(left_ref[...], right_ref[...], TN).astype(BF)


def tall_gradient(left, right, source, slot_of):
    rows, tall = left.shape
    width = right.shape[1]
    devices = source.shape[0]
    piece = tall // devices
    steps = tall // width
    left_block = pl.BlockSpec((rows, width), lambda j, *s: (0, j))
    right_block = pl.BlockSpec((rows, width), lambda j, *s: (0, 0))
    estimate = cost(2 * rows * tall * width, 2 * tall * width + 2 * rows * (tall + width))
    if piece % 16:
        whole = pl.pallas_call(
            plain_tall_kernel,
            grid=(steps,),
            in_specs=[left_block, right_block],
            out_specs=pl.BlockSpec((width, width), lambda j: (j, 0)),
            out_shape=jax.ShapeDtypeStruct((tall, width), BF),
            compiler_params=params(1),
            cost_estimate=estimate,
            name="tall_gradient",
        )(left, right)
        ordered = jnp.take(whole.reshape(devices, piece, width), source, axis=0)
        return (ordered[: devices // 2], ordered[devices // 2 :])
    block = pl.BlockSpec((devices // 2, piece, width), lambda j, s: (0, 0, 0))
    shape = jax.ShapeDtypeStruct((devices // 2, piece, width), BF)
    grid_spec = pltpu.PrefetchScalarGridSpec(
        num_scalar_prefetch=1,
        grid=(steps,),
        in_specs=[left_block, right_block],
        out_specs=[block, block],
        scratch_shapes=[pltpu.VMEM((width, width), F32)],
    )
    return pl.pallas_call(
        tall_kernel,
        grid_spec=grid_spec,
        out_shape=[shape, shape],
        compiler_params=params(1),
        cost_estimate=estimate,
        name="tall_gradient",
    )(slot_of, left, right)


def input_kernel(resid_ref, w_ref, *refs):
    out_ref = refs[-1]
    width = resid_ref.shape[1]
    total = resid_ref[...]
    for group, grad_ref in enumerate(refs[:-1]):
        here = grad_ref.shape[2]
        for part in range(3):
            total = total + dot(grad_ref[part], w_ref[:, pl.ds(part * width + group * here, here)], NT)
    out_ref[...] = total.astype(BF)


def input_gradient(resid, gathered, grads):
    rows, width = resid.shape
    return pl.pallas_call(
        input_kernel,
        grid=(rows // ROWS,),
        in_specs=[
            pl.BlockSpec((ROWS, width), lambda i: (i, 0)),
            pl.BlockSpec((width, 3 * width), lambda i: (0, 0), pipeline_mode=pl.Buffered(1)),
        ]
        + [pl.BlockSpec((3, ROWS, grad.shape[2]), lambda i: (0, i, 0)) for grad in grads],
        out_specs=pl.BlockSpec((ROWS, width), lambda i: (i, 0)),
        out_shape=jax.ShapeDtypeStruct((rows, width), BF),
        compiler_params=params(1),
        cost_estimate=cost(6 * rows * width * width, 12 * rows * width + 6 * width * width),
        name="input_gradient",
    )(resid, gathered, *grads)


def stages(devices):
    bits = devices.bit_length() - 1
    found = [(0, 1)]
    at = 1
    while at < bits:
        count = min(2, bits - at)
        found.append((at, count))
        at += count
    return found


def relative_order(devices):
    order = [0]
    for at, count in stages(devices):
        order = [base | (value << at) for base in order for value in range(1 << count)]
    return order


def swap(value, mask, devices):
    return lax.ppermute(value, "dp", [(index, index ^ mask) for index in range(devices)])


def sum_of(terms, begin, size):
    total = terms[0][begin : begin + size].astype(F32)
    for term in terms[1:]:
        total = total + term[begin : begin + size].astype(F32)
    return total


def reduce_to_owner(keep, send, devices):
    terms = [keep, swap(send, 1, devices)]
    for at, count in stages(devices)[1:]:
        size = terms[0].shape[0] >> count
        parts = [
            sum_of(terms, value * size, size).astype(keep.dtype) for value in range(1 << count)
        ]
        terms = [parts[0]] + [
            swap(parts[value], value << at, devices) for value in range(1, 1 << count)
        ]
    return sum_of(terms, 0, 1)[0]


def adamw(weight, grad, first, second, decay, rate):
    new_first = BETA_ONE * first + (1.0 - BETA_ONE) * grad
    new_second = BETA_TWO * second + (1.0 - BETA_TWO) * grad * grad
    corrected = new_first / (1.0 - BETA_ONE**STEP)
    scale_sq = new_second / (1.0 - BETA_TWO**STEP)
    new_weight = weight - rate * (corrected / (jnp.sqrt(scale_sq) + EPSILON_ADAM) + decay * weight)
    return (new_first, new_second, new_weight)


def on_device(
    hidden_in,
    lengths,
    cotangent,
    proj_qkv,
    proj_attn,
    proj_up,
    proj_down,
    vectors,
    first_qkv,
    first_attn,
    first_up,
    first_down,
    first_vectors,
    second_qkv,
    second_attn,
    second_up,
    second_down,
    second_vectors,
):
    devices = lax.axis_size("dp")
    me = lax.axis_index("dp")
    width = hidden_in.shape[1]
    piece = proj_qkv.shape[0]
    inner = proj_up.shape[1]
    ratio = inner // width
    relative = jnp.asarray(relative_order(devices), jnp.int32)
    source = relative ^ me
    slots = [0] * devices
    for slot, value in enumerate(relative_order(devices)):
        slots[value] = slot
    slot_of = jnp.take(jnp.asarray(slots, jnp.int32), jnp.arange(devices, dtype=jnp.int32) ^ me)

    entries = vectors.shape[0] // piece
    shard = jnp.concatenate(
        [
            proj_qkv.astype(BF),
            proj_attn.astype(BF),
            proj_up.astype(BF),
            proj_down.astype(BF).reshape(ratio, piece, width).transpose(1, 0, 2).reshape(piece, inner),
            jnp.pad(vectors.astype(BF).reshape(piece, entries), ((0, 0), (0, LANES - entries))),
        ],
        axis=1,
    )
    gathered = lax.all_gather(shard, "dp", axis=0, tiled=True)
    base = 4 * width + inner
    w_down = (
        gathered[:, base : base + inner]
        .reshape(devices, piece, ratio, width)
        .transpose(0, 2, 1, 3)
        .reshape(inner, width)
    )
    vec = gathered[:, base + inner : base + inner + entries].astype(F32).reshape(-1, width)

    packed = project_qkv(hidden_in, gathered, vec)
    mixed, lse = attend_forward(packed, lengths, width)
    output, first_low, active, grad_upper, grad_branch, grad_attn, grad_mixed, grad_one, sums = middle(
        hidden_in, mixed, cotangent, lengths, gathered, w_down, vec
    )
    total_down = reduce_to_owner(*tall_gradient(active, grad_branch, source, slot_of), devices)
    total_up = reduce_to_owner(*weight_gradient(first_low, grad_upper, source), devices)
    total_attn = reduce_to_owner(*weight_gradient(mixed, grad_attn, source), devices)
    totals = []
    parts = []
    part_sums = []
    for group in range(GROUPS):
        part = attend_backward(packed, lengths, lse, grad_mixed, group)
        keep, send, part_sum = weight_gradient(hidden_in, part, source, sums=True)
        totals.append(reduce_to_owner(keep, send, devices).reshape(piece, 3, -1))
        parts.append(part)
        part_sums.append(part_sum)
    total_qkv = jnp.concatenate(totals, axis=2).reshape(piece, 3 * width)
    part_sums = jnp.concatenate(part_sums, axis=2)
    vector_sums = jnp.concatenate([part_sums[0, :1], part_sums[2, :1], sums[2:]], axis=0)
    ordered = jnp.take(vector_sums.reshape(devices, 1, -1), source, axis=0)
    total_vectors = reduce_to_owner(ordered[: devices // 2], ordered[devices // 2 :], devices)[0]
    input_grad = input_gradient(grad_one, gathered, parts)

    m_qkv, v_qkv, w_qkv = adamw(proj_qkv, total_qkv, first_qkv, second_qkv, WEIGHT_DECAY, LEARN_RATE)
    m_attn, v_attn, w_attn = adamw(
        proj_attn, total_attn, first_attn, second_attn, WEIGHT_DECAY, LEARN_RATE
    )
    m_up, v_up, w_up = adamw(proj_up, total_up, first_up, second_up, WEIGHT_DECAY, LEARN_RATE)
    m_down, v_down, w_down = adamw(
        proj_down, total_down, first_down, second_down, WEIGHT_DECAY, LEARN_RATE
    )
    m_vec, v_vec, w_vec = adamw(
        vectors, total_vectors, first_vectors, second_vectors, 0.0, LEARN_RATE_VECTOR
    )
    return (
        output,
        input_grad,
        m_qkv,
        v_qkv,
        w_qkv,
        m_attn,
        v_attn,
        w_attn,
        m_up,
        v_up,
        w_up,
        m_down,
        v_down,
        w_down,
        m_vec,
        v_vec,
        w_vec,
    )


def solution(mesh):
    rows, flat = P("dp", None), P("dp")
    return jax.shard_map(
        on_device,
        mesh=mesh,
        in_specs=(rows, flat, rows) + (rows, rows, rows, rows, flat) * 3,
        out_specs=(rows, rows) + (rows,) * 12 + (flat,) * 3,
        check_vma=False,
    )
```

```python
import functools
import math

import jax
import jax.numpy as jnp
from jax import lax
from jax.experimental import pallas as pl
from jax.experimental.pallas import tpu as pltpu
from jax.sharding import PartitionSpec as P

HEAD = 64
STEP = 10

EPSILON_NORM = 1e-05
BETA_ONE = 0.9
BETA_TWO = 0.999
LEARN_RATE = 0.1
LEARN_RATE_VECTOR = 0.4
WEIGHT_DECAY = 0.01
EPSILON_ADAM = 1e-08

LANES = 128
ROWS = 256
GROUPS = 2
VMEM_BYTES = 56 * 1024 * 1024
BF = jnp.bfloat16
F32 = jnp.float32

NN = (((1,), (0,)), ((), ()))
NT = (((1,), (1,)), ((), ()))
TN = (((0,), (0,)), ((), ()))


def dot(left, right, dims=NN):
    return lax.dot_general(left, right, dims, preferred_element_type=F32)


def params(grid_rank):
    return pltpu.CompilerParams(
        dimension_semantics=("arbitrary",) * grid_rank, vmem_limit_bytes=VMEM_BYTES
    )


def cost(flops, moved, exps=0):
    return pl.CostEstimate(flops=int(flops), bytes_accessed=int(moved), transcendentals=int(exps))


def qkv_kernel(x_ref, w_ref, vec_ref, out_ref):
    width = x_ref.shape[1]
    x = x_ref[...]
    for part in range(3):
        cols = pl.ds(part * width, width)
        value = dot(x, w_ref[:, cols])
        if part == 0:
            value = value + vec_ref[0:1, :]
        if part == 2:
            value = value + vec_ref[1:2, :]
        out_ref[:, cols] = value.astype(BF)


def project_qkv(x, gathered, vec):
    rows, width = x.shape
    return pl.pallas_call(
        qkv_kernel,
        grid=(rows // ROWS,),
        in_specs=[
            pl.BlockSpec((ROWS, width), lambda i: (i, 0)),
            pl.BlockSpec((width, 3 * width), lambda i: (0, 0), pipeline_mode=pl.Buffered(1)),
            pl.BlockSpec(vec.shape, lambda i: (0, 0)),
        ],
        out_specs=pl.BlockSpec((ROWS, 3 * width), lambda i: (i, 0)),
        out_shape=jax.ShapeDtypeStruct((rows, 3 * width), BF),
        compiler_params=params(1),
        cost_estimate=cost(6 * rows * width * width, 2 * (4 * rows * width + 3 * width * width)),
        name="project_qkv",
    )(x, gathered, vec)


def attend_kernel(len_ref, q_ref, k_ref, v_ref, *refs, which):
    out_ref, lse_ref = refs[-2:]
    length = len_ref[which]
    seq = q_ref.shape[0]
    query = q_ref[...] * jnp.asarray(1.0 / math.sqrt(HEAD), BF)
    keyset = k_ref[...]
    val_t = v_ref[...].T
    lane = lax.broadcasted_iota(jnp.int32, (seq, LANES), 1)
    alive = lax.broadcasted_iota(jnp.int32, (seq, seq), 0) < length
    mixed = []
    for head in range(2):
        mine = (lane < HEAD) if head == 0 else (lane >= HEAD)
        scores = dot(keyset, jnp.where(mine, query, jnp.zeros_like(query)), NT)
        scores = jnp.where(alive, scores, -1e30)
        highest = jnp.max(scores, axis=0, keepdims=True)
        expo = jnp.exp(scores - highest)
        summed = jnp.sum(expo, axis=0, keepdims=True)
        probs = (expo * (1.0 / summed)).astype(BF)
        mixed.append(dot(val_t[head * HEAD : (head + 1) * HEAD], probs))
        lse_ref[0, head : head + 1, :] = highest + jnp.log(summed)
    out_ref[...] = jnp.concatenate(mixed, axis=0).T.astype(BF)


def attend_forward(packed, lengths, width, which, filled):
    rows = packed.shape[0]
    batch = lengths.shape[0]
    seq = rows // batch
    pairs = width // LANES
    grid_spec = pltpu.PrefetchScalarGridSpec(
        num_scalar_prefetch=1,
        grid=(pairs,),
        in_specs=[
            pl.BlockSpec((seq, LANES), lambda h, ln: (which, h)),
            pl.BlockSpec((seq, LANES), lambda h, ln: (which, pairs + h)),
            pl.BlockSpec((seq, LANES), lambda h, ln: (which, 2 * pairs + h)),
        ]
        + [pl.BlockSpec(memory_space=pl.ANY)] * len(filled),
        out_specs=[
            pl.BlockSpec((seq, LANES), lambda h, ln: (which, h)),
            pl.BlockSpec((1, 2, seq), lambda h, ln: (which * pairs + h, 0, 0)),
        ],
    )
    return pl.pallas_call(
        functools.partial(attend_kernel, which=which),
        grid_spec=grid_spec,
        out_shape=[
            jax.ShapeDtypeStruct((rows, width), BF),
            jax.ShapeDtypeStruct((batch * pairs, 2, seq), F32),
        ],
        input_output_aliases={4 + index: index for index in range(len(filled))},
        compiler_params=params(1),
        cost_estimate=cost(16 * seq * seq * width, 8 * seq * width, seq * seq * width // HEAD),
        name="attend_forward",
    )(lengths, packed, packed, packed, *filled)


def attend_back_kernel(len_ref, q_ref, k_ref, v_ref, g_ref, lse_ref, *refs, which):
    out_ref = refs[-1]
    length = len_ref[which]
    seq = q_ref.shape[0]
    factor = 1.0 / math.sqrt(HEAD)
    query = q_ref[...] * jnp.asarray(factor, BF)
    keyset = k_ref[...]
    valset = v_ref[...]
    grad = g_ref[...]
    key_t = keyset.T
    lane = lax.broadcasted_iota(jnp.int32, (seq, LANES), 1)
    alive = lax.broadcasted_iota(jnp.int32, (seq, seq), 0) < length
    grad_q = []
    grad_k = 0.0
    grad_v = 0.0
    for head in range(2):
        mine = (lane < HEAD) if head == 0 else (lane >= HEAD)
        query_h = jnp.where(mine, query, jnp.zeros_like(query))
        grad_h = jnp.where(mine, grad, jnp.zeros_like(grad))
        scores = jnp.where(alive, dot(keyset, query_h, NT), -1e30)
        probs = jnp.exp(scores - lse_ref[0, head : head + 1, :])
        grad_probs = dot(valset, grad_h, NT)
        total = jnp.sum(probs * grad_probs, axis=0, keepdims=True)
        grad_scores = (probs * (grad_probs - total)).astype(BF)
        grad_v = grad_v + dot(probs.astype(BF), grad_h)
        grad_k = grad_k + dot(grad_scores, query_h)
        grad_q.append(dot(key_t[head * HEAD : (head + 1) * HEAD], grad_scores))
    out_ref[0] = (jnp.concatenate(grad_q, axis=0).T * factor).astype(BF)
    out_ref[1] = grad_k.astype(BF)
    out_ref[2] = grad_v.astype(BF)


def attend_backward(packed, lengths, lse, grad_mixed, group, which, filled):
    rows, width = grad_mixed.shape
    batch = lengths.shape[0]
    seq = rows // batch
    pairs = width // LANES
    here = pairs // GROUPS
    base = group * here
    grid_spec = pltpu.PrefetchScalarGridSpec(
        num_scalar_prefetch=1,
        grid=(here,),
        in_specs=[
            pl.BlockSpec((seq, LANES), lambda h, ln: (which, base + h)),
            pl.BlockSpec((seq, LANES), lambda h, ln: (which, pairs + base + h)),
            pl.BlockSpec((seq, LANES), lambda h, ln: (which, 2 * pairs + base + h)),
            pl.BlockSpec((seq, LANES), lambda h, ln: (which, base + h)),
            pl.BlockSpec((1, 2, seq), lambda h, ln: (which * pairs + base + h, 0, 0)),
        ]
        + [pl.BlockSpec(memory_space=pl.ANY)] * len(filled),
        out_specs=pl.BlockSpec((3, seq, LANES), lambda h, ln: (0, which, h)),
    )
    return pl.pallas_call(
        functools.partial(attend_back_kernel, which=which),
        grid_spec=grid_spec,
        out_shape=jax.ShapeDtypeStruct((3, rows, here * LANES), BF),
        input_output_aliases={6 + index: index for index in range(len(filled))},
        compiler_params=params(1),
        cost_estimate=cost(
            40 * seq * seq * here * LANES, 14 * seq * here * LANES, seq * seq * here * 2
        ),
        name="attend_backward",
    )(lengths, packed, packed, packed, grad_mixed, lse, *filled)


def norm_forward(resid, gain, shift):
    centred = resid - jnp.mean(resid, axis=-1, keepdims=True)
    inverse = lax.rsqrt(jnp.mean(centred * centred, axis=-1, keepdims=True) + EPSILON_NORM)
    scaled = centred * inverse
    return (scaled * gain + shift, scaled, inverse)


def norm_backward(grad, scaled, inverse, gain):
    grad_scaled = grad * gain
    return inverse * (
        grad_scaled
        - jnp.mean(grad_scaled, axis=-1, keepdims=True)
        - scaled * jnp.mean(grad_scaled * scaled, axis=-1, keepdims=True)
    )


def column_sum(value):
    return jnp.sum(value, axis=0, keepdims=True)


def middle_kernel(
    len_ref,
    x_ref,
    mixed_ref,
    cot_ref,
    w_attn,
    w_up,
    w_down,
    vec_ref,
    out_ref,
    first_ref,
    active_ref,
    upper_ref,
    branch_ref,
    attn_ref,
    gmix_ref,
    resid_ref,
    sum_ref,
    slope_ref,
    *,
    seq,
):
    step = pl.program_id(0)
    rows, width = x_ref.shape
    chunks = w_up.shape[1] // width
    start = (step * rows) % seq
    length = len_ref[(step * rows) // seq]

    def vec(index):
        return vec_ref[index : index + 1, :]

    gain_one, shift_one, gain_two, shift_two = vec(8), vec(9), vec(10), vec(11)

    @pl.when(step == 0)
    def _():
        sum_ref[...] = jnp.zeros_like(sum_ref)

    resid_one = x_ref[...].astype(F32) + dot(mixed_ref[...], w_attn[...]) + vec(2)
    first, scaled_one, inverse_one = norm_forward(resid_one, gain_one, shift_one)
    first_low = first.astype(BF)
    first_ref[...] = first_low
    total = first + vec(7)
    for j in range(chunks):
        cols = pl.ds(j * width, width)
        upper = dot(first_low, w_up[:, cols]) + vec(3 + j)
        half = 0.5 + 0.5 * lax.erf(upper * (1.0 / math.sqrt(2.0)))
        active = (upper * half).astype(BF)
        active_ref[:, cols] = active
        slope_ref[:, cols] = half + upper * jnp.exp(-0.5 * upper * upper) * (
            1.0 / math.sqrt(2.0 * math.pi)
        )
        total = total + dot(active, w_down[cols, :])
    output, scaled_two, inverse_two = norm_forward(total, gain_two, shift_two)
    out_ref[...] = output.astype(BF)

    @pl.when(start < length)
    def _():
        alive = lax.broadcasted_iota(jnp.int32, (rows, 1), 0) + start < length
        grad_out = jnp.where(alive, cot_ref[...].astype(F32), 0.0)
        grad_two = norm_backward(grad_out, scaled_two, inverse_two, gain_two)
        branch = grad_two.astype(BF)
        branch_ref[...] = branch
        grad_first = grad_two
        for j in range(chunks):
            cols = pl.ds(j * width, width)
            grad_upper = (dot(branch, w_down[cols, :], NT) * slope_ref[:, cols]).astype(BF)
            upper_ref[:, cols] = grad_upper
            sum_ref[3 + j : 4 + j, :] += column_sum(grad_upper.astype(F32))
            grad_first = grad_first + dot(grad_upper, w_up[:, cols], NT)
        grad_one = norm_backward(grad_first, scaled_one, inverse_one, gain_one)
        resid_ref[...] = grad_one
        grad_attn = grad_one.astype(BF)
        attn_ref[...] = grad_attn
        gmix_ref[...] = dot(grad_attn, w_attn[...], NT).astype(BF)
        sum_ref[2:3, :] += column_sum(grad_attn.astype(F32))
        sum_ref[7:8, :] += column_sum(branch.astype(F32))
        sum_ref[8:9, :] += column_sum(grad_first * scaled_one)
        sum_ref[9:10, :] += column_sum(grad_first)
        sum_ref[10:11, :] += column_sum(grad_out * scaled_two)
        sum_ref[11:12, :] += column_sum(grad_out)

    @pl.when(start >= length)
    def _():
        upper_ref[...] = jnp.zeros_like(upper_ref)
        branch_ref[...] = jnp.zeros_like(branch_ref)
        attn_ref[...] = jnp.zeros_like(attn_ref)
        gmix_ref[...] = jnp.zeros_like(gmix_ref)
        resid_ref[...] = jnp.zeros_like(resid_ref)


def middle(x, mixed, cotangent, lengths, gathered, w_down, vec):
    rows, width = x.shape
    inner = w_down.shape[0]
    seq = rows // lengths.shape[0]
    once = pl.Buffered(1)
    thin = pl.BlockSpec((ROWS, width), lambda i, ln: (i, 0))
    wide = pl.BlockSpec((ROWS, inner), lambda i, ln: (i, 0))
    grid_spec = pltpu.PrefetchScalarGridSpec(
        num_scalar_prefetch=1,
        grid=(rows // ROWS,),
        in_specs=[
            thin,
            thin,
            thin,
            pl.BlockSpec((width, width), lambda i, ln: (0, inner // width), pipeline_mode=once),
            pl.BlockSpec((width, inner), lambda i, ln: (0, 0), pipeline_mode=once),
            pl.BlockSpec((inner, width), lambda i, ln: (0, 0), pipeline_mode=once),
            pl.BlockSpec(vec.shape, lambda i, ln: (0, 0)),
        ],
        out_specs=[
            thin,
            thin,
            wide,
            wide,
            thin,
            thin,
            thin,
            thin,
            pl.BlockSpec(vec.shape, lambda i, ln: (0, 0)),
        ],
        scratch_shapes=[pltpu.VMEM((ROWS, inner), F32)],
    )
    low = jax.ShapeDtypeStruct((rows, width), BF)
    low_wide = jax.ShapeDtypeStruct((rows, inner), BF)
    return pl.pallas_call(
        functools.partial(middle_kernel, seq=seq),
        grid_spec=grid_spec,
        out_shape=[
            low,
            low,
            low_wide,
            low_wide,
            low,
            low,
            low,
            jax.ShapeDtypeStruct((rows, width), F32),
            jax.ShapeDtypeStruct(vec.shape, F32),
        ],
        compiler_params=params(1),
        cost_estimate=cost(
            8 * rows * width * inner + 4 * rows * width * width,
            rows * (4 * inner + 20 * width) + 4 * width * inner,
            2 * rows * inner,
        ),
        name="middle",
    )(lengths, x, mixed, cotangent, gathered, gathered, w_down, vec)


def weight_kernel(src_ref, left_ref, right_ref, *refs, sums):
    keep_ref, send_ref, acc_ref = refs[0], refs[1], refs[-1]
    half, piece, _ = keep_ref.shape
    right = right_ref[0] if len(right_ref.shape) == 3 else right_ref[...]
    acc_ref[...] = dot(left_ref[...], right, TN)
    if sums:
        refs[2][0] = jnp.broadcast_to(column_sum(right.astype(F32)), refs[2].shape[1:])
    for slot in range(half):
        for ref, offset in ((keep_ref, 0), (send_ref, half)):
            begin = pl.multiple_of(src_ref[offset + slot] * piece, 8)
            ref[slot] = acc_ref[pl.ds(begin, piece), :].astype(BF)


def plain_weight_kernel(left_ref, right_ref, out_ref, *refs):
    right = right_ref[0] if len(right_ref.shape) == 3 else right_ref[...]
    out_ref[...] = dot(left_ref[...], right, TN).astype(BF)
    if refs:
        refs[0][0] = jnp.broadcast_to(column_sum(right.astype(F32)), refs[0].shape[1:])


def weight_gradient(left, right, source, sums=False):
    rows, tall = left.shape
    devices = source.shape[0]
    piece = tall // devices
    if right.ndim == 3:
        steps, _, tile = right.shape
        right_block = pl.BlockSpec((1, rows, tile), lambda j, *s: (j, 0, 0))
    else:
        tile = min(right.shape[1], 768)
        steps = right.shape[1] // tile
        right_block = pl.BlockSpec((rows, tile), lambda j, *s: (0, j))
    left_block = pl.BlockSpec((rows, tall), lambda j, *s: (0, 0))
    extra_specs = [pl.BlockSpec((1, 8, tile), lambda j, *s: (j, 0, 0))] if sums else []
    extra_shapes = [jax.ShapeDtypeStruct((steps, 8, tile), F32)] if sums else []
    estimate = cost(2 * rows * tall * tile * steps, 2 * tall * tile * steps + 2 * rows * (tall + tile * steps))
    if piece % 8:
        whole, *rest = pl.pallas_call(
            plain_weight_kernel,
            grid=(steps,),
            in_specs=[left_block, right_block],
            out_specs=[pl.BlockSpec((tall, tile), lambda j: (0, j))] + extra_specs,
            out_shape=[jax.ShapeDtypeStruct((tall, steps * tile), BF)] + extra_shapes,
            compiler_params=params(1),
            cost_estimate=estimate,
            name="weight_gradient",
        )(left, right)
        ordered = jnp.take(whole.reshape(devices, piece, steps * tile), source, axis=0)
        return (ordered[: devices // 2], ordered[devices // 2 :], *rest)
    block = pl.BlockSpec((devices // 2, piece, tile), lambda j, s: (0, 0, j))
    shape = jax.ShapeDtypeStruct((devices // 2, piece, steps * tile), BF)
    grid_spec = pltpu.PrefetchScalarGridSpec(
        num_scalar_prefetch=1,
        grid=(steps,),
        in_specs=[left_block, right_block],
        out_specs=[block, block] + extra_specs,
        scratch_shapes=[pltpu.VMEM((tall, tile), F32)],
    )
    return pl.pallas_call(
        functools.partial(weight_kernel, sums=sums),
        grid_spec=grid_spec,
        out_shape=[shape, shape] + extra_shapes,
        compiler_params=params(1),
        cost_estimate=estimate,
        name="weight_gradient",
    )(source, left, right)


def joint_kernel(src_ref, left_ref, last_left_ref, right_ref, last_right_ref, keep_ref, send_ref, acc_ref):
    half, piece, _ = keep_ref.shape
    last = pl.num_programs(0) - 1

    @pl.when(pl.program_id(0) < last)
    def _():
        acc_ref[...] = dot(left_ref[...], right_ref[...], TN)

    @pl.when(pl.program_id(0) == last)
    def _():
        acc_ref[...] = dot(last_left_ref[...], last_right_ref[...], TN)

    for slot in range(half):
        for ref, offset in ((keep_ref, 0), (send_ref, half)):
            begin = pl.multiple_of(src_ref[offset + slot] * piece, 8)
            ref[slot] = acc_ref[pl.ds(begin, piece), :].astype(BF)


def joint_gradient(left, right, last_left, last_right, source):
    rows, tall = left.shape
    devices = source.shape[0]
    piece = tall // devices
    tile = last_right.shape[1]
    wide = right.shape[1] // tile
    if piece % 8:
        one = weight_gradient(left, right, source)
        two = weight_gradient(last_left, last_right, source)
        return [jnp.concatenate(both, axis=2) for both in zip(one, two)]
    full = pl.BlockSpec((rows, tall), lambda j, s: (0, 0))
    block = pl.BlockSpec((devices // 2, piece, tile), lambda j, s: (0, 0, j))
    shape = jax.ShapeDtypeStruct((devices // 2, piece, (wide + 1) * tile), BF)
    grid_spec = pltpu.PrefetchScalarGridSpec(
        num_scalar_prefetch=1,
        grid=(wide + 1,),
        in_specs=[
            full,
            full,
            pl.BlockSpec((rows, tile), lambda j, s: (0, jnp.minimum(j, wide - 1))),
            pl.BlockSpec((rows, tile), lambda j, s: (0, 0)),
        ],
        out_specs=[block, block],
        scratch_shapes=[pltpu.VMEM((tall, tile), F32)],
    )
    return pl.pallas_call(
        joint_kernel,
        grid_spec=grid_spec,
        out_shape=[shape, shape],
        compiler_params=params(1),
        cost_estimate=cost(
            2 * rows * tall * tile * (wide + 1), 2 * (tall + rows) * tile * (wide + 1) + 4 * rows * tall
        ),
        name="joint_gradient",
    )(source, left, last_left, right, last_right)


def tall_kernel(slot_ref, left_ref, right_ref, keep_ref, send_ref, acc_ref):
    step = pl.program_id(0)
    half, piece, _ = keep_ref.shape
    here = left_ref.shape[1] // piece
    acc_ref[...] = dot(left_ref[...], right_ref[...], TN)
    for index in range(here):
        slot = slot_ref[step * here + index]
        part = acc_ref[index * piece : (index + 1) * piece, :].astype(BF)

        @pl.when(slot < half)
        def _():
            keep_ref[jnp.minimum(slot, half - 1)] = part

        @pl.when(slot >= half)
        def _():
            send_ref[jnp.maximum(slot - half, 0)] = part


def plain_tall_kernel(left_ref, right_ref, out_ref):
    out_ref[...] = dot(left_ref[...], right_ref[...], TN).astype(BF)


def tall_gradient(left, right, source, slot_of):
    rows, tall = left.shape
    width = right.shape[1]
    devices = source.shape[0]
    piece = tall // devices
    steps = tall // width
    left_block = pl.BlockSpec((rows, width), lambda j, *s: (0, j))
    right_block = pl.BlockSpec((rows, width), lambda j, *s: (0, 0))
    estimate = cost(2 * rows * tall * width, 2 * tall * width + 2 * rows * (tall + width))
    if piece % 16:
        whole = pl.pallas_call(
            plain_tall_kernel,
            grid=(steps,),
            in_specs=[left_block, right_block],
            out_specs=pl.BlockSpec((width, width), lambda j: (j, 0)),
            out_shape=jax.ShapeDtypeStruct((tall, width), BF),
            compiler_params=params(1),
            cost_estimate=estimate,
            name="tall_gradient",
        )(left, right)
        ordered = jnp.take(whole.reshape(devices, piece, width), source, axis=0)
        return (ordered[: devices // 2], ordered[devices // 2 :])
    block = pl.BlockSpec((devices // 2, piece, width), lambda j, s: (0, 0, 0))
    shape = jax.ShapeDtypeStruct((devices // 2, piece, width), BF)
    grid_spec = pltpu.PrefetchScalarGridSpec(
        num_scalar_prefetch=1,
        grid=(steps,),
        in_specs=[left_block, right_block],
        out_specs=[block, block],
        scratch_shapes=[pltpu.VMEM((width, width), F32)],
    )
    return pl.pallas_call(
        tall_kernel,
        grid_spec=grid_spec,
        out_shape=[shape, shape],
        compiler_params=params(1),
        cost_estimate=estimate,
        name="tall_gradient",
    )(slot_of, left, right)


def input_kernel(resid_ref, w_ref, *refs):
    out_ref = refs[-1]
    width = resid_ref.shape[1]
    total = resid_ref[...]
    for group, grad_ref in enumerate(refs[:-1]):
        here = grad_ref.shape[2]
        for part in range(3):
            total = total + dot(grad_ref[part], w_ref[:, pl.ds(part * width + group * here, here)], NT)
    out_ref[...] = total.astype(BF)


def input_gradient(resid, gathered, grads):
    rows, width = resid.shape
    return pl.pallas_call(
        input_kernel,
        grid=(rows // ROWS,),
        in_specs=[
            pl.BlockSpec((ROWS, width), lambda i: (i, 0)),
            pl.BlockSpec((width, 3 * width), lambda i: (0, 0), pipeline_mode=pl.Buffered(1)),
        ]
        + [pl.BlockSpec((3, ROWS, grad.shape[2]), lambda i: (0, i, 0)) for grad in grads],
        out_specs=pl.BlockSpec((ROWS, width), lambda i: (i, 0)),
        out_shape=jax.ShapeDtypeStruct((rows, width), BF),
        compiler_params=params(1),
        cost_estimate=cost(6 * rows * width * width, 12 * rows * width + 6 * width * width),
        name="input_gradient",
    )(resid, gathered, *grads)


def swap(value, mask, devices):
    return lax.ppermute(value, "dp", [(index, index ^ mask) for index in range(devices)])


def hold(value, *others):
    return lax.optimization_barrier((value, others))[0]


def masks_of(bits):
    found = [0]
    for bit in bits:
        found = found + [mask | (1 << bit) for mask in found]
    return found


def relative_order(order):
    relative = [0]
    for bits in order:
        relative = [base | mask for base in relative for mask in masks_of(bits)]
    return relative


def stage_orders(devices):
    bits = devices.bit_length() - 1
    rest = [(bit,) for bit in range(3, bits)]
    low = [(bit,) for bit in range(min(3, bits))]
    by_x = low + rest
    by_y = low[:1] + low[1:][::-1] + rest
    both = low[:1] + ([tuple(range(1, min(3, bits)))] if bits > 1 else []) + rest
    return by_x, by_y, both


class Reduce:
    def __init__(self, keep, send, order, devices):
        self.order, self.devices, self.at = order, devices, 0
        self.parts = [keep, send]
        self.terms = None

    def send(self):
        masks = masks_of(self.order[self.at])
        self.terms = [self.parts[0]] + [
            swap(part, mask, self.devices) for part, mask in zip(self.parts[1:], masks[1:])
        ]
        self.at += 1
        return self

    def total(self, begin, size):
        result = self.terms[0][begin : begin + size].astype(F32)
        for term in self.terms[1:]:
            result = result + term[begin : begin + size].astype(F32)
        return result

    def join(self):
        ways = len(masks_of(self.order[self.at]))
        size = self.terms[0].shape[0] // ways
        self.parts = [self.total(way * size, size).astype(BF) for way in range(ways)]
        return self

    def finish(self):
        if self.terms is None:
            self.send()
        while self.at < len(self.order):
            self.join().send()
        return self.total(0, 1)[0]


class Gather:
    def __init__(self, shard, order, devices):
        self.order, self.devices, self.at = order, devices, 0
        self.held = shard[None]
        self.taken = None

    def send(self):
        masks = masks_of(self.order[self.at])
        self.taken = [swap(self.held, mask, self.devices) for mask in masks[1:]]
        self.at += 1
        return self

    def join(self):
        self.held = jnp.concatenate([self.held] + self.taken, axis=0)
        return self


def lay_pairs_kernel(index_ref, odd_ref, held_ref, taken_ref, out_ref):
    half, piece, _ = held_ref.shape
    odd = odd_ref[0] == 1
    for slot in range(half):
        mine = held_ref[slot].astype(F32)
        other = taken_ref[slot].astype(F32)
        both = jnp.concatenate(
            [jnp.where(odd, other, mine), jnp.where(odd, mine, other)], axis=0
        ).astype(BF)
        begin = pl.multiple_of((index_ref[slot] // 2) * (2 * piece), 16)
        out_ref[pl.ds(begin, 2 * piece), :] = both


def lay_kernel(index_ref, odd_ref, held_ref, taken_ref, out_ref):
    half, piece, _ = held_ref.shape
    for slot in range(half):
        for ref, flip in ((held_ref, 0), (taken_ref, 1)):
            begin = pl.multiple_of((index_ref[slot] ^ flip) * piece, 16)
            out_ref[pl.ds(begin, piece), :] = ref[slot]


def lay_out(gather, me):
    held, taken = gather.held, gather.taken[0]
    half, piece, columns = held.shape
    devices = 2 * half
    relative = [0]
    for bits in gather.order[:-1]:
        relative = [base | mask for mask in masks_of(bits) for base in relative]
    index = jnp.asarray(relative, jnp.int32) ^ me
    if piece % 8:
        where = [0] * devices
        for slot, value in enumerate(relative):
            where[value], where[value ^ 1] = slot, half + slot
        natural = jnp.take(jnp.asarray(where, jnp.int32), jnp.arange(devices, dtype=jnp.int32) ^ me)
        both = jnp.concatenate([held, taken], axis=0)
        return jnp.take(both, natural, axis=0).reshape(devices * piece, columns)
    whole = pl.BlockSpec(held.shape, lambda i, *s: (0, 0, 0))
    grid_spec = pltpu.PrefetchScalarGridSpec(
        num_scalar_prefetch=2,
        grid=(1,),
        in_specs=[whole, whole],
        out_specs=pl.BlockSpec((devices * piece, columns), lambda i, *s: (0, 0)),
    )
    return pl.pallas_call(
        lay_pairs_kernel if piece % 16 else lay_kernel,
        grid_spec=grid_spec,
        out_shape=jax.ShapeDtypeStruct((devices * piece, columns), BF),
        compiler_params=params(1),
        cost_estimate=cost(devices * piece * columns, 4 * devices * piece * columns),
        name="lay_out",
    )(index, (me & 1).reshape(1), held, taken)


def adamw(weight, grad, first, second, decay, rate):
    new_first = BETA_ONE * first + (1.0 - BETA_ONE) * grad
    new_second = BETA_TWO * second + (1.0 - BETA_TWO) * grad * grad
    corrected = new_first / (1.0 - BETA_ONE**STEP)
    scale_sq = new_second / (1.0 - BETA_TWO**STEP)
    new_weight = weight - rate * (corrected / (jnp.sqrt(scale_sq) + EPSILON_ADAM) + decay * weight)
    return (new_first, new_second, new_weight)


def on_device(
    hidden_in,
    lengths,
    cotangent,
    proj_qkv,
    proj_attn,
    proj_up,
    proj_down,
    vectors,
    first_qkv,
    first_attn,
    first_up,
    first_down,
    first_vectors,
    second_qkv,
    second_attn,
    second_up,
    second_down,
    second_vectors,
):
    devices = lax.axis_size("dp")
    me = lax.axis_index("dp")
    width = hidden_in.shape[1]
    piece = proj_qkv.shape[0]
    inner = proj_up.shape[1]
    batch = lengths.shape[0]
    by_x, by_y, both = stage_orders(devices)
    outward = both[::-1]

    def source_of(order):
        return jnp.asarray(relative_order(order), jnp.int32) ^ me

    slots = [0] * devices
    for slot, value in enumerate(relative_order(by_x)):
        slots[value] = slot
    slot_of = jnp.take(jnp.asarray(slots, jnp.int32), jnp.arange(devices, dtype=jnp.int32) ^ me)

    entries = vectors.shape[0] // piece
    wide = lax.all_gather(
        jnp.concatenate([proj_up.astype(BF), proj_attn.astype(BF)], axis=1), "dp", axis=0, tiled=True
    )
    shard = jnp.concatenate(
        [
            proj_qkv.astype(BF),
            jnp.pad(vectors.astype(BF).reshape(piece, entries), ((0, 0), (0, LANES - entries))),
        ],
        axis=1,
    )
    qkv = Gather(shard, outward, devices)
    down = Gather(proj_down.astype(BF), outward, devices)
    for _ in range(len(outward) - 2):
        qkv.send().join()
    down.held = hold(down.held, qkv.held)
    qkv.send()
    for _ in range(len(outward) - 2):
        down.send().join()
    qkv.join()
    down.held = hold(down.held, qkv.held)
    qkv.held = hold(qkv.held, down.held)
    down.send()
    qkv.send()
    gathered = lay_out(qkv, me)
    vec = gathered[:, 3 * width : 3 * width + entries].astype(F32).reshape(-1, width)

    packed = project_qkv(hidden_in, gathered, vec)
    filled = ()
    for which in range(batch):
        filled = attend_forward(packed, lengths, width, which, filled)
        if which == 0:
            down.taken = [hold(value, filled) for value in down.taken]
            down.join()
            packed = hold(packed, down.held)
            down.send()
    mixed, lse = filled
    w_down = lay_out(down, me)
    output, first_low, active, grad_upper, grad_branch, grad_attn, grad_mixed, grad_one, sums = middle(
        hidden_in, mixed, cotangent, lengths, wide, w_down, vec
    )

    total = Reduce(*tall_gradient(active, grad_branch, source_of(by_x), slot_of), by_x, devices)
    total.send()
    grad_upper = hold(grad_upper, total.parts)
    joint = Reduce(
        *joint_gradient(first_low, grad_upper, mixed, grad_attn, source_of(by_y)), by_y, devices
    )
    total.join()
    grad_mixed = hold(grad_mixed, total.parts, joint.parts)
    total.send()
    joint.send()
    parts, part_sums, queue = [], [], []
    for group in range(GROUPS):
        part = ()
        for which in range(batch):
            part = (attend_backward(packed, lengths, lse, grad_mixed, group, which, part),)
            if group == 0 and which == 0:
                joint.join()
                grad_mixed = hold(grad_mixed, joint.parts)
                joint.send()
            if group == 1 and which == 0:
                queue[0].join()
                grad_mixed = hold(grad_mixed, queue[0].parts)
                queue[0].send()
        if group == GROUPS - 1:
            joint.join()
            part = (hold(part[0], joint.parts),)
            joint.send()
        keep, send, part_sum = weight_gradient(hidden_in, part[0], source_of(both), sums=True)
        parts.append(part[0])
        part_sums.append(part_sum)
        if group == 0:
            queue.append(Reduce(keep, send, both, devices))
            total.join()
            grad_mixed = hold(grad_mixed, total.parts, keep)
            total.send()
            queue[0].send()
    part_sums = jnp.concatenate(part_sums, axis=2)
    vector_sums = jnp.concatenate([part_sums[0, :1], part_sums[2, :1], sums[2:]], axis=0)
    ordered = jnp.take(vector_sums.reshape(devices, piece, entries), source_of(both), axis=0)
    ordered = jnp.pad(ordered.astype(BF), ((0, 0), (0, 0), (0, LANES - entries)))
    keep = jnp.concatenate([keep, ordered[: devices // 2]], axis=2)
    send = jnp.concatenate([send, ordered[devices // 2 :]], axis=2)
    queue.append(Reduce(keep, send, both, devices).send())
    grad_one = hold(grad_one, queue[1].parts)
    input_grad = input_gradient(grad_one, gathered, parts)

    total_qkv = [chain.finish() for chain in queue]
    total_vectors = total_qkv[1][:, 3 * width // GROUPS : 3 * width // GROUPS + entries].reshape(-1)
    here = width // GROUPS
    total_qkv = jnp.concatenate(
        [part[:, at * here : (at + 1) * here] for at in range(3) for part in total_qkv], axis=1
    )
    total_wide = joint.finish()
    total_up, total_attn = total_wide[:, :inner], total_wide[:, inner:]
    total_down = total.finish()

    m_qkv, v_qkv, w_qkv = adamw(proj_qkv, total_qkv, first_qkv, second_qkv, WEIGHT_DECAY, LEARN_RATE)
    m_attn, v_attn, w_attn = adamw(
        proj_attn, total_attn, first_attn, second_attn, WEIGHT_DECAY, LEARN_RATE
    )
    m_up, v_up, w_up = adamw(proj_up, total_up, first_up, second_up, WEIGHT_DECAY, LEARN_RATE)
    m_down, v_down, w_down = adamw(
        proj_down, total_down, first_down, second_down, WEIGHT_DECAY, LEARN_RATE
    )
    m_vec, v_vec, w_vec = adamw(
        vectors, total_vectors, first_vectors, second_vectors, 0.0, LEARN_RATE_VECTOR
    )
    return (
        output,
        input_grad,
        m_qkv,
        v_qkv,
        w_qkv,
        m_attn,
        v_attn,
        w_attn,
        m_up,
        v_up,
        w_up,
        m_down,
        v_down,
        w_down,
        m_vec,
        v_vec,
        w_vec,
    )


def solution(mesh):
    rows, flat = P("dp", None), P("dp")
    return jax.shard_map(
        on_device,
        mesh=mesh,
        in_specs=(rows, flat, rows) + (rows, rows, rows, rows, flat) * 3,
        out_specs=(rows, rows) + (rows,) * 12 + (flat,) * 3,
        check_vma=False,
    )
```

```python
import functools
import math

import jax
import jax.numpy as jnp
from jax import lax
from jax.experimental import pallas as pl
from jax.experimental.pallas import tpu as pltpu
from jax.sharding import PartitionSpec as P

HEAD = 64
STEP = 10

EPSILON_NORM = 1e-05
BETA_ONE = 0.9
BETA_TWO = 0.999
LEARN_RATE = 0.1
LEARN_RATE_VECTOR = 0.4
WEIGHT_DECAY = 0.01
EPSILON_ADAM = 1e-08

LANES = 128
ROWS = 256
GROUPS = 2
VMEM_BYTES = 56 * 1024 * 1024
BF = jnp.bfloat16
F32 = jnp.float32

NN = (((1,), (0,)), ((), ()))
NT = (((1,), (1,)), ((), ()))
TN = (((0,), (0,)), ((), ()))


def dot(left, right, dims=NN):
    return lax.dot_general(left, right, dims, preferred_element_type=F32)


def params(grid_rank):
    return pltpu.CompilerParams(
        dimension_semantics=("arbitrary",) * grid_rank, vmem_limit_bytes=VMEM_BYTES
    )


def cost(flops, moved, exps=0, longer=1):
    return pl.CostEstimate(
        flops=longer * int(flops), bytes_accessed=int(moved), transcendentals=int(exps)
    )


def qkv_kernel(x_ref, w_ref, vec_ref, out_ref):
    width = x_ref.shape[1]
    x = x_ref[...]
    for part in range(3):
        cols = pl.ds(part * width, width)
        value = dot(x, w_ref[:, cols])
        if part == 0:
            value = value + vec_ref[0:1, :]
        if part == 2:
            value = value + vec_ref[1:2, :]
        out_ref[:, cols] = value.astype(BF)


def project_qkv(x, gathered, vec):
    rows, width = x.shape
    return pl.pallas_call(
        qkv_kernel,
        grid=(rows // ROWS,),
        in_specs=[
            pl.BlockSpec((ROWS, width), lambda i: (i, 0)),
            pl.BlockSpec((width, 3 * width), lambda i: (0, 0), pipeline_mode=pl.Buffered(1)),
            pl.BlockSpec(vec.shape, lambda i: (0, 0)),
        ],
        out_specs=pl.BlockSpec((ROWS, 3 * width), lambda i: (i, 0)),
        out_shape=jax.ShapeDtypeStruct((rows, 3 * width), BF),
        compiler_params=params(1),
        cost_estimate=cost(6 * rows * width * width, 2 * (4 * rows * width + 3 * width * width)),
        name="project_qkv",
    )(x, gathered, vec)


def attend_kernel(len_ref, q_ref, k_ref, v_ref, *refs, which):
    out_ref, lse_ref = refs[-2:]
    length = len_ref[which]
    seq = q_ref.shape[0]
    query = q_ref[...] * jnp.asarray(1.0 / math.sqrt(HEAD), BF)
    keyset = k_ref[...]
    val_t = v_ref[...].T
    lane = lax.broadcasted_iota(jnp.int32, (seq, LANES), 1)
    alive = lax.broadcasted_iota(jnp.int32, (seq, seq), 0) < length
    mixed = []
    for head in range(2):
        mine = (lane < HEAD) if head == 0 else (lane >= HEAD)
        scores = dot(keyset, jnp.where(mine, query, jnp.zeros_like(query)), NT)
        scores = jnp.where(alive, scores, -1e30)
        highest = jnp.max(scores, axis=0, keepdims=True)
        expo = jnp.exp(scores - highest)
        summed = jnp.sum(expo, axis=0, keepdims=True)
        probs = (expo * (1.0 / summed)).astype(BF)
        mixed.append(dot(val_t[head * HEAD : (head + 1) * HEAD], probs))
        lse_ref[0, head : head + 1, :] = highest + jnp.log(summed)
    out_ref[...] = jnp.concatenate(mixed, axis=0).T.astype(BF)


def attend_forward(packed, lengths, width, which, filled):
    rows = packed.shape[0]
    batch = lengths.shape[0]
    seq = rows // batch
    pairs = width // LANES
    grid_spec = pltpu.PrefetchScalarGridSpec(
        num_scalar_prefetch=1,
        grid=(pairs,),
        in_specs=[
            pl.BlockSpec((seq, LANES), lambda h, ln: (which, h)),
            pl.BlockSpec((seq, LANES), lambda h, ln: (which, pairs + h)),
            pl.BlockSpec((seq, LANES), lambda h, ln: (which, 2 * pairs + h)),
        ]
        + [pl.BlockSpec(memory_space=pl.ANY)] * len(filled),
        out_specs=[
            pl.BlockSpec((seq, LANES), lambda h, ln: (which, h)),
            pl.BlockSpec((1, 2, seq), lambda h, ln: (which * pairs + h, 0, 0)),
        ],
    )
    return pl.pallas_call(
        functools.partial(attend_kernel, which=which),
        grid_spec=grid_spec,
        out_shape=[
            jax.ShapeDtypeStruct((rows, width), BF),
            jax.ShapeDtypeStruct((batch * pairs, 2, seq), F32),
        ],
        input_output_aliases={4 + index: index for index in range(len(filled))},
        compiler_params=params(1),
        cost_estimate=cost(16 * seq * seq * width, 8 * seq * width, seq * seq * width // HEAD),
        name="attend_forward",
    )(lengths, packed, packed, packed, *filled)


def attend_back_kernel(len_ref, q_ref, k_ref, v_ref, g_ref, lse_ref, *refs, which):
    out_ref = refs[-1]
    length = len_ref[which]
    seq = q_ref.shape[0]
    factor = 1.0 / math.sqrt(HEAD)
    query = q_ref[...] * jnp.asarray(factor, BF)
    keyset = k_ref[...]
    valset = v_ref[...]
    grad = g_ref[...]
    key_t = keyset.T
    lane = lax.broadcasted_iota(jnp.int32, (seq, LANES), 1)
    alive = lax.broadcasted_iota(jnp.int32, (seq, seq), 0) < length
    grad_q = []
    grad_k = 0.0
    grad_v = 0.0
    for head in range(2):
        mine = (lane < HEAD) if head == 0 else (lane >= HEAD)
        query_h = jnp.where(mine, query, jnp.zeros_like(query))
        grad_h = jnp.where(mine, grad, jnp.zeros_like(grad))
        scores = jnp.where(alive, dot(keyset, query_h, NT), -1e30)
        probs = jnp.exp(scores - lse_ref[0, head : head + 1, :])
        grad_probs = dot(valset, grad_h, NT)
        total = jnp.sum(probs * grad_probs, axis=0, keepdims=True)
        grad_scores = (probs * (grad_probs - total)).astype(BF)
        grad_v = grad_v + dot(probs.astype(BF), grad_h)
        grad_k = grad_k + dot(grad_scores, query_h)
        grad_q.append(dot(key_t[head * HEAD : (head + 1) * HEAD], grad_scores))
    out_ref[0] = (jnp.concatenate(grad_q, axis=0).T * factor).astype(BF)
    out_ref[1] = grad_k.astype(BF)
    out_ref[2] = grad_v.astype(BF)


def attend_backward(packed, lengths, lse, grad_mixed, group, which, filled):
    rows, width = grad_mixed.shape
    batch = lengths.shape[0]
    seq = rows // batch
    pairs = width // LANES
    here = pairs // GROUPS
    base = group * here
    grid_spec = pltpu.PrefetchScalarGridSpec(
        num_scalar_prefetch=1,
        grid=(here,),
        in_specs=[
            pl.BlockSpec((seq, LANES), lambda h, ln: (which, base + h)),
            pl.BlockSpec((seq, LANES), lambda h, ln: (which, pairs + base + h)),
            pl.BlockSpec((seq, LANES), lambda h, ln: (which, 2 * pairs + base + h)),
            pl.BlockSpec((seq, LANES), lambda h, ln: (which, base + h)),
            pl.BlockSpec((1, 2, seq), lambda h, ln: (which * pairs + base + h, 0, 0)),
        ]
        + [pl.BlockSpec(memory_space=pl.ANY)] * len(filled),
        out_specs=pl.BlockSpec((3, seq, LANES), lambda h, ln: (0, which, h)),
    )
    return pl.pallas_call(
        functools.partial(attend_back_kernel, which=which),
        grid_spec=grid_spec,
        out_shape=jax.ShapeDtypeStruct((3, rows, here * LANES), BF),
        input_output_aliases={6 + index: index for index in range(len(filled))},
        compiler_params=params(1),
        cost_estimate=cost(
            40 * seq * seq * here * LANES, 14 * seq * here * LANES, seq * seq * here * 2, 8
        ),
        name="attend_backward",
    )(lengths, packed, packed, packed, grad_mixed, lse, *filled)


def norm_forward(resid, gain, shift):
    centred = resid - jnp.mean(resid, axis=-1, keepdims=True)
    inverse = lax.rsqrt(jnp.mean(centred * centred, axis=-1, keepdims=True) + EPSILON_NORM)
    scaled = centred * inverse
    return (scaled * gain + shift, scaled, inverse)


def norm_backward(grad, scaled, inverse, gain):
    grad_scaled = grad * gain
    return inverse * (
        grad_scaled
        - jnp.mean(grad_scaled, axis=-1, keepdims=True)
        - scaled * jnp.mean(grad_scaled * scaled, axis=-1, keepdims=True)
    )


def column_sum(value):
    return jnp.sum(value, axis=0, keepdims=True)


def middle_kernel(
    len_ref,
    x_ref,
    mixed_ref,
    cot_ref,
    w_attn,
    w_up,
    w_down,
    vec_ref,
    out_ref,
    first_ref,
    active_ref,
    upper_ref,
    branch_ref,
    attn_ref,
    gmix_ref,
    resid_ref,
    sum_ref,
    slope_ref,
    *,
    seq,
):
    step = pl.program_id(0)
    rows, width = x_ref.shape
    chunks = w_up.shape[1] // width
    start = (step * rows) % seq
    length = len_ref[(step * rows) // seq]

    def vec(index):
        return vec_ref[index : index + 1, :]

    gain_one, shift_one, gain_two, shift_two = vec(8), vec(9), vec(10), vec(11)

    @pl.when(step == 0)
    def _():
        sum_ref[...] = jnp.zeros_like(sum_ref)

    resid_one = x_ref[...].astype(F32) + dot(mixed_ref[...], w_attn[...]) + vec(2)
    first, scaled_one, inverse_one = norm_forward(resid_one, gain_one, shift_one)
    first_low = first.astype(BF)
    first_ref[...] = first_low
    total = first + vec(7)
    for j in range(chunks):
        cols = pl.ds(j * width, width)
        upper = dot(first_low, w_up[:, cols]) + vec(3 + j)
        half = 0.5 + 0.5 * lax.erf(upper * (1.0 / math.sqrt(2.0)))
        active = (upper * half).astype(BF)
        active_ref[:, cols] = active
        slope_ref[:, cols] = half + upper * jnp.exp(-0.5 * upper * upper) * (
            1.0 / math.sqrt(2.0 * math.pi)
        )
        total = total + dot(active, w_down[cols, :])
    output, scaled_two, inverse_two = norm_forward(total, gain_two, shift_two)
    out_ref[...] = output.astype(BF)

    @pl.when(start < length)
    def _():
        alive = lax.broadcasted_iota(jnp.int32, (rows, 1), 0) + start < length
        grad_out = jnp.where(alive, cot_ref[...].astype(F32), 0.0)
        grad_two = norm_backward(grad_out, scaled_two, inverse_two, gain_two)
        branch = grad_two.astype(BF)
        branch_ref[...] = branch
        grad_first = grad_two
        for j in range(chunks):
            cols = pl.ds(j * width, width)
            grad_upper = (dot(branch, w_down[cols, :], NT) * slope_ref[:, cols]).astype(BF)
            upper_ref[:, cols] = grad_upper
            sum_ref[3 + j : 4 + j, :] += column_sum(grad_upper.astype(F32))
            grad_first = grad_first + dot(grad_upper, w_up[:, cols], NT)
        grad_one = norm_backward(grad_first, scaled_one, inverse_one, gain_one)
        resid_ref[...] = grad_one
        grad_attn = grad_one.astype(BF)
        attn_ref[...] = grad_attn
        gmix_ref[...] = dot(grad_attn, w_attn[...], NT).astype(BF)
        sum_ref[2:3, :] += column_sum(grad_attn.astype(F32))
        sum_ref[7:8, :] += column_sum(branch.astype(F32))
        sum_ref[8:9, :] += column_sum(grad_first * scaled_one)
        sum_ref[9:10, :] += column_sum(grad_first)
        sum_ref[10:11, :] += column_sum(grad_out * scaled_two)
        sum_ref[11:12, :] += column_sum(grad_out)

    @pl.when(start >= length)
    def _():
        upper_ref[...] = jnp.zeros_like(upper_ref)
        branch_ref[...] = jnp.zeros_like(branch_ref)
        attn_ref[...] = jnp.zeros_like(attn_ref)
        gmix_ref[...] = jnp.zeros_like(gmix_ref)
        resid_ref[...] = jnp.zeros_like(resid_ref)


def middle(x, mixed, cotangent, lengths, gathered, w_down, vec):
    rows, width = x.shape
    inner = w_down.shape[0]
    seq = rows // lengths.shape[0]
    once = pl.Buffered(1)
    thin = pl.BlockSpec((ROWS, width), lambda i, ln: (i, 0))
    wide = pl.BlockSpec((ROWS, inner), lambda i, ln: (i, 0))
    grid_spec = pltpu.PrefetchScalarGridSpec(
        num_scalar_prefetch=1,
        grid=(rows // ROWS,),
        in_specs=[
            thin,
            thin,
            thin,
            pl.BlockSpec((width, width), lambda i, ln: (0, inner // width), pipeline_mode=once),
            pl.BlockSpec((width, inner), lambda i, ln: (0, 0), pipeline_mode=once),
            pl.BlockSpec((inner, width), lambda i, ln: (0, 0), pipeline_mode=once),
            pl.BlockSpec(vec.shape, lambda i, ln: (0, 0)),
        ],
        out_specs=[
            thin,
            thin,
            wide,
            wide,
            thin,
            thin,
            thin,
            thin,
            pl.BlockSpec(vec.shape, lambda i, ln: (0, 0)),
        ],
        scratch_shapes=[pltpu.VMEM((ROWS, inner), F32)],
    )
    low = jax.ShapeDtypeStruct((rows, width), BF)
    low_wide = jax.ShapeDtypeStruct((rows, inner), BF)
    return pl.pallas_call(
        functools.partial(middle_kernel, seq=seq),
        grid_spec=grid_spec,
        out_shape=[
            low,
            low,
            low_wide,
            low_wide,
            low,
            low,
            low,
            jax.ShapeDtypeStruct((rows, width), F32),
            jax.ShapeDtypeStruct(vec.shape, F32),
        ],
        compiler_params=params(1),
        cost_estimate=cost(
            8 * rows * width * inner + 4 * rows * width * width,
            rows * (4 * inner + 20 * width) + 4 * width * inner,
            2 * rows * inner,
        ),
        name="middle",
    )(lengths, x, mixed, cotangent, gathered, gathered, w_down, vec)


def weight_kernel(src_ref, left_ref, right_ref, *refs, sums):
    keep_ref, send_ref, acc_ref = refs[0], refs[1], refs[-1]
    half, piece, _ = keep_ref.shape
    right = right_ref[0] if len(right_ref.shape) == 3 else right_ref[...]
    acc_ref[...] = dot(left_ref[...], right, TN)
    if sums:
        refs[2][0] = jnp.broadcast_to(column_sum(right.astype(F32)), refs[2].shape[1:])
    for slot in range(half):
        for ref, offset in ((keep_ref, 0), (send_ref, half)):
            begin = pl.multiple_of(src_ref[offset + slot] * piece, 8)
            ref[slot] = acc_ref[pl.ds(begin, piece), :].astype(BF)


def plain_weight_kernel(left_ref, right_ref, out_ref, *refs):
    right = right_ref[0] if len(right_ref.shape) == 3 else right_ref[...]
    out_ref[...] = dot(left_ref[...], right, TN).astype(BF)
    if refs:
        refs[0][0] = jnp.broadcast_to(column_sum(right.astype(F32)), refs[0].shape[1:])


def weight_gradient(left, right, source, sums=False):
    rows, tall = left.shape
    devices = source.shape[0]
    piece = tall // devices
    if right.ndim == 3:
        steps, _, tile = right.shape
        right_block = pl.BlockSpec((1, rows, tile), lambda j, *s: (j, 0, 0))
    else:
        tile = min(right.shape[1], 768)
        steps = right.shape[1] // tile
        right_block = pl.BlockSpec((rows, tile), lambda j, *s: (0, j))
    left_block = pl.BlockSpec((rows, tall), lambda j, *s: (0, 0))
    extra_specs = [pl.BlockSpec((1, 8, tile), lambda j, *s: (j, 0, 0))] if sums else []
    extra_shapes = [jax.ShapeDtypeStruct((steps, 8, tile), F32)] if sums else []
    estimate = cost(
        2 * rows * tall * tile * steps,
        2 * tall * tile * steps + 2 * rows * (tall + tile * steps),
        longer=64,
    )
    if piece % 8:
        whole, *rest = pl.pallas_call(
            plain_weight_kernel,
            grid=(steps,),
            in_specs=[left_block, right_block],
            out_specs=[pl.BlockSpec((tall, tile), lambda j: (0, j))] + extra_specs,
            out_shape=[jax.ShapeDtypeStruct((tall, steps * tile), BF)] + extra_shapes,
            compiler_params=params(1),
            cost_estimate=estimate,
            name="weight_gradient",
        )(left, right)
        ordered = jnp.take(whole.reshape(devices, piece, steps * tile), source, axis=0)
        return (ordered[: devices // 2], ordered[devices // 2 :], *rest)
    block = pl.BlockSpec((devices // 2, piece, tile), lambda j, s: (0, 0, j))
    shape = jax.ShapeDtypeStruct((devices // 2, piece, steps * tile), BF)
    grid_spec = pltpu.PrefetchScalarGridSpec(
        num_scalar_prefetch=1,
        grid=(steps,),
        in_specs=[left_block, right_block],
        out_specs=[block, block] + extra_specs,
        scratch_shapes=[pltpu.VMEM((tall, tile), F32)],
    )
    return pl.pallas_call(
        functools.partial(weight_kernel, sums=sums),
        grid_spec=grid_spec,
        out_shape=[shape, shape] + extra_shapes,
        compiler_params=params(1),
        cost_estimate=estimate,
        name="weight_gradient",
    )(source, left, right)


def joint_kernel(src_ref, left_ref, last_left_ref, right_ref, last_right_ref, keep_ref, send_ref, acc_ref):
    half, piece, _ = keep_ref.shape
    last = pl.num_programs(0) - 1

    @pl.when(pl.program_id(0) < last)
    def _():
        acc_ref[...] = dot(left_ref[...], right_ref[...], TN)

    @pl.when(pl.program_id(0) == last)
    def _():
        acc_ref[...] = dot(last_left_ref[...], last_right_ref[...], TN)

    for slot in range(half):
        for ref, offset in ((keep_ref, 0), (send_ref, half)):
            begin = pl.multiple_of(src_ref[offset + slot] * piece, 8)
            ref[slot] = acc_ref[pl.ds(begin, piece), :].astype(BF)


def joint_gradient(left, right, last_left, last_right, source):
    rows, tall = left.shape
    devices = source.shape[0]
    piece = tall // devices
    tile = last_right.shape[1]
    wide = right.shape[1] // tile
    if piece % 8:
        one = weight_gradient(left, right, source)
        two = weight_gradient(last_left, last_right, source)
        return [jnp.concatenate(both, axis=2) for both in zip(one, two)]
    full = pl.BlockSpec((rows, tall), lambda j, s: (0, 0))
    block = pl.BlockSpec((devices // 2, piece, tile), lambda j, s: (0, 0, j))
    shape = jax.ShapeDtypeStruct((devices // 2, piece, (wide + 1) * tile), BF)
    grid_spec = pltpu.PrefetchScalarGridSpec(
        num_scalar_prefetch=1,
        grid=(wide + 1,),
        in_specs=[
            full,
            full,
            pl.BlockSpec((rows, tile), lambda j, s: (0, jnp.minimum(j, wide - 1))),
            pl.BlockSpec((rows, tile), lambda j, s: (0, 0)),
        ],
        out_specs=[block, block],
        scratch_shapes=[pltpu.VMEM((tall, tile), F32)],
    )
    return pl.pallas_call(
        joint_kernel,
        grid_spec=grid_spec,
        out_shape=[shape, shape],
        compiler_params=params(1),
        cost_estimate=cost(
            2 * rows * tall * tile * (wide + 1),
            2 * (tall + rows) * tile * (wide + 1) + 4 * rows * tall,
            longer=8,
        ),
        name="joint_gradient",
    )(source, left, last_left, right, last_right)


def tall_kernel(slot_ref, left_ref, right_ref, keep_ref, send_ref, acc_ref):
    step = pl.program_id(0)
    half, piece, _ = keep_ref.shape
    here = left_ref.shape[1] // piece
    acc_ref[...] = dot(left_ref[...], right_ref[...], TN)
    for index in range(here):
        slot = slot_ref[step * here + index]
        part = acc_ref[index * piece : (index + 1) * piece, :].astype(BF)

        @pl.when(slot < half)
        def _():
            keep_ref[jnp.minimum(slot, half - 1)] = part

        @pl.when(slot >= half)
        def _():
            send_ref[jnp.maximum(slot - half, 0)] = part


def plain_tall_kernel(left_ref, right_ref, out_ref):
    out_ref[...] = dot(left_ref[...], right_ref[...], TN).astype(BF)


def tall_gradient(left, right, source, slot_of):
    rows, tall = left.shape
    width = right.shape[1]
    devices = source.shape[0]
    piece = tall // devices
    steps = tall // width
    left_block = pl.BlockSpec((rows, width), lambda j, *s: (0, j))
    right_block = pl.BlockSpec((rows, width), lambda j, *s: (0, 0))
    estimate = cost(2 * rows * tall * width, 2 * tall * width + 2 * rows * (tall + width))
    if piece % 16:
        whole = pl.pallas_call(
            plain_tall_kernel,
            grid=(steps,),
            in_specs=[left_block, right_block],
            out_specs=pl.BlockSpec((width, width), lambda j: (j, 0)),
            out_shape=jax.ShapeDtypeStruct((tall, width), BF),
            compiler_params=params(1),
            cost_estimate=estimate,
            name="tall_gradient",
        )(left, right)
        ordered = jnp.take(whole.reshape(devices, piece, width), source, axis=0)
        return (ordered[: devices // 2], ordered[devices // 2 :])
    block = pl.BlockSpec((devices // 2, piece, width), lambda j, s: (0, 0, 0))
    shape = jax.ShapeDtypeStruct((devices // 2, piece, width), BF)
    grid_spec = pltpu.PrefetchScalarGridSpec(
        num_scalar_prefetch=1,
        grid=(steps,),
        in_specs=[left_block, right_block],
        out_specs=[block, block],
        scratch_shapes=[pltpu.VMEM((width, width), F32)],
    )
    return pl.pallas_call(
        tall_kernel,
        grid_spec=grid_spec,
        out_shape=[shape, shape],
        compiler_params=params(1),
        cost_estimate=estimate,
        name="tall_gradient",
    )(slot_of, left, right)


def input_kernel(resid_ref, w_ref, *refs, groups):
    out_ref = refs[-1]
    width = resid_ref.shape[1]
    total = resid_ref[...]
    for group, grad_ref in enumerate(refs[:groups]):
        here = grad_ref.shape[2]
        for part in range(3):
            total = total + dot(grad_ref[part], w_ref[:, pl.ds(part * width + group * here, here)], NT)
    out_ref[...] = total.astype(BF)


def input_gradient(resid, gathered, grads, which, batch, filled):
    rows, width = resid.shape
    steps = rows // batch // ROWS
    base = which * steps
    return pl.pallas_call(
        functools.partial(input_kernel, groups=len(grads)),
        grid=(steps,),
        in_specs=[
            pl.BlockSpec((ROWS, width), lambda i: (base + i, 0)),
            pl.BlockSpec((width, 3 * width), lambda i: (0, 0), pipeline_mode=pl.Buffered(1)),
        ]
        + [pl.BlockSpec((3, ROWS, grad.shape[2]), lambda i: (0, base + i, 0)) for grad in grads]
        + [pl.BlockSpec(memory_space=pl.ANY)] * len(filled),
        out_specs=pl.BlockSpec((ROWS, width), lambda i: (base + i, 0)),
        out_shape=jax.ShapeDtypeStruct((rows, width), BF),
        input_output_aliases={2 + len(grads): 0} if filled else {},
        compiler_params=params(1),
        cost_estimate=cost(
            6 * rows * width * width // batch,
            (12 * rows * width + 6 * width * width) // batch,
            longer=64,
        ),
        name="input_gradient",
    )(resid, gathered, *grads, *filled)


def swap(value, mask, devices):
    return lax.ppermute(value, "dp", [(index, index ^ mask) for index in range(devices)])


def hold(value, *others):
    return lax.optimization_barrier((value, others))[0]


def masks_of(bits):
    found = [0]
    for bit in bits:
        found = found + [mask | (1 << bit) for mask in found]
    return found


def relative_order(order):
    relative = [0]
    for bits in order:
        relative = [base | mask for base in relative for mask in masks_of(bits)]
    return relative


def stage_orders(devices):
    bits = devices.bit_length() - 1
    rest = [(bit,) for bit in range(3, bits)]
    low = [(bit,) for bit in range(min(3, bits))]
    by_x = low + rest
    by_y = low[:1] + low[1:][::-1] + rest
    both = low[:1] + ([tuple(range(1, min(3, bits)))] if bits > 1 else []) + rest
    return by_x, by_y, both


class Reduce:
    def __init__(self, keep, send, order, devices):
        self.order, self.devices, self.at = order, devices, 0
        self.parts = [keep, send]
        self.terms = None

    def send(self):
        masks = masks_of(self.order[self.at])
        self.terms = [self.parts[0]] + [
            swap(part, mask, self.devices) for part, mask in zip(self.parts[1:], masks[1:])
        ]
        self.at += 1
        return self

    def total(self, begin, size):
        result = self.terms[0][begin : begin + size].astype(F32)
        for term in self.terms[1:]:
            result = result + term[begin : begin + size].astype(F32)
        return result

    def join(self):
        ways = len(masks_of(self.order[self.at]))
        size = self.terms[0].shape[0] // ways
        self.parts = [self.total(way * size, size).astype(BF) for way in range(ways)]
        return self

    def after(self, *values):
        self.terms = list(lax.optimization_barrier((tuple(self.terms), values))[0])
        return self

    def finish(self):
        if self.terms is None:
            self.send()
        while self.at < len(self.order):
            self.join().send()
        return self.total(0, 1)[0]


class Gather:
    def __init__(self, shard, order, devices):
        self.order, self.devices, self.at = order, devices, 0
        self.held = shard[None]
        self.taken = None

    def send(self):
        masks = masks_of(self.order[self.at])
        self.taken = [swap(self.held, mask, self.devices) for mask in masks[1:]]
        self.at += 1
        return self

    def join(self):
        self.held = jnp.concatenate([self.held] + self.taken, axis=0)
        return self


def lay_pairs_kernel(index_ref, odd_ref, held_ref, taken_ref, out_ref):
    half, piece, _ = held_ref.shape
    odd = odd_ref[0] == 1
    for slot in range(half):
        mine = held_ref[slot].astype(F32)
        other = taken_ref[slot].astype(F32)
        both = jnp.concatenate(
            [jnp.where(odd, other, mine), jnp.where(odd, mine, other)], axis=0
        ).astype(BF)
        begin = pl.multiple_of((index_ref[slot] // 2) * (2 * piece), 16)
        out_ref[pl.ds(begin, 2 * piece), :] = both


def lay_kernel(index_ref, odd_ref, held_ref, taken_ref, out_ref):
    half, piece, _ = held_ref.shape
    for slot in range(half):
        for ref, flip in ((held_ref, 0), (taken_ref, 1)):
            begin = pl.multiple_of((index_ref[slot] ^ flip) * piece, 16)
            out_ref[pl.ds(begin, piece), :] = ref[slot]


def lay_out(gather, me):
    held, taken = gather.held, gather.taken[0]
    half, piece, columns = held.shape
    devices = 2 * half
    relative = [0]
    for bits in gather.order[:-1]:
        relative = [base | mask for mask in masks_of(bits) for base in relative]
    index = jnp.asarray(relative, jnp.int32) ^ me
    if piece % 8:
        where = [0] * devices
        for slot, value in enumerate(relative):
            where[value], where[value ^ 1] = slot, half + slot
        natural = jnp.take(jnp.asarray(where, jnp.int32), jnp.arange(devices, dtype=jnp.int32) ^ me)
        both = jnp.concatenate([held, taken], axis=0)
        return jnp.take(both, natural, axis=0).reshape(devices * piece, columns)
    whole = pl.BlockSpec(held.shape, lambda i, *s: (0, 0, 0))
    grid_spec = pltpu.PrefetchScalarGridSpec(
        num_scalar_prefetch=2,
        grid=(1,),
        in_specs=[whole, whole],
        out_specs=pl.BlockSpec((devices * piece, columns), lambda i, *s: (0, 0)),
    )
    return pl.pallas_call(
        lay_pairs_kernel if piece % 16 else lay_kernel,
        grid_spec=grid_spec,
        out_shape=jax.ShapeDtypeStruct((devices * piece, columns), BF),
        compiler_params=params(1),
        cost_estimate=cost(devices * piece * columns, 4 * devices * piece * columns),
        name="lay_out",
    )(index, (me & 1).reshape(1), held, taken)


def adamw(weight, grad, first, second, decay, rate):
    new_first = BETA_ONE * first + (1.0 - BETA_ONE) * grad
    new_second = BETA_TWO * second + (1.0 - BETA_TWO) * grad * grad
    corrected = new_first / (1.0 - BETA_ONE**STEP)
    scale_sq = new_second / (1.0 - BETA_TWO**STEP)
    new_weight = weight - rate * (corrected / (jnp.sqrt(scale_sq) + EPSILON_ADAM) + decay * weight)
    return (new_first, new_second, new_weight)


def on_device(
    hidden_in,
    lengths,
    cotangent,
    proj_qkv,
    proj_attn,
    proj_up,
    proj_down,
    vectors,
    first_qkv,
    first_attn,
    first_up,
    first_down,
    first_vectors,
    second_qkv,
    second_attn,
    second_up,
    second_down,
    second_vectors,
):
    devices = lax.axis_size("dp")
    me = lax.axis_index("dp")
    width = hidden_in.shape[1]
    piece = proj_qkv.shape[0]
    inner = proj_up.shape[1]
    batch = lengths.shape[0]
    by_x, by_y, both = stage_orders(devices)
    outward = both[::-1]

    def source_of(order):
        return jnp.asarray(relative_order(order), jnp.int32) ^ me

    slots = [0] * devices
    for slot, value in enumerate(relative_order(by_x)):
        slots[value] = slot
    slot_of = jnp.take(jnp.asarray(slots, jnp.int32), jnp.arange(devices, dtype=jnp.int32) ^ me)

    entries = vectors.shape[0] // piece
    wide = lax.all_gather(
        jnp.concatenate([proj_up.astype(BF), proj_attn.astype(BF)], axis=1), "dp", axis=0, tiled=True
    )
    shard = jnp.concatenate(
        [
            proj_qkv.astype(BF),
            jnp.pad(vectors.astype(BF).reshape(piece, entries), ((0, 0), (0, LANES - entries))),
        ],
        axis=1,
    )
    qkv = Gather(shard, outward, devices)
    down = Gather(proj_down.astype(BF), outward, devices)
    for _ in range(len(outward) - 2):
        qkv.send().join()
    down.held = hold(down.held, qkv.held)
    qkv.send()
    for _ in range(len(outward) - 2):
        down.send().join()
    qkv.join()
    down.held = hold(down.held, qkv.held)
    qkv.held = hold(qkv.held, down.held)
    down.send()
    qkv.send()
    gathered = lay_out(qkv, me)
    vec = gathered[:, 3 * width : 3 * width + entries].astype(F32).reshape(-1, width)

    packed = project_qkv(hidden_in, gathered, vec)
    filled = ()
    for which in range(batch):
        filled = attend_forward(packed, lengths, width, which, filled)
        if which == 0:
            down.taken = [hold(value, filled) for value in down.taken]
            down.join()
            packed = hold(packed, down.held)
            down.send()
    mixed, lse = filled
    w_down = lay_out(down, me)
    output, first_low, active, grad_upper, grad_branch, grad_attn, grad_mixed, grad_one, sums = middle(
        hidden_in, mixed, cotangent, lengths, wide, w_down, vec
    )

    total = Reduce(*tall_gradient(active, grad_branch, source_of(by_x), slot_of), by_x, devices)
    total.send()
    grad_upper = hold(grad_upper, total.parts)
    joint = Reduce(
        *joint_gradient(first_low, grad_upper, mixed, grad_attn, source_of(by_y)), by_y, devices
    )
    total.after(joint.parts).join()
    grad_mixed = hold(grad_mixed, total.parts, joint.parts)
    total.send()
    joint.send()
    parts, part_sums, queue = [], [], []
    for group in range(GROUPS):
        final = group == GROUPS - 1
        part = ()
        for which in range(batch):
            part = (attend_backward(packed, lengths, lse, grad_mixed, group, which, part),)
            if which == 0 and group < 2:
                chain = joint if group == 0 else queue[0]
                chain.after(part).join()
                grad_mixed = hold(grad_mixed, chain.parts)
                chain.send()
        left = hidden_in
        if final:
            for chain in (joint, total, *queue):
                chain.after(part).join()
            left = hold(hidden_in, *(chain.parts for chain in (joint, total, *queue)))
            for chain in (joint, total, *queue):
                chain.send()
        order = both if final else by_x
        keep, send, part_sum = weight_gradient(left, part[0], source_of(order), sums=True)
        parts.append(part[0])
        part_sums.append(part_sum)
        if group == 0:
            queue.append(Reduce(keep, send, order, devices).send())
            total.after(keep).join()
            grad_mixed = hold(grad_mixed, total.parts, keep)
            total.send()
    part_sums = jnp.concatenate(part_sums, axis=2)
    vector_sums = jnp.concatenate([part_sums[0, :1], part_sums[2, :1], sums[2:]], axis=0)
    ordered = jnp.take(vector_sums.reshape(devices, piece, entries), source_of(both), axis=0)
    ordered = jnp.pad(ordered.astype(BF), ((0, 0), (0, 0), (0, LANES - entries)))
    keep = jnp.concatenate([keep, ordered[: devices // 2]], axis=2)
    send = jnp.concatenate([send, ordered[devices // 2 :]], axis=2)
    queue.append(Reduce(keep, send, both, devices).send())
    grad_one = hold(grad_one, send)
    filled = ()
    for which in range(batch):
        if which == batch - 1:
            for chain in (queue[1], joint, total, queue[0]):
                chain.after(filled).join()
            grad_one = hold(grad_one, *(chain.parts for chain in (joint, total, *queue)))
            for chain in (queue[1], joint, total, queue[0]):
                chain.send()
        filled = (input_gradient(grad_one, gathered, parts, which, batch, filled),)
    input_grad = filled[0]
    for chain in (joint, total, *queue):
        chain.after(filled)

    total_qkv = [chain.finish() for chain in queue]
    total_vectors = total_qkv[1][:, 3 * width // GROUPS : 3 * width // GROUPS + entries].reshape(-1)
    here = width // GROUPS
    total_qkv = jnp.concatenate(
        [part[:, at * here : (at + 1) * here] for at in range(3) for part in total_qkv], axis=1
    )
    total_wide = joint.finish()
    total_up, total_attn = total_wide[:, :inner], total_wide[:, inner:]
    total_down = total.finish()

    m_qkv, v_qkv, w_qkv = adamw(proj_qkv, total_qkv, first_qkv, second_qkv, WEIGHT_DECAY, LEARN_RATE)
    m_attn, v_attn, w_attn = adamw(
        proj_attn, total_attn, first_attn, second_attn, WEIGHT_DECAY, LEARN_RATE
    )
    m_up, v_up, w_up = adamw(proj_up, total_up, first_up, second_up, WEIGHT_DECAY, LEARN_RATE)
    m_down, v_down, w_down = adamw(
        proj_down, total_down, first_down, second_down, WEIGHT_DECAY, LEARN_RATE
    )
    m_vec, v_vec, w_vec = adamw(
        vectors, total_vectors, first_vectors, second_vectors, 0.0, LEARN_RATE_VECTOR
    )
    return (
        output,
        input_grad,
        m_qkv,
        v_qkv,
        w_qkv,
        m_attn,
        v_attn,
        w_attn,
        m_up,
        v_up,
        w_up,
        m_down,
        v_down,
        w_down,
        m_vec,
        v_vec,
        w_vec,
    )


def solution(mesh):
    rows, flat = P("dp", None), P("dp")
    return jax.shard_map(
        on_device,
        mesh=mesh,
        in_specs=(rows, flat, rows) + (rows, rows, rows, rows, flat) * 3,
        out_specs=(rows, rows) + (rows,) * 12 + (flat,) * 3,
        check_vma=False,
    )
```

```python
import functools
import math

import jax
import jax.numpy as jnp
from jax import lax
from jax.experimental import pallas as pl
from jax.experimental.pallas import tpu as pltpu
from jax.sharding import PartitionSpec as P

HEAD = 64
STEP = 10

EPSILON_NORM = 1e-05
BETA_ONE = 0.9
BETA_TWO = 0.999
LEARN_RATE = 0.1
LEARN_RATE_VECTOR = 0.4
WEIGHT_DECAY = 0.01
EPSILON_ADAM = 1e-08

LANES = 128
ROWS = 256
VMEM_BYTES = 56 * 1024 * 1024
BF = jnp.bfloat16
F32 = jnp.float32

NN = (((1,), (0,)), ((), ()))
NT = (((1,), (1,)), ((), ()))
TN = (((0,), (0,)), ((), ()))


def dot(left, right, dims=NN):
    return lax.dot_general(left, right, dims, preferred_element_type=F32)


def params(grid_rank):
    return pltpu.CompilerParams(
        dimension_semantics=("arbitrary",) * grid_rank, vmem_limit_bytes=VMEM_BYTES
    )


def cost(flops, moved, exps=0, longer=1):
    return pl.CostEstimate(
        flops=longer * int(flops), bytes_accessed=int(moved), transcendentals=int(exps)
    )


def qkv_kernel(x_ref, w_ref, vec_ref, out_ref):
    width = x_ref.shape[1]
    x = x_ref[...]
    for part in range(3):
        cols = pl.ds(part * width, width)
        value = dot(x, w_ref[:, cols])
        if part == 0:
            value = value + vec_ref[0:1, :]
        if part == 2:
            value = value + vec_ref[1:2, :]
        out_ref[:, cols] = value.astype(BF)


def project_qkv(x, gathered, vec):
    rows, width = x.shape
    return pl.pallas_call(
        qkv_kernel,
        grid=(rows // ROWS,),
        in_specs=[
            pl.BlockSpec((ROWS, width), lambda i: (i, 0)),
            pl.BlockSpec((width, 3 * width), lambda i: (0, 0), pipeline_mode=pl.Buffered(1)),
            pl.BlockSpec(vec.shape, lambda i: (0, 0)),
        ],
        out_specs=pl.BlockSpec((ROWS, 3 * width), lambda i: (i, 0)),
        out_shape=jax.ShapeDtypeStruct((rows, 3 * width), BF),
        compiler_params=params(1),
        cost_estimate=cost(6 * rows * width * width, 2 * (4 * rows * width + 3 * width * width)),
        name="project_qkv",
    )(x, gathered, vec)


def attend_kernel(len_ref, q_ref, k_ref, v_ref, *refs, which):
    out_ref, lse_ref = refs[-2:]
    length = len_ref[which]
    seq = q_ref.shape[0]
    query = q_ref[...] * jnp.asarray(1.0 / math.sqrt(HEAD), BF)
    keyset = k_ref[...]
    val_t = v_ref[...].T
    lane = lax.broadcasted_iota(jnp.int32, (seq, LANES), 1)
    alive = lax.broadcasted_iota(jnp.int32, (seq, seq), 0) < length
    mixed = []
    for head in range(2):
        mine = (lane < HEAD) if head == 0 else (lane >= HEAD)
        scores = dot(keyset, jnp.where(mine, query, jnp.zeros_like(query)), NT)
        scores = jnp.where(alive, scores, -1e30)
        highest = jnp.max(scores, axis=0, keepdims=True)
        expo = jnp.exp(scores - highest)
        summed = jnp.sum(expo, axis=0, keepdims=True)
        probs = (expo * (1.0 / summed)).astype(BF)
        mixed.append(dot(val_t[head * HEAD : (head + 1) * HEAD], probs))
        lse_ref[0, head : head + 1, :] = highest + jnp.log(summed)
    out_ref[...] = jnp.concatenate(mixed, axis=0).T.astype(BF)


def attend_forward(packed, lengths, width, which, filled):
    rows = packed.shape[0]
    batch = lengths.shape[0]
    seq = rows // batch
    pairs = width // LANES
    grid_spec = pltpu.PrefetchScalarGridSpec(
        num_scalar_prefetch=1,
        grid=(pairs,),
        in_specs=[
            pl.BlockSpec((seq, LANES), lambda h, ln: (which, h)),
            pl.BlockSpec((seq, LANES), lambda h, ln: (which, pairs + h)),
            pl.BlockSpec((seq, LANES), lambda h, ln: (which, 2 * pairs + h)),
        ]
        + [pl.BlockSpec(memory_space=pl.ANY)] * len(filled),
        out_specs=[
            pl.BlockSpec((seq, LANES), lambda h, ln: (which, h)),
            pl.BlockSpec((1, 2, seq), lambda h, ln: (which * pairs + h, 0, 0)),
        ],
    )
    return pl.pallas_call(
        functools.partial(attend_kernel, which=which),
        grid_spec=grid_spec,
        out_shape=[
            jax.ShapeDtypeStruct((rows, width), BF),
            jax.ShapeDtypeStruct((batch * pairs, 2, seq), F32),
        ],
        input_output_aliases={4 + index: index for index in range(len(filled))},
        compiler_params=params(1),
        cost_estimate=cost(16 * seq * seq * width, 8 * seq * width, seq * seq * width // HEAD),
        name="attend_forward",
    )(lengths, packed, packed, packed, *filled)


def attend_back_kernel(len_ref, q_ref, k_ref, v_ref, g_ref, lse_ref, *refs, which):
    out_ref = refs[-1]
    length = len_ref[which]
    seq = q_ref.shape[0]
    factor = 1.0 / math.sqrt(HEAD)
    query = q_ref[...] * jnp.asarray(factor, BF)
    keyset = k_ref[...]
    valset = v_ref[...]
    grad = g_ref[...]
    key_t = keyset.T
    lane = lax.broadcasted_iota(jnp.int32, (seq, LANES), 1)
    alive = lax.broadcasted_iota(jnp.int32, (seq, seq), 0) < length
    grad_q = []
    grad_k = 0.0
    grad_v = 0.0
    for head in range(2):
        mine = (lane < HEAD) if head == 0 else (lane >= HEAD)
        query_h = jnp.where(mine, query, jnp.zeros_like(query))
        grad_h = jnp.where(mine, grad, jnp.zeros_like(grad))
        scores = jnp.where(alive, dot(keyset, query_h, NT), -1e30)
        probs = jnp.exp(scores - lse_ref[0, head : head + 1, :])
        grad_probs = dot(valset, grad_h, NT)
        total = jnp.sum(probs * grad_probs, axis=0, keepdims=True)
        grad_scores = (probs * (grad_probs - total)).astype(BF)
        grad_v = grad_v + dot(probs.astype(BF), grad_h)
        grad_k = grad_k + dot(grad_scores, query_h)
        grad_q.append(dot(key_t[head * HEAD : (head + 1) * HEAD], grad_scores))
    out_ref[0] = (jnp.concatenate(grad_q, axis=0).T * factor).astype(BF)
    out_ref[1] = grad_k.astype(BF)
    out_ref[2] = grad_v.astype(BF)


def pair_groups(pairs):
    first = 2 * pairs // 3
    return ((0, first), (first, pairs - first))


def attend_backward(packed, lengths, lse, grad_mixed, span, which, filled):
    rows, width = grad_mixed.shape
    batch = lengths.shape[0]
    seq = rows // batch
    pairs = width // LANES
    base, here = span
    grid_spec = pltpu.PrefetchScalarGridSpec(
        num_scalar_prefetch=1,
        grid=(here,),
        in_specs=[
            pl.BlockSpec((seq, LANES), lambda h, ln: (which, base + h)),
            pl.BlockSpec((seq, LANES), lambda h, ln: (which, pairs + base + h)),
            pl.BlockSpec((seq, LANES), lambda h, ln: (which, 2 * pairs + base + h)),
            pl.BlockSpec((seq, LANES), lambda h, ln: (which, base + h)),
            pl.BlockSpec((1, 2, seq), lambda h, ln: (which * pairs + base + h, 0, 0)),
        ]
        + [pl.BlockSpec(memory_space=pl.ANY)] * len(filled),
        out_specs=pl.BlockSpec((3, seq, LANES), lambda h, ln: (0, which, h)),
    )
    return pl.pallas_call(
        functools.partial(attend_back_kernel, which=which),
        grid_spec=grid_spec,
        out_shape=jax.ShapeDtypeStruct((3, rows, here * LANES), BF),
        input_output_aliases={6 + index: index for index in range(len(filled))},
        compiler_params=params(1),
        cost_estimate=cost(
            40 * seq * seq * here * LANES, 14 * seq * here * LANES, seq * seq * here * 2, 8
        ),
        name="attend_backward",
    )(lengths, packed, packed, packed, grad_mixed, lse, *filled)


def norm_forward(resid, gain, shift):
    centred = resid - jnp.mean(resid, axis=-1, keepdims=True)
    inverse = lax.rsqrt(jnp.mean(centred * centred, axis=-1, keepdims=True) + EPSILON_NORM)
    scaled = centred * inverse
    return (scaled * gain + shift, scaled, inverse)


def norm_backward(grad, scaled, inverse, gain):
    grad_scaled = grad * gain
    return inverse * (
        grad_scaled
        - jnp.mean(grad_scaled, axis=-1, keepdims=True)
        - scaled * jnp.mean(grad_scaled * scaled, axis=-1, keepdims=True)
    )


def column_sum(value):
    return jnp.sum(value, axis=0, keepdims=True)


def middle_kernel(
    len_ref,
    x_ref,
    mixed_ref,
    cot_ref,
    w_attn,
    w_up,
    w_down,
    vec_ref,
    out_ref,
    first_ref,
    active_ref,
    upper_ref,
    branch_ref,
    attn_ref,
    gmix_ref,
    resid_ref,
    sum_ref,
    slope_ref,
    *down_refs,
    seq,
    piece,
):
    step = pl.program_id(0)
    rows, width = x_ref.shape
    chunks = w_up.shape[1] // width
    if down_refs:
        columns_ref, w_down = w_down, down_refs[0]

        @pl.when(step == 0)
        def _():
            def lay(pair, carry):
                begin = pl.multiple_of(pair * 2 * piece, 16)
                strips = [
                    columns_ref[pl.ds(begin, 2 * piece), pl.ds(j * width, width)].astype(F32)
                    for j in range(chunks)
                ]
                both = [strip[:piece] for strip in strips] + [strip[piece:] for strip in strips]
                there = pl.multiple_of(pair * 2 * chunks * piece, 16)
                w_down[pl.ds(there, 2 * chunks * piece), :] = jnp.concatenate(both, axis=0).astype(BF)
                return carry

            lax.fori_loop(0, width // (2 * piece), lay, 0)

    start = (step * rows) % seq
    length = len_ref[(step * rows) // seq]

    def vec(index):
        return vec_ref[index : index + 1, :]

    gain_one, shift_one, gain_two, shift_two = vec(8), vec(9), vec(10), vec(11)

    @pl.when(step == 0)
    def _():
        sum_ref[...] = jnp.zeros_like(sum_ref)

    resid_one = x_ref[...].astype(F32) + dot(mixed_ref[...], w_attn[...]) + vec(2)
    first, scaled_one, inverse_one = norm_forward(resid_one, gain_one, shift_one)
    first_low = first.astype(BF)
    first_ref[...] = first_low
    total = first + vec(7)
    for j in range(chunks):
        cols = pl.ds(j * width, width)
        upper = dot(first_low, w_up[:, cols]) + vec(3 + j)
        half = 0.5 + 0.5 * lax.erf(upper * (1.0 / math.sqrt(2.0)))
        active = (upper * half).astype(BF)
        active_ref[:, cols] = active
        slope_ref[:, cols] = half + upper * jnp.exp(-0.5 * upper * upper) * (
            1.0 / math.sqrt(2.0 * math.pi)
        )
        total = total + dot(active, w_down[cols, :])
    output, scaled_two, inverse_two = norm_forward(total, gain_two, shift_two)
    out_ref[...] = output.astype(BF)

    @pl.when(start < length)
    def _():
        alive = lax.broadcasted_iota(jnp.int32, (rows, 1), 0) + start < length
        grad_out = jnp.where(alive, cot_ref[...].astype(F32), 0.0)
        grad_two = norm_backward(grad_out, scaled_two, inverse_two, gain_two)
        branch = grad_two.astype(BF)
        branch_ref[...] = branch
        grad_first = grad_two
        for j in range(chunks):
            cols = pl.ds(j * width, width)
            grad_upper = (dot(branch, w_down[cols, :], NT) * slope_ref[:, cols]).astype(BF)
            upper_ref[:, cols] = grad_upper
            sum_ref[3 + j : 4 + j, :] += column_sum(grad_upper.astype(F32))
            grad_first = grad_first + dot(grad_upper, w_up[:, cols], NT)
        grad_one = norm_backward(grad_first, scaled_one, inverse_one, gain_one)
        resid_ref[...] = grad_one
        grad_attn = grad_one.astype(BF)
        attn_ref[...] = grad_attn
        gmix_ref[...] = dot(grad_attn, w_attn[...], NT).astype(BF)
        sum_ref[2:3, :] += column_sum(grad_attn.astype(F32))
        sum_ref[7:8, :] += column_sum(branch.astype(F32))
        sum_ref[8:9, :] += column_sum(grad_first * scaled_one)
        sum_ref[9:10, :] += column_sum(grad_first)
        sum_ref[10:11, :] += column_sum(grad_out * scaled_two)
        sum_ref[11:12, :] += column_sum(grad_out)

    @pl.when(start >= length)
    def _():
        upper_ref[...] = jnp.zeros_like(upper_ref)
        branch_ref[...] = jnp.zeros_like(branch_ref)
        attn_ref[...] = jnp.zeros_like(attn_ref)
        gmix_ref[...] = jnp.zeros_like(gmix_ref)
        resid_ref[...] = jnp.zeros_like(resid_ref)


def middle(x, mixed, cotangent, lengths, gathered, vec, piece):
    rows, width = x.shape
    inner = (gathered.shape[1] - width) // 2
    ratio = inner // width
    if piece % 8:
        w_down = gathered[:, inner + width :].reshape(width // piece, piece, ratio, width)
        w_down = w_down.transpose(0, 2, 1, 3).reshape(inner, width)
        down_block = (inner, width), 0
    else:
        w_down = gathered
        down_block = (width, inner), 1
    seq = rows // lengths.shape[0]
    once = pl.Buffered(1)
    thin = pl.BlockSpec((ROWS, width), lambda i, ln: (i, 0))
    wide = pl.BlockSpec((ROWS, inner), lambda i, ln: (i, 0))
    grid_spec = pltpu.PrefetchScalarGridSpec(
        num_scalar_prefetch=1,
        grid=(rows // ROWS,),
        in_specs=[
            thin,
            thin,
            thin,
            pl.BlockSpec((width, width), lambda i, ln: (0, 2 * ratio), pipeline_mode=once),
            pl.BlockSpec((width, inner), lambda i, ln: (0, 0), pipeline_mode=once),
            pl.BlockSpec(down_block[0], lambda i, ln: (0, down_block[1]), pipeline_mode=once),
            pl.BlockSpec(vec.shape, lambda i, ln: (0, 0)),
        ],
        out_specs=[
            thin,
            thin,
            wide,
            wide,
            thin,
            thin,
            thin,
            thin,
            pl.BlockSpec(vec.shape, lambda i, ln: (0, 0)),
        ],
        scratch_shapes=[pltpu.VMEM((ROWS, inner), F32)]
        + ([] if piece % 8 else [pltpu.VMEM((inner, width), BF)]),
    )
    low = jax.ShapeDtypeStruct((rows, width), BF)
    low_wide = jax.ShapeDtypeStruct((rows, inner), BF)
    return pl.pallas_call(
        functools.partial(middle_kernel, seq=seq, piece=piece),
        grid_spec=grid_spec,
        out_shape=[
            low,
            low,
            low_wide,
            low_wide,
            low,
            low,
            low,
            jax.ShapeDtypeStruct((rows, width), F32),
            jax.ShapeDtypeStruct(vec.shape, F32),
        ],
        compiler_params=params(1),
        cost_estimate=cost(
            8 * rows * width * inner + 4 * rows * width * width,
            rows * (4 * inner + 20 * width) + 4 * width * inner,
            2 * rows * inner,
        ),
        name="middle",
    )(lengths, x, mixed, cotangent, gathered, gathered, w_down, vec)


def weight_kernel(src_ref, left_ref, right_ref, *refs, sums):
    keep_ref, send_ref, acc_ref, turned_ref = refs[0], refs[1], refs[-2], refs[-1]
    half, piece, _ = keep_ref.shape
    right = right_ref[0] if len(right_ref.shape) == 3 else right_ref[...]

    @pl.when(pl.program_id(0) == 0)
    def _():
        turned_ref[...] = left_ref[...].T

    acc_ref[...] = dot(turned_ref[...], right)
    if sums:
        refs[2][0] = jnp.broadcast_to(column_sum(right.astype(F32)), refs[2].shape[1:])
    for slot in range(half):
        for ref, offset in ((keep_ref, 0), (send_ref, half)):
            begin = pl.multiple_of(src_ref[offset + slot] * piece, 8)
            ref[slot] = acc_ref[pl.ds(begin, piece), :].astype(BF)


def plain_weight_kernel(left_ref, right_ref, out_ref, *refs):
    right = right_ref[0] if len(right_ref.shape) == 3 else right_ref[...]
    out_ref[...] = dot(left_ref[...], right, TN).astype(BF)
    if refs:
        refs[0][0] = jnp.broadcast_to(column_sum(right.astype(F32)), refs[0].shape[1:])


def weight_gradient(left, right, source, sums=False):
    rows, tall = left.shape
    devices = source.shape[0]
    piece = tall // devices
    if right.ndim == 3:
        steps, _, tile = right.shape
        right_block = pl.BlockSpec((1, rows, tile), lambda j, *s: (j, 0, 0))
    else:
        tile = min(right.shape[1], 768)
        steps = right.shape[1] // tile
        right_block = pl.BlockSpec((rows, tile), lambda j, *s: (0, j))
    left_block = pl.BlockSpec((rows, tall), lambda j, *s: (0, 0))
    extra_specs = [pl.BlockSpec((1, 8, tile), lambda j, *s: (j, 0, 0))] if sums else []
    extra_shapes = [jax.ShapeDtypeStruct((steps, 8, tile), F32)] if sums else []
    estimate = cost(
        2 * rows * tall * tile * steps,
        2 * tall * tile * steps + 2 * rows * (tall + tile * steps),
        longer=64,
    )
    if piece % 8:
        whole, *rest = pl.pallas_call(
            plain_weight_kernel,
            grid=(steps,),
            in_specs=[left_block, right_block],
            out_specs=[pl.BlockSpec((tall, tile), lambda j: (0, j))] + extra_specs,
            out_shape=[jax.ShapeDtypeStruct((tall, steps * tile), BF)] + extra_shapes,
            compiler_params=params(1),
            cost_estimate=estimate,
            name="weight_gradient",
        )(left, right)
        ordered = jnp.take(whole.reshape(devices, piece, steps * tile), source, axis=0)
        return (ordered[: devices // 2], ordered[devices // 2 :], *rest)
    block = pl.BlockSpec((devices // 2, piece, tile), lambda j, s: (0, 0, j))
    shape = jax.ShapeDtypeStruct((devices // 2, piece, steps * tile), BF)
    grid_spec = pltpu.PrefetchScalarGridSpec(
        num_scalar_prefetch=1,
        grid=(steps,),
        in_specs=[left_block, right_block],
        out_specs=[block, block] + extra_specs,
        scratch_shapes=[pltpu.VMEM((tall, tile), F32), pltpu.VMEM((tall, rows), BF)],
    )
    return pl.pallas_call(
        functools.partial(weight_kernel, sums=sums),
        grid_spec=grid_spec,
        out_shape=[shape, shape] + extra_shapes,
        compiler_params=params(1),
        cost_estimate=estimate,
        name="weight_gradient",
    )(source, left, right)


def joint_kernel(
    src_ref,
    left_ref,
    last_left_ref,
    right_ref,
    last_right_ref,
    keep_ref,
    send_ref,
    acc_ref,
    turned_ref,
):
    half, piece, _ = keep_ref.shape
    last = pl.num_programs(0) - 1

    @pl.when(pl.program_id(0) == 0)
    def _():
        turned_ref[...] = left_ref[...].T

    @pl.when(pl.program_id(0) < last)
    def _():
        acc_ref[...] = dot(turned_ref[...], right_ref[...])

    @pl.when(pl.program_id(0) == last)
    def _():
        acc_ref[...] = dot(last_left_ref[...], last_right_ref[...], TN)

    for slot in range(half):
        for ref, offset in ((keep_ref, 0), (send_ref, half)):
            begin = pl.multiple_of(src_ref[offset + slot] * piece, 8)
            ref[slot] = acc_ref[pl.ds(begin, piece), :].astype(BF)


def joint_gradient(left, right, last_left, last_right, source):
    rows, tall = left.shape
    devices = source.shape[0]
    piece = tall // devices
    tile = last_right.shape[1]
    wide = right.shape[1] // tile
    if piece % 8:
        one = weight_gradient(left, right, source)
        two = weight_gradient(last_left, last_right, source)
        return [jnp.concatenate(both, axis=2) for both in zip(one, two)]
    full = pl.BlockSpec((rows, tall), lambda j, s: (0, 0))
    block = pl.BlockSpec((devices // 2, piece, tile), lambda j, s: (0, 0, j))
    shape = jax.ShapeDtypeStruct((devices // 2, piece, (wide + 1) * tile), BF)
    grid_spec = pltpu.PrefetchScalarGridSpec(
        num_scalar_prefetch=1,
        grid=(wide + 1,),
        in_specs=[
            full,
            full,
            pl.BlockSpec((rows, tile), lambda j, s: (0, jnp.minimum(j, wide - 1))),
            pl.BlockSpec((rows, tile), lambda j, s: (0, 0)),
        ],
        out_specs=[block, block],
        scratch_shapes=[pltpu.VMEM((tall, tile), F32), pltpu.VMEM((tall, rows), BF)],
    )
    return pl.pallas_call(
        joint_kernel,
        grid_spec=grid_spec,
        out_shape=[shape, shape],
        compiler_params=params(1),
        cost_estimate=cost(
            2 * rows * tall * tile * (wide + 1),
            2 * (tall + rows) * tile * (wide + 1) + 4 * rows * tall,
            longer=8,
        ),
        name="joint_gradient",
    )(source, left, last_left, right, last_right)


def tall_kernel(slot_ref, left_ref, right_ref, keep_ref, send_ref, acc_ref):
    step = pl.program_id(0)
    half, piece, _ = keep_ref.shape
    here = left_ref.shape[1] // piece
    acc_ref[...] = dot(left_ref[...], right_ref[...], TN)
    for index in range(here):
        slot = slot_ref[step * here + index]
        part = acc_ref[index * piece : (index + 1) * piece, :].astype(BF)

        @pl.when(slot < half)
        def _():
            keep_ref[jnp.minimum(slot, half - 1)] = part

        @pl.when(slot >= half)
        def _():
            send_ref[jnp.maximum(slot - half, 0)] = part


def plain_tall_kernel(left_ref, right_ref, out_ref):
    out_ref[...] = dot(left_ref[...], right_ref[...], TN).astype(BF)


def tall_gradient(left, right, source, slot_of):
    rows, tall = left.shape
    width = right.shape[1]
    devices = source.shape[0]
    piece = tall // devices
    steps = tall // width
    left_block = pl.BlockSpec((rows, width), lambda j, *s: (0, j))
    right_block = pl.BlockSpec((rows, width), lambda j, *s: (0, 0))
    estimate = cost(2 * rows * tall * width, 2 * tall * width + 2 * rows * (tall + width))
    if piece % 16:
        whole = pl.pallas_call(
            plain_tall_kernel,
            grid=(steps,),
            in_specs=[left_block, right_block],
            out_specs=pl.BlockSpec((width, width), lambda j: (j, 0)),
            out_shape=jax.ShapeDtypeStruct((tall, width), BF),
            compiler_params=params(1),
            cost_estimate=estimate,
            name="tall_gradient",
        )(left, right)
        ordered = jnp.take(whole.reshape(devices, piece, width), source, axis=0)
        return (ordered[: devices // 2], ordered[devices // 2 :])
    block = pl.BlockSpec((devices // 2, piece, width), lambda j, s: (0, 0, 0))
    shape = jax.ShapeDtypeStruct((devices // 2, piece, width), BF)
    grid_spec = pltpu.PrefetchScalarGridSpec(
        num_scalar_prefetch=1,
        grid=(steps,),
        in_specs=[left_block, right_block],
        out_specs=[block, block],
        scratch_shapes=[pltpu.VMEM((width, width), F32)],
    )
    return pl.pallas_call(
        tall_kernel,
        grid_spec=grid_spec,
        out_shape=[shape, shape],
        compiler_params=params(1),
        cost_estimate=estimate,
        name="tall_gradient",
    )(slot_of, left, right)


def input_kernel(resid_ref, w_ref, *refs, groups):
    out_ref = refs[-1]
    width = resid_ref.shape[1]
    total = resid_ref[...]
    base = 0
    for grad_ref in refs[:groups]:
        here = grad_ref.shape[2]
        for part in range(3):
            total = total + dot(grad_ref[part], w_ref[:, pl.ds(part * width + base, here)], NT)
        base += here
    out_ref[...] = total.astype(BF)


def input_gradient(resid, gathered, grads, which, batch, filled):
    rows, width = resid.shape
    steps = rows // batch // ROWS
    base = which * steps
    return pl.pallas_call(
        functools.partial(input_kernel, groups=len(grads)),
        grid=(steps,),
        in_specs=[
            pl.BlockSpec((ROWS, width), lambda i: (base + i, 0)),
            pl.BlockSpec((width, 3 * width), lambda i: (0, 0), pipeline_mode=pl.Buffered(1)),
        ]
        + [pl.BlockSpec((3, ROWS, grad.shape[2]), lambda i: (0, base + i, 0)) for grad in grads]
        + [pl.BlockSpec(memory_space=pl.ANY)] * len(filled),
        out_specs=pl.BlockSpec((ROWS, width), lambda i: (base + i, 0)),
        out_shape=jax.ShapeDtypeStruct((rows, width), BF),
        input_output_aliases={2 + len(grads): 0} if filled else {},
        compiler_params=params(1),
        cost_estimate=cost(
            6 * rows * width * width // batch,
            (12 * rows * width + 6 * width * width) // batch,
            longer=64,
        ),
        name="input_gradient",
    )(resid, gathered, *grads, *filled)


def swap(value, mask, devices):
    return lax.ppermute(value, "dp", [(index, index ^ mask) for index in range(devices)])


def hold(value, *others):
    return lax.optimization_barrier((value, others))[0]


def masks_of(bits):
    found = [0]
    for bit in bits:
        found = found + [mask | (1 << bit) for mask in found]
    return found


def relative_order(order):
    relative = [0]
    for bits in order:
        relative = [base | mask for base in relative for mask in masks_of(bits)]
    return relative


def stage_orders(devices):
    bits = devices.bit_length() - 1
    rest = [(bit,) for bit in range(3, bits)]
    low = [(bit,) for bit in range(min(3, bits))]
    by_x = low + rest
    by_y = low[:1] + low[1:][::-1] + rest
    both = low[:1] + ([tuple(range(1, min(3, bits)))] if bits > 1 else []) + rest
    return by_x, by_y, both


class Reduce:
    def __init__(self, keep, send, order, devices):
        self.order, self.devices, self.at = order, devices, 0
        self.parts = [keep, send]
        self.terms = None

    def send(self):
        masks = masks_of(self.order[self.at])
        self.terms = [self.parts[0]] + [
            swap(part, mask, self.devices) for part, mask in zip(self.parts[1:], masks[1:])
        ]
        self.at += 1
        return self

    def total(self, begin, size):
        result = self.terms[0][begin : begin + size].astype(F32)
        for term in self.terms[1:]:
            result = result + term[begin : begin + size].astype(F32)
        return result

    def join(self):
        ways = len(masks_of(self.order[self.at]))
        size = self.terms[0].shape[0] // ways
        self.parts = [self.total(way * size, size).astype(BF) for way in range(ways)]
        return self

    def after(self, *values):
        self.terms = list(lax.optimization_barrier((tuple(self.terms), values))[0])
        return self

    def finish(self):
        if self.terms is None:
            self.send()
        while self.at < len(self.order):
            self.join().send()
        return self.total(0, 1)[0]


class Gather:
    def __init__(self, shard, order, devices):
        self.order, self.devices, self.at = order, devices, 0
        self.held = shard[None]
        self.taken = None

    def send(self):
        masks = masks_of(self.order[self.at])
        self.taken = [swap(self.held, mask, self.devices) for mask in masks[1:]]
        self.at += 1
        return self

    def join(self):
        self.held = jnp.concatenate([self.held] + self.taken, axis=0)
        return self


def lay_pairs_kernel(index_ref, odd_ref, held_ref, taken_ref, out_ref):
    half, piece, _ = held_ref.shape
    odd = odd_ref[0] == 1
    for slot in range(half):
        mine = held_ref[slot].astype(F32)
        other = taken_ref[slot].astype(F32)
        both = jnp.concatenate(
            [jnp.where(odd, other, mine), jnp.where(odd, mine, other)], axis=0
        ).astype(BF)
        begin = pl.multiple_of((index_ref[slot] // 2) * (2 * piece), 16)
        out_ref[pl.ds(begin, 2 * piece), :] = both


def lay_out(gather, me):
    held, taken = gather.held, gather.taken[0]
    half, piece, columns = held.shape
    devices = 2 * half
    relative = [0]
    for bits in gather.order[:-1]:
        relative = [base | mask for mask in masks_of(bits) for base in relative]
    index = jnp.asarray(relative, jnp.int32) ^ me
    if piece % 8:
        where = [0] * devices
        for slot, value in enumerate(relative):
            where[value], where[value ^ 1] = slot, half + slot
        natural = jnp.take(jnp.asarray(where, jnp.int32), jnp.arange(devices, dtype=jnp.int32) ^ me)
        both = jnp.concatenate([held, taken], axis=0)
        return jnp.take(both, natural, axis=0).reshape(devices * piece, columns)
    tile = columns // 5 if columns % (5 * LANES) == 0 else columns
    block = pl.BlockSpec((half, piece, tile), lambda i, *s: (0, 0, i))
    grid_spec = pltpu.PrefetchScalarGridSpec(
        num_scalar_prefetch=2,
        grid=(columns // tile,),
        in_specs=[block, block],
        out_specs=pl.BlockSpec((devices * piece, tile), lambda i, *s: (0, i)),
    )
    return pl.pallas_call(
        lay_pairs_kernel,
        grid_spec=grid_spec,
        out_shape=jax.ShapeDtypeStruct((devices * piece, columns), BF),
        compiler_params=params(1),
        cost_estimate=cost(devices * piece * columns, 4 * devices * piece * columns),
        name="lay_out",
    )(index, (me & 1).reshape(1), held, taken)


def adamw(weight, grad, first, second, decay, rate):
    new_first = BETA_ONE * first + (1.0 - BETA_ONE) * grad
    new_second = BETA_TWO * second + (1.0 - BETA_TWO) * grad * grad
    corrected = new_first / (1.0 - BETA_ONE**STEP)
    scale_sq = new_second / (1.0 - BETA_TWO**STEP)
    new_weight = weight - rate * (corrected / (jnp.sqrt(scale_sq) + EPSILON_ADAM) + decay * weight)
    return (new_first, new_second, new_weight)


def on_device(
    hidden_in,
    lengths,
    cotangent,
    proj_qkv,
    proj_attn,
    proj_up,
    proj_down,
    vectors,
    first_qkv,
    first_attn,
    first_up,
    first_down,
    first_vectors,
    second_qkv,
    second_attn,
    second_up,
    second_down,
    second_vectors,
):
    devices = lax.axis_size("dp")
    me = lax.axis_index("dp")
    width = hidden_in.shape[1]
    piece = proj_qkv.shape[0]
    inner = proj_up.shape[1]
    batch = lengths.shape[0]
    by_x, by_y, both = stage_orders(devices)
    outward = both[::-1]

    def source_of(order):
        return jnp.asarray(relative_order(order), jnp.int32) ^ me

    slots = [0] * devices
    for slot, value in enumerate(relative_order(by_x)):
        slots[value] = slot
    slot_of = jnp.take(jnp.asarray(slots, jnp.int32), jnp.arange(devices, dtype=jnp.int32) ^ me)

    entries = vectors.shape[0] // piece
    ratio = inner // width
    down_columns = proj_down.astype(BF).reshape(ratio, piece, width).transpose(1, 0, 2)
    wide = lax.all_gather(
        jnp.concatenate(
            [proj_up.astype(BF), down_columns.reshape(piece, inner), proj_attn.astype(BF)], axis=1
        ),
        "dp",
        axis=0,
        tiled=True,
    )
    shard = jnp.concatenate(
        [
            proj_qkv.astype(BF),
            jnp.pad(vectors.astype(BF).reshape(piece, entries), ((0, 0), (0, 2 * LANES - entries))),
        ],
        axis=1,
    )
    qkv = Gather(shard, outward, devices)
    for _ in range(len(outward) - 1):
        qkv.send().join()
    qkv.send()
    gathered = lay_out(qkv, me)
    vec = gathered[:, 3 * width : 3 * width + entries].astype(F32).reshape(-1, width)

    packed = project_qkv(hidden_in, gathered, vec)
    filled = ()
    for which in range(batch):
        filled = attend_forward(packed, lengths, width, which, filled)
    mixed, lse = filled
    output, first_low, active, grad_upper, grad_branch, grad_attn, grad_mixed, grad_one, sums = middle(
        hidden_in, mixed, cotangent, lengths, wide, vec, piece
    )

    total = Reduce(*tall_gradient(active, grad_branch, source_of(by_x), slot_of), by_x, devices)
    total.send()
    grad_upper = hold(grad_upper, total.parts)
    joint = Reduce(
        *joint_gradient(first_low, grad_upper, mixed, grad_attn, source_of(by_y)), by_y, devices
    )
    total.after(joint.parts)
    joint.parts = list(hold(tuple(joint.parts), *total.terms))
    joint.send()
    total.join()
    joint.join()
    grad_mixed = hold(grad_mixed, total.parts, joint.parts)
    total.send()
    joint.send()
    parts, part_sums, queue = [], [], []
    spans = pair_groups(width // LANES)
    for group, span in enumerate(spans):
        final = group == len(spans) - 1
        part = ()
        for which in range(batch):
            part = (attend_backward(packed, lengths, lse, grad_mixed, span, which, part),)
            if which == 0 and final:
                queue[0].after(part).join()
                grad_mixed = hold(grad_mixed, queue[0].parts)
                queue[0].send()
        left = hidden_in
        if final:
            for chain in (joint, total):
                chain.after(part).join()
            left = hold(hidden_in, joint.parts, total.parts)
            for chain in (joint, total):
                chain.send()
        order = both if final else by_x
        keep, send, part_sum = weight_gradient(left, part[0], source_of(order), sums=True)
        parts.append(part[0])
        part_sums.append(part_sum)
        if group == 0:
            queue.append(Reduce(keep, send, order, devices).send())
            for chain in (joint, total):
                chain.after(keep).join()
            grad_mixed = hold(grad_mixed, joint.parts, total.parts, keep)
            for chain in (joint, total):
                chain.send()
    part_sums = jnp.concatenate(part_sums, axis=2)
    vector_sums = jnp.concatenate([part_sums[0, :1], part_sums[2, :1], sums[2:]], axis=0)
    ordered = jnp.take(vector_sums.reshape(devices, piece, entries), source_of(both), axis=0)
    ordered = jnp.pad(ordered.astype(BF), ((0, 0), (0, 0), (0, LANES - entries)))
    keep = jnp.concatenate([keep, ordered[: devices // 2]], axis=2)
    send = jnp.concatenate([send, ordered[devices // 2 :]], axis=2)
    queue.append(Reduce(keep, send, both, devices).send())
    grad_one = hold(grad_one, send)
    filled = ()
    for which in range(batch):
        if which == batch - 1:
            for chain in (queue[1], joint, total, queue[0]):
                chain.after(filled).join()
            grad_one = hold(grad_one, *(chain.parts for chain in (joint, total, *queue)))
            for chain in (queue[1], joint, total, queue[0]):
                chain.send()
        filled = (input_gradient(grad_one, gathered, parts, which, batch, filled),)
    input_grad = filled[0]
    for chain in (joint, total, *queue):
        chain.after(filled)

    total_qkv = [chain.finish() for chain in queue]
    here = spans[1][1] * LANES
    total_vectors = total_qkv[1][:, 3 * here : 3 * here + entries].reshape(-1)
    total_qkv = jnp.concatenate(
        [
            part[:, at * pairs * LANES : (at + 1) * pairs * LANES]
            for at in range(3)
            for part, (_, pairs) in zip(total_qkv, spans)
        ],
        axis=1,
    )
    total_wide = joint.finish()
    total_up, total_attn = total_wide[:, :inner], total_wide[:, inner:]
    total_down = total.finish()

    m_qkv, v_qkv, w_qkv = adamw(proj_qkv, total_qkv, first_qkv, second_qkv, WEIGHT_DECAY, LEARN_RATE)
    m_attn, v_attn, w_attn = adamw(
        proj_attn, total_attn, first_attn, second_attn, WEIGHT_DECAY, LEARN_RATE
    )
    m_up, v_up, w_up = adamw(proj_up, total_up, first_up, second_up, WEIGHT_DECAY, LEARN_RATE)
    m_down, v_down, w_down = adamw(
        proj_down, total_down, first_down, second_down, WEIGHT_DECAY, LEARN_RATE
    )
    m_vec, v_vec, w_vec = adamw(
        vectors, total_vectors, first_vectors, second_vectors, 0.0, LEARN_RATE_VECTOR
    )
    return (
        output,
        input_grad,
        m_qkv,
        v_qkv,
        w_qkv,
        m_attn,
        v_attn,
        w_attn,
        m_up,
        v_up,
        w_up,
        m_down,
        v_down,
        w_down,
        m_vec,
        v_vec,
        w_vec,
    )


def solution(mesh):
    rows, flat = P("dp", None), P("dp")
    return jax.shard_map(
        on_device,
        mesh=mesh,
        in_specs=(rows, flat, rows) + (rows, rows, rows, rows, flat) * 3,
        out_specs=(rows, rows) + (rows,) * 12 + (flat,) * 3,
        check_vma=False,
    )
```

```python
import functools
import math

import jax
import jax.numpy as jnp
from jax import lax
from jax.experimental import pallas as pl
from jax.experimental.pallas import tpu as pltpu
from jax.sharding import PartitionSpec as P

HEAD = 64
STEP = 10

EPSILON_NORM = 1e-05
BETA_ONE = 0.9
BETA_TWO = 0.999
LEARN_RATE = 0.1
LEARN_RATE_VECTOR = 0.4
WEIGHT_DECAY = 0.01
EPSILON_ADAM = 1e-08

LANES = 128
ROWS = 256
VMEM_BYTES = 56 * 1024 * 1024
BF = jnp.bfloat16
F32 = jnp.float32

NN = (((1,), (0,)), ((), ()))
NT = (((1,), (1,)), ((), ()))
TN = (((0,), (0,)), ((), ()))


def dot(left, right, dims=NN):
    return lax.dot_general(left, right, dims, preferred_element_type=F32)


def params(grid_rank):
    return pltpu.CompilerParams(
        dimension_semantics=("arbitrary",) * grid_rank, vmem_limit_bytes=VMEM_BYTES
    )


def cost(flops, moved, exps=0, longer=1):
    return pl.CostEstimate(
        flops=longer * int(flops), bytes_accessed=int(moved), transcendentals=int(exps)
    )


def qkv_kernel(x_ref, w_ref, vec_ref, out_ref):
    width = x_ref.shape[1]
    x = x_ref[...]
    for part in range(3):
        cols = pl.ds(part * width, width)
        value = dot(x, w_ref[:, cols])
        if part == 0:
            value = value + vec_ref[0:1, :]
        if part == 2:
            value = value + vec_ref[1:2, :]
        out_ref[:, cols] = value.astype(BF)


def project_qkv(x, gathered, vec):
    rows, width = x.shape
    return pl.pallas_call(
        qkv_kernel,
        grid=(rows // ROWS,),
        in_specs=[
            pl.BlockSpec((ROWS, width), lambda i: (i, 0)),
            pl.BlockSpec((width, 3 * width), lambda i: (0, 0), pipeline_mode=pl.Buffered(1)),
            pl.BlockSpec(vec.shape, lambda i: (0, 0)),
        ],
        out_specs=pl.BlockSpec((ROWS, 3 * width), lambda i: (i, 0)),
        out_shape=jax.ShapeDtypeStruct((rows, 3 * width), BF),
        compiler_params=params(1),
        cost_estimate=cost(6 * rows * width * width, 2 * (4 * rows * width + 3 * width * width)),
        name="project_qkv",
    )(x, gathered, vec)


def attend_kernel(len_ref, q_ref, k_ref, v_ref, *refs, which):
    out_ref, lse_ref = refs[-2:]
    length = len_ref[which]
    seq = q_ref.shape[0]
    query = q_ref[...] * jnp.asarray(1.0 / math.sqrt(HEAD), BF)
    keyset = k_ref[...]
    val_t = v_ref[...].T
    lane = lax.broadcasted_iota(jnp.int32, (seq, LANES), 1)
    alive = lax.broadcasted_iota(jnp.int32, (seq, seq), 0) < length
    mixed = []
    for head in range(2):
        mine = (lane < HEAD) if head == 0 else (lane >= HEAD)
        scores = dot(keyset, jnp.where(mine, query, jnp.zeros_like(query)), NT)
        scores = jnp.where(alive, scores, -1e30)
        highest = jnp.max(scores, axis=0, keepdims=True)
        expo = jnp.exp(scores - highest)
        summed = jnp.sum(expo, axis=0, keepdims=True)
        probs = (expo * (1.0 / summed)).astype(BF)
        mixed.append(dot(val_t[head * HEAD : (head + 1) * HEAD], probs))
        lse_ref[0, head : head + 1, :] = highest + jnp.log(summed)
    out_ref[...] = jnp.concatenate(mixed, axis=0).T.astype(BF)


def attend_forward(packed, lengths, width, which, filled):
    rows = packed.shape[0]
    batch = lengths.shape[0]
    seq = rows // batch
    pairs = width // LANES
    grid_spec = pltpu.PrefetchScalarGridSpec(
        num_scalar_prefetch=1,
        grid=(pairs,),
        in_specs=[
            pl.BlockSpec((seq, LANES), lambda h, ln: (which, h)),
            pl.BlockSpec((seq, LANES), lambda h, ln: (which, pairs + h)),
            pl.BlockSpec((seq, LANES), lambda h, ln: (which, 2 * pairs + h)),
        ]
        + [pl.BlockSpec(memory_space=pl.ANY)] * len(filled),
        out_specs=[
            pl.BlockSpec((seq, LANES), lambda h, ln: (which, h)),
            pl.BlockSpec((1, 2, seq), lambda h, ln: (which * pairs + h, 0, 0)),
        ],
    )
    return pl.pallas_call(
        functools.partial(attend_kernel, which=which),
        grid_spec=grid_spec,
        out_shape=[
            jax.ShapeDtypeStruct((rows, width), BF),
            jax.ShapeDtypeStruct((batch * pairs, 2, seq), F32),
        ],
        input_output_aliases={4 + index: index for index in range(len(filled))},
        compiler_params=params(1),
        cost_estimate=cost(16 * seq * seq * width, 8 * seq * width, seq * seq * width // HEAD),
        name="attend_forward",
    )(lengths, packed, packed, packed, *filled)


def attend_back_kernel(len_ref, q_ref, k_ref, v_ref, g_ref, lse_ref, *refs, which):
    out_ref = refs[-1]
    length = len_ref[which]
    seq = q_ref.shape[0]
    factor = 1.0 / math.sqrt(HEAD)
    query = q_ref[...] * jnp.asarray(factor, BF)
    keyset = k_ref[...]
    valset = v_ref[...]
    grad = g_ref[...]
    key_t = keyset.T
    lane = lax.broadcasted_iota(jnp.int32, (seq, LANES), 1)
    alive = lax.broadcasted_iota(jnp.int32, (seq, seq), 0) < length
    grad_q = []
    grad_k = 0.0
    grad_v = 0.0
    for head in range(2):
        mine = (lane < HEAD) if head == 0 else (lane >= HEAD)
        query_h = jnp.where(mine, query, jnp.zeros_like(query))
        grad_h = jnp.where(mine, grad, jnp.zeros_like(grad))
        scores = jnp.where(alive, dot(keyset, query_h, NT), -1e30)
        probs = jnp.exp(scores - lse_ref[0, head : head + 1, :])
        grad_probs = dot(valset, grad_h, NT)
        total = jnp.sum(probs * grad_probs, axis=0, keepdims=True)
        grad_scores = (probs * (grad_probs - total)).astype(BF)
        grad_v = grad_v + dot(probs.astype(BF), grad_h)
        grad_k = grad_k + dot(grad_scores, query_h)
        grad_q.append(dot(key_t[head * HEAD : (head + 1) * HEAD], grad_scores))
    out_ref[0] = (jnp.concatenate(grad_q, axis=0).T * factor).astype(BF)
    out_ref[1] = grad_k.astype(BF)
    out_ref[2] = grad_v.astype(BF)


def pair_groups(pairs):
    first = 2 * pairs // 3
    return ((0, first), (first, pairs - first))


def attend_backward(packed, lengths, lse, grad_mixed, span, which, filled):
    rows, width = grad_mixed.shape
    batch = lengths.shape[0]
    seq = rows // batch
    pairs = width // LANES
    base, here = span
    grid_spec = pltpu.PrefetchScalarGridSpec(
        num_scalar_prefetch=1,
        grid=(here,),
        in_specs=[
            pl.BlockSpec((seq, LANES), lambda h, ln: (which, base + h)),
            pl.BlockSpec((seq, LANES), lambda h, ln: (which, pairs + base + h)),
            pl.BlockSpec((seq, LANES), lambda h, ln: (which, 2 * pairs + base + h)),
            pl.BlockSpec((seq, LANES), lambda h, ln: (which, base + h)),
            pl.BlockSpec((1, 2, seq), lambda h, ln: (which * pairs + base + h, 0, 0)),
        ]
        + [pl.BlockSpec(memory_space=pl.ANY)] * len(filled),
        out_specs=pl.BlockSpec((3, seq, LANES), lambda h, ln: (0, which, h)),
    )
    return pl.pallas_call(
        functools.partial(attend_back_kernel, which=which),
        grid_spec=grid_spec,
        out_shape=jax.ShapeDtypeStruct((3, rows, here * LANES), BF),
        input_output_aliases={6 + index: index for index in range(len(filled))},
        compiler_params=params(1),
        cost_estimate=cost(
            40 * seq * seq * here * LANES, 14 * seq * here * LANES, seq * seq * here * 2, 8
        ),
        name="attend_backward",
    )(lengths, packed, packed, packed, grad_mixed, lse, *filled)


def norm_forward(resid, gain, shift):
    centred = resid - jnp.mean(resid, axis=-1, keepdims=True)
    inverse = lax.rsqrt(jnp.mean(centred * centred, axis=-1, keepdims=True) + EPSILON_NORM)
    scaled = centred * inverse
    return (scaled * gain + shift, scaled, inverse)


def norm_backward(grad, scaled, inverse, gain):
    grad_scaled = grad * gain
    return inverse * (
        grad_scaled
        - jnp.mean(grad_scaled, axis=-1, keepdims=True)
        - scaled * jnp.mean(grad_scaled * scaled, axis=-1, keepdims=True)
    )


def column_sum(value):
    return jnp.sum(value, axis=0, keepdims=True)


def middle_kernel(
    len_ref,
    x_ref,
    mixed_ref,
    cot_ref,
    w_attn,
    w_up,
    w_down,
    vec_ref,
    out_ref,
    first_ref,
    active_ref,
    upper_ref,
    branch_ref,
    attn_ref,
    gmix_ref,
    resid_ref,
    sum_ref,
    slope_ref,
    *down_refs,
    seq,
    piece,
):
    step = pl.program_id(0)
    rows, width = x_ref.shape
    chunks = w_up.shape[1] // width
    if down_refs:
        columns_ref, w_down = w_down, down_refs[0]

        @pl.when(step == 0)
        def _():
            def lay(pair, carry):
                begin = pl.multiple_of(pair * 2 * piece, 16)
                strips = [
                    columns_ref[pl.ds(begin, 2 * piece), pl.ds(j * width, width)].astype(F32)
                    for j in range(chunks)
                ]
                both = [strip[:piece] for strip in strips] + [strip[piece:] for strip in strips]
                there = pl.multiple_of(pair * 2 * chunks * piece, 16)
                w_down[pl.ds(there, 2 * chunks * piece), :] = jnp.concatenate(both, axis=0).astype(BF)
                return carry

            lax.fori_loop(0, width // (2 * piece), lay, 0)

    start = (step * rows) % seq
    length = len_ref[(step * rows) // seq]

    def vec(index):
        return vec_ref[index : index + 1, :]

    gain_one, shift_one, gain_two, shift_two = vec(8), vec(9), vec(10), vec(11)

    @pl.when(step == 0)
    def _():
        sum_ref[...] = jnp.zeros_like(sum_ref)

    resid_one = x_ref[...].astype(F32) + dot(mixed_ref[...], w_attn[...]) + vec(2)
    first, scaled_one, inverse_one = norm_forward(resid_one, gain_one, shift_one)
    first_low = first.astype(BF)
    first_ref[...] = first_low
    total = first + vec(7)
    for j in range(chunks):
        cols = pl.ds(j * width, width)
        upper = dot(first_low, w_up[:, cols]) + vec(3 + j)
        half = 0.5 + 0.5 * lax.erf(upper * (1.0 / math.sqrt(2.0)))
        active = (upper * half).astype(BF)
        active_ref[:, cols] = active
        slope_ref[:, cols] = half + upper * jnp.exp(-0.5 * upper * upper) * (
            1.0 / math.sqrt(2.0 * math.pi)
        )
        total = total + dot(active, w_down[cols, :])
    output, scaled_two, inverse_two = norm_forward(total, gain_two, shift_two)
    out_ref[...] = output.astype(BF)

    @pl.when(start < length)
    def _():
        alive = lax.broadcasted_iota(jnp.int32, (rows, 1), 0) + start < length
        grad_out = jnp.where(alive, cot_ref[...].astype(F32), 0.0)
        grad_two = norm_backward(grad_out, scaled_two, inverse_two, gain_two)
        branch = grad_two.astype(BF)
        branch_ref[...] = branch
        grad_first = grad_two
        for j in range(chunks):
            cols = pl.ds(j * width, width)
            grad_upper = (dot(branch, w_down[cols, :], NT) * slope_ref[:, cols]).astype(BF)
            upper_ref[:, cols] = grad_upper
            sum_ref[3 + j : 4 + j, :] += column_sum(grad_upper.astype(F32))
            grad_first = grad_first + dot(grad_upper, w_up[:, cols], NT)
        grad_one = norm_backward(grad_first, scaled_one, inverse_one, gain_one)
        resid_ref[...] = grad_one
        grad_attn = grad_one.astype(BF)
        attn_ref[...] = grad_attn
        gmix_ref[...] = dot(grad_attn, w_attn[...], NT).astype(BF)
        sum_ref[2:3, :] += column_sum(grad_attn.astype(F32))
        sum_ref[7:8, :] += column_sum(branch.astype(F32))
        sum_ref[8:9, :] += column_sum(grad_first * scaled_one)
        sum_ref[9:10, :] += column_sum(grad_first)
        sum_ref[10:11, :] += column_sum(grad_out * scaled_two)
        sum_ref[11:12, :] += column_sum(grad_out)

    @pl.when(start >= length)
    def _():
        upper_ref[...] = jnp.zeros_like(upper_ref)
        branch_ref[...] = jnp.zeros_like(branch_ref)
        attn_ref[...] = jnp.zeros_like(attn_ref)
        gmix_ref[...] = jnp.zeros_like(gmix_ref)
        resid_ref[...] = jnp.zeros_like(resid_ref)


def middle(x, mixed, cotangent, lengths, gathered, vec, piece):
    rows, width = x.shape
    inner = (gathered.shape[1] - width) // 2
    ratio = inner // width
    if piece % 8:
        w_down = gathered[:, inner + width :].reshape(width // piece, piece, ratio, width)
        w_down = w_down.transpose(0, 2, 1, 3).reshape(inner, width)
        down_block = (inner, width), 0
    else:
        w_down = gathered
        down_block = (width, inner), 1
    seq = rows // lengths.shape[0]
    once = pl.Buffered(1)
    thin = pl.BlockSpec((ROWS, width), lambda i, ln: (i, 0))
    wide = pl.BlockSpec((ROWS, inner), lambda i, ln: (i, 0))
    grid_spec = pltpu.PrefetchScalarGridSpec(
        num_scalar_prefetch=1,
        grid=(rows // ROWS,),
        in_specs=[
            thin,
            thin,
            thin,
            pl.BlockSpec((width, width), lambda i, ln: (0, 2 * ratio), pipeline_mode=once),
            pl.BlockSpec((width, inner), lambda i, ln: (0, 0), pipeline_mode=once),
            pl.BlockSpec(down_block[0], lambda i, ln: (0, down_block[1]), pipeline_mode=once),
            pl.BlockSpec(vec.shape, lambda i, ln: (0, 0)),
        ],
        out_specs=[
            thin,
            thin,
            wide,
            wide,
            thin,
            thin,
            thin,
            thin,
            pl.BlockSpec(vec.shape, lambda i, ln: (0, 0)),
        ],
        scratch_shapes=[pltpu.VMEM((ROWS, inner), F32)]
        + ([] if piece % 8 else [pltpu.VMEM((inner, width), BF)]),
    )
    low = jax.ShapeDtypeStruct((rows, width), BF)
    low_wide = jax.ShapeDtypeStruct((rows, inner), BF)
    return pl.pallas_call(
        functools.partial(middle_kernel, seq=seq, piece=piece),
        grid_spec=grid_spec,
        out_shape=[
            low,
            low,
            low_wide,
            low_wide,
            low,
            low,
            low,
            jax.ShapeDtypeStruct((rows, width), F32),
            jax.ShapeDtypeStruct(vec.shape, F32),
        ],
        compiler_params=params(1),
        cost_estimate=cost(
            8 * rows * width * inner + 4 * rows * width * width,
            rows * (4 * inner + 20 * width) + 4 * width * inner,
            2 * rows * inner,
        ),
        name="middle",
    )(lengths, x, mixed, cotangent, gathered, gathered, w_down, vec)


def weight_kernel(src_ref, left_ref, right_ref, *refs, sums):
    keep_ref, send_ref, acc_ref, turned_ref = refs[0], refs[1], refs[-2], refs[-1]
    half, piece, _ = keep_ref.shape
    right = right_ref[0] if len(right_ref.shape) == 3 else right_ref[...]

    @pl.when(pl.program_id(0) == 0)
    def _():
        turned_ref[...] = left_ref[...].T

    acc_ref[...] = dot(turned_ref[...], right)
    if sums:
        refs[2][0] = jnp.broadcast_to(column_sum(right.astype(F32)), refs[2].shape[1:])
    for slot in range(half):
        for ref, offset in ((keep_ref, 0), (send_ref, half)):
            begin = pl.multiple_of(src_ref[offset + slot] * piece, 8)
            ref[slot] = acc_ref[pl.ds(begin, piece), :].astype(BF)


def plain_weight_kernel(left_ref, right_ref, out_ref, *refs):
    right = right_ref[0] if len(right_ref.shape) == 3 else right_ref[...]
    out_ref[...] = dot(left_ref[...], right, TN).astype(BF)
    if refs:
        refs[0][0] = jnp.broadcast_to(column_sum(right.astype(F32)), refs[0].shape[1:])


def weight_gradient(left, right, source, sums=False):
    rows, tall = left.shape
    devices = source.shape[0]
    piece = tall // devices
    if right.ndim == 3:
        steps, _, tile = right.shape
        right_block = pl.BlockSpec((1, rows, tile), lambda j, *s: (j, 0, 0))
    else:
        tile = min(right.shape[1], 768)
        steps = right.shape[1] // tile
        right_block = pl.BlockSpec((rows, tile), lambda j, *s: (0, j))
    left_block = pl.BlockSpec((rows, tall), lambda j, *s: (0, 0))
    extra_specs = [pl.BlockSpec((1, 8, tile), lambda j, *s: (j, 0, 0))] if sums else []
    extra_shapes = [jax.ShapeDtypeStruct((steps, 8, tile), F32)] if sums else []
    estimate = cost(
        2 * rows * tall * tile * steps,
        2 * tall * tile * steps + 2 * rows * (tall + tile * steps),
        longer=64,
    )
    if piece % 8:
        whole, *rest = pl.pallas_call(
            plain_weight_kernel,
            grid=(steps,),
            in_specs=[left_block, right_block],
            out_specs=[pl.BlockSpec((tall, tile), lambda j: (0, j))] + extra_specs,
            out_shape=[jax.ShapeDtypeStruct((tall, steps * tile), BF)] + extra_shapes,
            compiler_params=params(1),
            cost_estimate=estimate,
            name="weight_gradient",
        )(left, right)
        ordered = jnp.take(whole.reshape(devices, piece, steps * tile), source, axis=0)
        return (ordered[: devices // 2], ordered[devices // 2 :], *rest)
    block = pl.BlockSpec((devices // 2, piece, tile), lambda j, s: (0, 0, j))
    shape = jax.ShapeDtypeStruct((devices // 2, piece, steps * tile), BF)
    grid_spec = pltpu.PrefetchScalarGridSpec(
        num_scalar_prefetch=1,
        grid=(steps,),
        in_specs=[left_block, right_block],
        out_specs=[block, block] + extra_specs,
        scratch_shapes=[pltpu.VMEM((tall, tile), F32), pltpu.VMEM((tall, rows), BF)],
    )
    return pl.pallas_call(
        functools.partial(weight_kernel, sums=sums),
        grid_spec=grid_spec,
        out_shape=[shape, shape] + extra_shapes,
        compiler_params=params(1),
        cost_estimate=estimate,
        name="weight_gradient",
    )(source, left, right)


def joint_kernel(
    src_ref,
    left_ref,
    last_left_ref,
    right_ref,
    last_right_ref,
    keep_ref,
    send_ref,
    acc_ref,
    turned_ref,
):
    half, piece, _ = keep_ref.shape
    last = pl.num_programs(0) - 1

    @pl.when(pl.program_id(0) == 0)
    def _():
        turned_ref[...] = left_ref[...].T

    @pl.when(pl.program_id(0) < last)
    def _():
        acc_ref[...] = dot(turned_ref[...], right_ref[...])

    @pl.when(pl.program_id(0) == last)
    def _():
        acc_ref[...] = dot(last_left_ref[...], last_right_ref[...], TN)

    for slot in range(half):
        for ref, offset in ((keep_ref, 0), (send_ref, half)):
            begin = pl.multiple_of(src_ref[offset + slot] * piece, 8)
            ref[slot] = acc_ref[pl.ds(begin, piece), :].astype(BF)


def joint_gradient(left, right, last_left, last_right, source):
    rows, tall = left.shape
    devices = source.shape[0]
    piece = tall // devices
    tile = last_right.shape[1]
    wide = right.shape[1] // tile
    if piece % 8:
        one = weight_gradient(left, right, source)
        two = weight_gradient(last_left, last_right, source)
        return [jnp.concatenate(both, axis=2) for both in zip(one, two)]
    full = pl.BlockSpec((rows, tall), lambda j, s: (0, 0))
    block = pl.BlockSpec((devices // 2, piece, tile), lambda j, s: (0, 0, j))
    shape = jax.ShapeDtypeStruct((devices // 2, piece, (wide + 1) * tile), BF)
    grid_spec = pltpu.PrefetchScalarGridSpec(
        num_scalar_prefetch=1,
        grid=(wide + 1,),
        in_specs=[
            full,
            full,
            pl.BlockSpec((rows, tile), lambda j, s: (0, jnp.minimum(j, wide - 1))),
            pl.BlockSpec((rows, tile), lambda j, s: (0, 0)),
        ],
        out_specs=[block, block],
        scratch_shapes=[pltpu.VMEM((tall, tile), F32), pltpu.VMEM((tall, rows), BF)],
    )
    return pl.pallas_call(
        joint_kernel,
        grid_spec=grid_spec,
        out_shape=[shape, shape],
        compiler_params=params(1),
        cost_estimate=cost(
            2 * rows * tall * tile * (wide + 1),
            2 * (tall + rows) * tile * (wide + 1) + 4 * rows * tall,
            longer=8,
        ),
        name="joint_gradient",
    )(source, left, last_left, right, last_right)


def tall_kernel(slot_ref, left_ref, right_ref, keep_ref, send_ref, acc_ref):
    step = pl.program_id(0)
    half, piece, _ = keep_ref.shape
    here = left_ref.shape[1] // piece
    acc_ref[...] = dot(left_ref[...], right_ref[...], TN)
    for index in range(here):
        slot = slot_ref[step * here + index]
        part = acc_ref[index * piece : (index + 1) * piece, :].astype(BF)

        @pl.when(slot < half)
        def _():
            keep_ref[jnp.minimum(slot, half - 1)] = part

        @pl.when(slot >= half)
        def _():
            send_ref[jnp.maximum(slot - half, 0)] = part


def plain_tall_kernel(left_ref, right_ref, out_ref):
    out_ref[...] = dot(left_ref[...], right_ref[...], TN).astype(BF)


def tall_gradient(left, right, source, slot_of):
    rows, tall = left.shape
    width = right.shape[1]
    devices = source.shape[0]
    piece = tall // devices
    steps = tall // width
    left_block = pl.BlockSpec((rows, width), lambda j, *s: (0, j))
    right_block = pl.BlockSpec((rows, width), lambda j, *s: (0, 0))
    estimate = cost(2 * rows * tall * width, 2 * tall * width + 2 * rows * (tall + width))
    if piece % 16:
        whole = pl.pallas_call(
            plain_tall_kernel,
            grid=(steps,),
            in_specs=[left_block, right_block],
            out_specs=pl.BlockSpec((width, width), lambda j: (j, 0)),
            out_shape=jax.ShapeDtypeStruct((tall, width), BF),
            compiler_params=params(1),
            cost_estimate=estimate,
            name="tall_gradient",
        )(left, right)
        ordered = jnp.take(whole.reshape(devices, piece, width), source, axis=0)
        return (ordered[: devices // 2], ordered[devices // 2 :])
    block = pl.BlockSpec((devices // 2, piece, width), lambda j, s: (0, 0, 0))
    shape = jax.ShapeDtypeStruct((devices // 2, piece, width), BF)
    grid_spec = pltpu.PrefetchScalarGridSpec(
        num_scalar_prefetch=1,
        grid=(steps,),
        in_specs=[left_block, right_block],
        out_specs=[block, block],
        scratch_shapes=[pltpu.VMEM((width, width), F32)],
    )
    return pl.pallas_call(
        tall_kernel,
        grid_spec=grid_spec,
        out_shape=[shape, shape],
        compiler_params=params(1),
        cost_estimate=estimate,
        name="tall_gradient",
    )(slot_of, left, right)


def input_kernel(resid_ref, w_ref, *refs, groups):
    out_ref = refs[-1]
    width = resid_ref.shape[1]
    total = resid_ref[...]
    base = 0
    for grad_ref in refs[:groups]:
        here = grad_ref.shape[2]
        for part in range(3):
            total = total + dot(grad_ref[part], w_ref[:, pl.ds(part * width + base, here)], NT)
        base += here
    out_ref[...] = total.astype(BF)


def input_gradient(resid, gathered, grads, which, batch, filled):
    rows, width = resid.shape
    steps = rows // batch // ROWS
    base = which * steps
    return pl.pallas_call(
        functools.partial(input_kernel, groups=len(grads)),
        grid=(steps,),
        in_specs=[
            pl.BlockSpec((ROWS, width), lambda i: (base + i, 0)),
            pl.BlockSpec((width, 3 * width), lambda i: (0, 0), pipeline_mode=pl.Buffered(1)),
        ]
        + [pl.BlockSpec((3, ROWS, grad.shape[2]), lambda i: (0, base + i, 0)) for grad in grads]
        + [pl.BlockSpec(memory_space=pl.ANY)] * len(filled),
        out_specs=pl.BlockSpec((ROWS, width), lambda i: (base + i, 0)),
        out_shape=jax.ShapeDtypeStruct((rows, width), BF),
        input_output_aliases={2 + len(grads): 0} if filled else {},
        compiler_params=params(1),
        cost_estimate=cost(
            6 * rows * width * width // batch,
            (12 * rows * width + 6 * width * width) // batch,
            longer=64,
        ),
        name="input_gradient",
    )(resid, gathered, *grads, *filled)


def swap(value, mask, devices):
    return lax.ppermute(value, "dp", [(index, index ^ mask) for index in range(devices)])


def hold(value, *others):
    return lax.optimization_barrier((value, others))[0]


def masks_of(bits):
    found = [0]
    for bit in bits:
        found = found + [mask | (1 << bit) for mask in found]
    return found


def relative_order(order):
    relative = [0]
    for bits in order:
        relative = [base | mask for base in relative for mask in masks_of(bits)]
    return relative


def stage_orders(devices):
    bits = devices.bit_length() - 1
    rest = [(bit,) for bit in range(3, bits)]
    low = [(bit,) for bit in range(min(3, bits))]
    by_x = low + rest
    by_y = low[:1] + low[1:][::-1] + rest
    middle_bits = [tuple(range(1, min(3, bits)))] if bits > 1 else []
    outward = (low[:1] + middle_bits + rest)[::-1]
    high = range(3, bits)
    pairs = [tuple(high[at : at + 2]) for at in range(0, len(high), 2)]
    return by_x, by_y, low[:1] + middle_bits + pairs, outward


class Reduce:
    def __init__(self, keep, send, order, devices):
        self.order, self.devices, self.at = order, devices, 0
        self.parts = [keep, send]
        self.terms = None

    def send(self):
        masks = masks_of(self.order[self.at])
        self.terms = [self.parts[0]] + [
            swap(part, mask, self.devices) for part, mask in zip(self.parts[1:], masks[1:])
        ]
        self.at += 1
        return self

    def total(self, begin, size):
        result = self.terms[0][begin : begin + size].astype(F32)
        for term in self.terms[1:]:
            result = result + term[begin : begin + size].astype(F32)
        return result

    def join(self):
        ways = len(masks_of(self.order[self.at]))
        size = self.terms[0].shape[0] // ways
        self.parts = [self.total(way * size, size).astype(BF) for way in range(ways)]
        return self

    def after(self, *values):
        self.terms = list(lax.optimization_barrier((tuple(self.terms), values))[0])
        return self

    def finish(self):
        if self.terms is None:
            self.send()
        while self.at < len(self.order):
            self.join().send()
        return self.total(0, 1)[0]


class Gather:
    def __init__(self, shard, order, devices):
        self.order, self.devices, self.at = order, devices, 0
        self.held = shard[None]
        self.taken = None

    def send(self):
        masks = masks_of(self.order[self.at])
        self.taken = [swap(self.held, mask, self.devices) for mask in masks[1:]]
        self.at += 1
        return self

    def join(self):
        self.held = jnp.concatenate([self.held] + self.taken, axis=0)
        return self


def lay_pairs_kernel(index_ref, odd_ref, held_ref, taken_ref, out_ref):
    half, piece, _ = held_ref.shape
    odd = odd_ref[0] == 1
    for slot in range(half):
        mine = held_ref[slot].astype(F32)
        other = taken_ref[slot].astype(F32)
        both = jnp.concatenate(
            [jnp.where(odd, other, mine), jnp.where(odd, mine, other)], axis=0
        ).astype(BF)
        begin = pl.multiple_of((index_ref[slot] // 2) * (2 * piece), 16)
        out_ref[pl.ds(begin, 2 * piece), :] = both


def lay_out(gather, me):
    held, taken = gather.held, gather.taken[0]
    half, piece, columns = held.shape
    devices = 2 * half
    relative = [0]
    for bits in gather.order[:-1]:
        relative = [base | mask for mask in masks_of(bits) for base in relative]
    index = jnp.asarray(relative, jnp.int32) ^ me
    if piece % 8:
        where = [0] * devices
        for slot, value in enumerate(relative):
            where[value], where[value ^ 1] = slot, half + slot
        natural = jnp.take(jnp.asarray(where, jnp.int32), jnp.arange(devices, dtype=jnp.int32) ^ me)
        both = jnp.concatenate([held, taken], axis=0)
        return jnp.take(both, natural, axis=0).reshape(devices * piece, columns)
    tile = columns // 5 if columns % (5 * LANES) == 0 else columns
    block = pl.BlockSpec((half, piece, tile), lambda i, *s: (0, 0, i))
    grid_spec = pltpu.PrefetchScalarGridSpec(
        num_scalar_prefetch=2,
        grid=(columns // tile,),
        in_specs=[block, block],
        out_specs=pl.BlockSpec((devices * piece, tile), lambda i, *s: (0, i)),
    )
    return pl.pallas_call(
        lay_pairs_kernel,
        grid_spec=grid_spec,
        out_shape=jax.ShapeDtypeStruct((devices * piece, columns), BF),
        compiler_params=params(1),
        cost_estimate=cost(devices * piece * columns, 4 * devices * piece * columns),
        name="lay_out",
    )(index, (me & 1).reshape(1), held, taken)


def adamw(weight, grad, first, second, decay, rate):
    new_first = BETA_ONE * first + (1.0 - BETA_ONE) * grad
    new_second = BETA_TWO * second + (1.0 - BETA_TWO) * grad * grad
    corrected = new_first / (1.0 - BETA_ONE**STEP)
    scale_sq = new_second / (1.0 - BETA_TWO**STEP)
    new_weight = weight - rate * (corrected / (jnp.sqrt(scale_sq) + EPSILON_ADAM) + decay * weight)
    return (new_first, new_second, new_weight)


def on_device(
    hidden_in,
    lengths,
    cotangent,
    proj_qkv,
    proj_attn,
    proj_up,
    proj_down,
    vectors,
    first_qkv,
    first_attn,
    first_up,
    first_down,
    first_vectors,
    second_qkv,
    second_attn,
    second_up,
    second_down,
    second_vectors,
):
    devices = lax.axis_size("dp")
    me = lax.axis_index("dp")
    width = hidden_in.shape[1]
    piece = proj_qkv.shape[0]
    inner = proj_up.shape[1]
    batch = lengths.shape[0]
    by_x, by_y, both, outward = stage_orders(devices)

    def source_of(order):
        return jnp.asarray(relative_order(order), jnp.int32) ^ me

    slots = [0] * devices
    for slot, value in enumerate(relative_order(by_x)):
        slots[value] = slot
    slot_of = jnp.take(jnp.asarray(slots, jnp.int32), jnp.arange(devices, dtype=jnp.int32) ^ me)

    entries = vectors.shape[0] // piece
    ratio = inner // width
    down_columns = proj_down.astype(BF).reshape(ratio, piece, width).transpose(1, 0, 2)
    wide = lax.all_gather(
        jnp.concatenate(
            [proj_up.astype(BF), down_columns.reshape(piece, inner), proj_attn.astype(BF)], axis=1
        ),
        "dp",
        axis=0,
        tiled=True,
    )
    shard = jnp.concatenate(
        [
            proj_qkv.astype(BF),
            jnp.pad(vectors.astype(BF).reshape(piece, entries), ((0, 0), (0, 2 * LANES - entries))),
        ],
        axis=1,
    )
    qkv = Gather(shard, outward, devices)
    for _ in range(len(outward) - 1):
        qkv.send().join()
    qkv.send()
    gathered = lay_out(qkv, me)
    vec = gathered[:, 3 * width : 3 * width + entries].astype(F32).reshape(-1, width)

    packed = project_qkv(hidden_in, gathered, vec)
    filled = ()
    for which in range(batch):
        filled = attend_forward(packed, lengths, width, which, filled)
    mixed, lse = filled
    output, first_low, active, grad_upper, grad_branch, grad_attn, grad_mixed, grad_one, sums = middle(
        hidden_in, mixed, cotangent, lengths, wide, vec, piece
    )

    joint = Reduce(
        *joint_gradient(first_low, grad_upper, mixed, grad_attn, source_of(by_y)), by_y, devices
    )
    joint.send()
    active = hold(active, joint.parts)
    total = Reduce(*tall_gradient(active, grad_branch, source_of(by_x), slot_of), by_x, devices)
    joint.after(total.parts).join()
    grad_mixed = hold(grad_mixed, total.parts, joint.parts)
    joint.send()
    total.send()
    parts, part_sums, queue = [], [], []
    spans = pair_groups(width // LANES)
    for group, span in enumerate(spans):
        final = group == len(spans) - 1
        part = ()
        for which in range(batch):
            part = (attend_backward(packed, lengths, lse, grad_mixed, span, which, part),)
            if which == 0:
                chain = queue[0] if final else total
                chain.after(part).join()
                grad_mixed = hold(grad_mixed, chain.parts)
                chain.send()
        left = hidden_in
        if final:
            for chain in (joint, total):
                chain.after(part).join()
            left = hold(hidden_in, joint.parts, total.parts)
            for chain in (joint, total):
                chain.send()
        order = both if final else by_x
        keep, send, part_sum = weight_gradient(left, part[0], source_of(order), sums=True)
        parts.append(part[0])
        part_sums.append(part_sum)
        if group == 0:
            queue.append(Reduce(keep, send, order, devices).send())
            for chain in (joint, total):
                chain.after(keep).join()
            grad_mixed = hold(grad_mixed, joint.parts, total.parts, keep)
            for chain in (joint, total):
                chain.send()
    part_sums = jnp.concatenate(part_sums, axis=2)
    vector_sums = jnp.concatenate([part_sums[0, :1], part_sums[2, :1], sums[2:]], axis=0)
    ordered = jnp.take(vector_sums.reshape(devices, piece, entries), source_of(both), axis=0)
    ordered = jnp.pad(ordered.astype(BF), ((0, 0), (0, 0), (0, LANES - entries)))
    keep = jnp.concatenate([keep, ordered[: devices // 2]], axis=2)
    send = jnp.concatenate([send, ordered[devices // 2 :]], axis=2)
    queue.append(Reduce(keep, send, both, devices).send())
    for chain in (joint, total, queue[0]):
        chain.after(keep).join()
    grad_one = hold(grad_one, send, *(chain.parts for chain in (joint, total, queue[0])))
    for chain in (queue[0], joint, total):
        chain.send()
    filled = ()
    for which in range(batch):
        if which == batch - 1:
            for chain in queue[::-1]:
                chain.after(filled).join()
            grad_one = hold(
                grad_one, *(chain.parts for chain in queue), joint.terms, total.terms
            )
            for chain in queue[::-1]:
                chain.send()
        filled = (input_gradient(grad_one, gathered, parts, which, batch, filled),)
    input_grad = filled[0]
    for chain in (joint, total, *queue):
        chain.after(filled)

    total_qkv = [chain.finish() for chain in queue]
    here = spans[1][1] * LANES
    total_vectors = total_qkv[1][:, 3 * here : 3 * here + entries].reshape(-1)
    total_qkv = jnp.concatenate(
        [
            part[:, at * pairs * LANES : (at + 1) * pairs * LANES]
            for at in range(3)
            for part, (_, pairs) in zip(total_qkv, spans)
        ],
        axis=1,
    )
    total_wide = joint.finish()
    total_up, total_attn = total_wide[:, :inner], total_wide[:, inner:]
    total_down = total.finish()

    m_qkv, v_qkv, w_qkv = adamw(proj_qkv, total_qkv, first_qkv, second_qkv, WEIGHT_DECAY, LEARN_RATE)
    m_attn, v_attn, w_attn = adamw(
        proj_attn, total_attn, first_attn, second_attn, WEIGHT_DECAY, LEARN_RATE
    )
    m_up, v_up, w_up = adamw(proj_up, total_up, first_up, second_up, WEIGHT_DECAY, LEARN_RATE)
    m_down, v_down, w_down = adamw(
        proj_down, total_down, first_down, second_down, WEIGHT_DECAY, LEARN_RATE
    )
    m_vec, v_vec, w_vec = adamw(
        vectors, total_vectors, first_vectors, second_vectors, 0.0, LEARN_RATE_VECTOR
    )
    return (
        output,
        input_grad,
        m_qkv,
        v_qkv,
        w_qkv,
        m_attn,
        v_attn,
        w_attn,
        m_up,
        v_up,
        w_up,
        m_down,
        v_down,
        w_down,
        m_vec,
        v_vec,
        w_vec,
    )


def solution(mesh):
    rows, flat = P("dp", None), P("dp")
    return jax.shard_map(
        on_device,
        mesh=mesh,
        in_specs=(rows, flat, rows) + (rows, rows, rows, rows, flat) * 3,
        out_specs=(rows, rows) + (rows,) * 12 + (flat,) * 3,
        check_vma=False,
    )
```

```python
import functools
import math

import jax
import jax.numpy as jnp
from jax import lax
from jax.experimental import pallas as pl
from jax.experimental.pallas import tpu as pltpu
from jax.sharding import PartitionSpec as P

HEAD = 64
STEP = 10

EPSILON_NORM = 1e-05
BETA_ONE = 0.9
BETA_TWO = 0.999
LEARN_RATE = 0.1
LEARN_RATE_VECTOR = 0.4
WEIGHT_DECAY = 0.01
EPSILON_ADAM = 1e-08

LANES = 128
ROWS = 256
VMEM_BYTES = 56 * 1024 * 1024
BF = jnp.bfloat16
F32 = jnp.float32

NN = (((1,), (0,)), ((), ()))
NT = (((1,), (1,)), ((), ()))
TN = (((0,), (0,)), ((), ()))


def dot(left, right, dims=NN):
    return lax.dot_general(left, right, dims, preferred_element_type=F32)


def params(grid_rank):
    return pltpu.CompilerParams(
        dimension_semantics=("arbitrary",) * grid_rank, vmem_limit_bytes=VMEM_BYTES
    )


def cost(flops, moved, exps=0, longer=1):
    return pl.CostEstimate(
        flops=longer * int(flops), bytes_accessed=int(moved), transcendentals=int(exps)
    )


def qkv_kernel(x_ref, w_ref, vec_ref, out_ref):
    width = x_ref.shape[1]
    x = x_ref[...]
    for part in range(3):
        cols = pl.ds(part * width, width)
        value = dot(x, w_ref[:, cols])
        if part == 0:
            value = value + vec_ref[0:1, :]
        if part == 2:
            value = value + vec_ref[1:2, :]
        out_ref[:, cols] = value.astype(BF)


def project_qkv(x, gathered, vec):
    rows, width = x.shape
    return pl.pallas_call(
        qkv_kernel,
        grid=(rows // ROWS,),
        in_specs=[
            pl.BlockSpec((ROWS, width), lambda i: (i, 0)),
            pl.BlockSpec((width, 3 * width), lambda i: (0, 0), pipeline_mode=pl.Buffered(1)),
            pl.BlockSpec(vec.shape, lambda i: (0, 0)),
        ],
        out_specs=pl.BlockSpec((ROWS, 3 * width), lambda i: (i, 0)),
        out_shape=jax.ShapeDtypeStruct((rows, 3 * width), BF),
        compiler_params=params(1),
        cost_estimate=cost(6 * rows * width * width, 2 * (4 * rows * width + 3 * width * width)),
        name="project_qkv",
    )(x, gathered, vec)


def masked_scores(query, keyset, length, head):
    lane = lax.broadcasted_iota(jnp.int32, query.shape, 1)
    alive = lax.broadcasted_iota(jnp.int32, query.shape, 0) < length
    mine = (lane < HEAD) if head == 0 else (lane >= HEAD)
    spare = lane == (HEAD if head == 0 else 0)
    zeros = jnp.zeros(query.shape, F32)
    adding = jnp.where(alive, zeros, -1e30)
    key_side = jnp.where(mine, keyset.astype(F32), jnp.where(spare, adding, zeros)).astype(BF)
    query_side = jnp.where(mine, query.astype(F32), jnp.where(spare, 1.0, 0.0)).astype(BF)
    return dot(key_side, query_side, NT)


def attend_kernel(len_ref, q_ref, k_ref, v_ref, *refs, which):
    out_ref, lse_ref = refs[-2:]
    length = len_ref[which]
    seq = q_ref.shape[0]
    query = q_ref[...] * jnp.asarray(1.0 / math.sqrt(HEAD), BF)
    keyset = k_ref[...]
    val_t = v_ref[...].T
    mixed = []
    for head in range(2):
        scores = masked_scores(query, keyset, length, head)
        highest = jnp.max(scores, axis=0, keepdims=True)
        expo = jnp.exp(scores - highest)
        summed = jnp.sum(expo, axis=0, keepdims=True)
        probs = (expo * (1.0 / summed)).astype(BF)
        mixed.append(dot(val_t[head * HEAD : (head + 1) * HEAD], probs))
        lse_ref[0, head : head + 1, :] = highest + jnp.log(summed)
    out_ref[...] = jnp.concatenate(mixed, axis=0).T.astype(BF)


def attend_forward(packed, lengths, width, which, filled):
    rows = packed.shape[0]
    batch = lengths.shape[0]
    seq = rows // batch
    pairs = width // LANES
    grid_spec = pltpu.PrefetchScalarGridSpec(
        num_scalar_prefetch=1,
        grid=(pairs,),
        in_specs=[
            pl.BlockSpec((seq, LANES), lambda h, ln: (which, h)),
            pl.BlockSpec((seq, LANES), lambda h, ln: (which, pairs + h)),
            pl.BlockSpec((seq, LANES), lambda h, ln: (which, 2 * pairs + h)),
        ]
        + [pl.BlockSpec(memory_space=pl.ANY)] * len(filled),
        out_specs=[
            pl.BlockSpec((seq, LANES), lambda h, ln: (which, h)),
            pl.BlockSpec((1, 2, seq), lambda h, ln: (which * pairs + h, 0, 0)),
        ],
    )
    return pl.pallas_call(
        functools.partial(attend_kernel, which=which),
        grid_spec=grid_spec,
        out_shape=[
            jax.ShapeDtypeStruct((rows, width), BF),
            jax.ShapeDtypeStruct((batch * pairs, 2, seq), F32),
        ],
        input_output_aliases={4 + index: index for index in range(len(filled))},
        compiler_params=params(1),
        cost_estimate=cost(16 * seq * seq * width, 8 * seq * width, seq * seq * width // HEAD),
        name="attend_forward",
    )(lengths, packed, packed, packed, *filled)


def attend_back_kernel(len_ref, q_ref, k_ref, v_ref, g_ref, lse_ref, *refs, which):
    out_ref = refs[-1]
    length = len_ref[which]
    seq = q_ref.shape[0]
    factor = 1.0 / math.sqrt(HEAD)
    query = q_ref[...] * jnp.asarray(factor, BF)
    keyset = k_ref[...]
    valset = v_ref[...]
    grad = g_ref[...]
    key_t = keyset.T
    lane = lax.broadcasted_iota(jnp.int32, (seq, LANES), 1)
    grad_q = []
    grad_k = 0.0
    grad_v = 0.0
    for head in range(2):
        mine = (lane < HEAD) if head == 0 else (lane >= HEAD)
        query_h = jnp.where(mine, query, jnp.zeros_like(query))
        grad_h = jnp.where(mine, grad, jnp.zeros_like(grad))
        scores = masked_scores(query, keyset, length, head)
        probs = jnp.exp(scores - lse_ref[0, head : head + 1, :])
        grad_probs = dot(valset, grad_h, NT)
        total = jnp.sum(probs * grad_probs, axis=0, keepdims=True)
        grad_scores = (probs * (grad_probs - total)).astype(BF)
        grad_v = grad_v + dot(probs.astype(BF), grad_h)
        grad_k = grad_k + dot(grad_scores, query_h)
        grad_q.append(dot(key_t[head * HEAD : (head + 1) * HEAD], grad_scores))
    out_ref[0] = (jnp.concatenate(grad_q, axis=0).T * factor).astype(BF)
    out_ref[1] = grad_k.astype(BF)
    out_ref[2] = grad_v.astype(BF)


def attend_backward(packed, lengths, lse, grad_mixed, which, filled):
    rows, width = grad_mixed.shape
    batch = lengths.shape[0]
    seq = rows // batch
    pairs = width // LANES
    base, here = 0, pairs
    grid_spec = pltpu.PrefetchScalarGridSpec(
        num_scalar_prefetch=1,
        grid=(here,),
        in_specs=[
            pl.BlockSpec((seq, LANES), lambda h, ln: (which, base + h)),
            pl.BlockSpec((seq, LANES), lambda h, ln: (which, pairs + base + h)),
            pl.BlockSpec((seq, LANES), lambda h, ln: (which, 2 * pairs + base + h)),
            pl.BlockSpec((seq, LANES), lambda h, ln: (which, base + h)),
            pl.BlockSpec((1, 2, seq), lambda h, ln: (which * pairs + base + h, 0, 0)),
        ]
        + [pl.BlockSpec(memory_space=pl.ANY)] * len(filled),
        out_specs=pl.BlockSpec((3, seq, LANES), lambda h, ln: (0, which, h)),
    )
    return pl.pallas_call(
        functools.partial(attend_back_kernel, which=which),
        grid_spec=grid_spec,
        out_shape=jax.ShapeDtypeStruct((3, rows, here * LANES), BF),
        input_output_aliases={6 + index: index for index in range(len(filled))},
        compiler_params=params(1),
        cost_estimate=cost(
            40 * seq * seq * here * LANES, 14 * seq * here * LANES, seq * seq * here * 2, 8
        ),
        name="attend_backward",
    )(lengths, packed, packed, packed, grad_mixed, lse, *filled)


def norm_forward(resid, gain, shift):
    centred = resid - jnp.mean(resid, axis=-1, keepdims=True)
    inverse = lax.rsqrt(jnp.mean(centred * centred, axis=-1, keepdims=True) + EPSILON_NORM)
    scaled = centred * inverse
    return (scaled * gain + shift, scaled, inverse)


def norm_backward(grad, scaled, inverse, gain):
    grad_scaled = grad * gain
    return inverse * (
        grad_scaled
        - jnp.mean(grad_scaled, axis=-1, keepdims=True)
        - scaled * jnp.mean(grad_scaled * scaled, axis=-1, keepdims=True)
    )


def column_sum(value):
    return jnp.sum(value, axis=0, keepdims=True)


def middle_kernel(
    len_ref,
    x_ref,
    mixed_ref,
    cot_ref,
    w_attn,
    w_up,
    w_down,
    vec_ref,
    out_ref,
    first_ref,
    active_ref,
    upper_ref,
    branch_ref,
    attn_ref,
    gmix_ref,
    resid_ref,
    sum_ref,
    slope_ref,
    *down_refs,
    seq,
    piece,
):
    step = pl.program_id(0)
    rows, width = x_ref.shape
    chunks = w_up.shape[1] // width
    if down_refs:
        columns_ref, w_down = w_down, down_refs[0]

        @pl.when(step == 0)
        def _():
            def lay(pair, carry):
                begin = pl.multiple_of(pair * 2 * piece, 16)
                strips = [
                    columns_ref[pl.ds(begin, 2 * piece), pl.ds(j * width, width)].astype(F32)
                    for j in range(chunks)
                ]
                both = [strip[:piece] for strip in strips] + [strip[piece:] for strip in strips]
                there = pl.multiple_of(pair * 2 * chunks * piece, 16)
                w_down[pl.ds(there, 2 * chunks * piece), :] = jnp.concatenate(both, axis=0).astype(BF)
                return carry

            lax.fori_loop(0, width // (2 * piece), lay, 0)

    start = (step * rows) % seq
    length = len_ref[(step * rows) // seq]

    def vec(index):
        return vec_ref[index : index + 1, :]

    gain_one, shift_one, gain_two, shift_two = vec(8), vec(9), vec(10), vec(11)

    @pl.when(step == 0)
    def _():
        sum_ref[...] = jnp.zeros_like(sum_ref)

    resid_one = x_ref[...].astype(F32) + dot(mixed_ref[...], w_attn[...]) + vec(2)
    first, scaled_one, inverse_one = norm_forward(resid_one, gain_one, shift_one)
    first_low = first.astype(BF)
    first_ref[...] = first_low
    total = first + vec(7)
    for j in range(chunks):
        cols = pl.ds(j * width, width)
        upper = dot(first_low, w_up[:, cols]) + vec(3 + j)
        half = 0.5 + 0.5 * lax.erf(upper * (1.0 / math.sqrt(2.0)))
        active = (upper * half).astype(BF)
        active_ref[:, cols] = active
        slope_ref[:, cols] = half + upper * jnp.exp(-0.5 * upper * upper) * (
            1.0 / math.sqrt(2.0 * math.pi)
        )
        total = total + dot(active, w_down[cols, :])
    output, scaled_two, inverse_two = norm_forward(total, gain_two, shift_two)
    out_ref[...] = output.astype(BF)

    @pl.when(start < length)
    def _():
        alive = lax.broadcasted_iota(jnp.int32, (rows, 1), 0) + start < length
        grad_out = jnp.where(alive, cot_ref[...].astype(F32), 0.0)
        grad_two = norm_backward(grad_out, scaled_two, inverse_two, gain_two)
        branch = grad_two.astype(BF)
        branch_ref[...] = branch
        grad_first = grad_two
        for j in range(chunks):
            cols = pl.ds(j * width, width)
            grad_upper = (dot(branch, w_down[cols, :], NT) * slope_ref[:, cols]).astype(BF)
            upper_ref[:, cols] = grad_upper
            sum_ref[3 + j : 4 + j, :] += column_sum(grad_upper.astype(F32))
            grad_first = grad_first + dot(grad_upper, w_up[:, cols], NT)
        grad_one = norm_backward(grad_first, scaled_one, inverse_one, gain_one)
        resid_ref[...] = grad_one
        grad_attn = grad_one.astype(BF)
        attn_ref[...] = grad_attn
        gmix_ref[...] = dot(grad_attn, w_attn[...], NT).astype(BF)
        sum_ref[2:3, :] += column_sum(grad_attn.astype(F32))
        sum_ref[7:8, :] += column_sum(branch.astype(F32))
        sum_ref[8:9, :] += column_sum(grad_first * scaled_one)
        sum_ref[9:10, :] += column_sum(grad_first)
        sum_ref[10:11, :] += column_sum(grad_out * scaled_two)
        sum_ref[11:12, :] += column_sum(grad_out)

    @pl.when(start >= length)
    def _():
        upper_ref[...] = jnp.zeros_like(upper_ref)
        branch_ref[...] = jnp.zeros_like(branch_ref)
        attn_ref[...] = jnp.zeros_like(attn_ref)
        gmix_ref[...] = jnp.zeros_like(gmix_ref)
        resid_ref[...] = jnp.zeros_like(resid_ref)


def middle(x, mixed, cotangent, lengths, gathered, vec, piece):
    rows, width = x.shape
    inner = (gathered.shape[1] - width) // 2
    ratio = inner // width
    if piece % 8:
        w_down = gathered[:, inner + width :].reshape(width // piece, piece, ratio, width)
        w_down = w_down.transpose(0, 2, 1, 3).reshape(inner, width)
        down_block = (inner, width), 0
    else:
        w_down = gathered
        down_block = (width, inner), 1
    seq = rows // lengths.shape[0]
    once = pl.Buffered(1)
    thin = pl.BlockSpec((ROWS, width), lambda i, ln: (i, 0))
    wide = pl.BlockSpec((ROWS, inner), lambda i, ln: (i, 0))
    grid_spec = pltpu.PrefetchScalarGridSpec(
        num_scalar_prefetch=1,
        grid=(rows // ROWS,),
        in_specs=[
            thin,
            thin,
            thin,
            pl.BlockSpec((width, width), lambda i, ln: (0, 2 * ratio), pipeline_mode=once),
            pl.BlockSpec((width, inner), lambda i, ln: (0, 0), pipeline_mode=once),
            pl.BlockSpec(down_block[0], lambda i, ln: (0, down_block[1]), pipeline_mode=once),
            pl.BlockSpec(vec.shape, lambda i, ln: (0, 0)),
        ],
        out_specs=[
            thin,
            thin,
            wide,
            wide,
            thin,
            thin,
            thin,
            thin,
            pl.BlockSpec(vec.shape, lambda i, ln: (0, 0)),
        ],
        scratch_shapes=[pltpu.VMEM((ROWS, inner), F32)]
        + ([] if piece % 8 else [pltpu.VMEM((inner, width), BF)]),
    )
    low = jax.ShapeDtypeStruct((rows, width), BF)
    low_wide = jax.ShapeDtypeStruct((rows, inner), BF)
    return pl.pallas_call(
        functools.partial(middle_kernel, seq=seq, piece=piece),
        grid_spec=grid_spec,
        out_shape=[
            low,
            low,
            low_wide,
            low_wide,
            low,
            low,
            low,
            jax.ShapeDtypeStruct((rows, width), F32),
            jax.ShapeDtypeStruct(vec.shape, F32),
        ],
        compiler_params=params(1),
        cost_estimate=cost(
            8 * rows * width * inner + 4 * rows * width * width,
            rows * (4 * inner + 20 * width) + 4 * width * inner,
            2 * rows * inner,
        ),
        name="middle",
    )(lengths, x, mixed, cotangent, gathered, gathered, w_down, vec)


def weight_kernel(src_ref, left_ref, right_ref, *refs, sums):
    keep_ref, send_ref, acc_ref, turned_ref = refs[0], refs[1], refs[-2], refs[-1]
    half, piece, _ = keep_ref.shape
    right = right_ref[0] if len(right_ref.shape) == 3 else right_ref[...]

    @pl.when(pl.program_id(0) == 0)
    def _():
        turned_ref[...] = left_ref[...].T

    acc_ref[...] = dot(turned_ref[...], right)
    if sums:
        refs[2][0] = jnp.broadcast_to(column_sum(right.astype(F32)), refs[2].shape[1:])
    for slot in range(half):
        for ref, offset in ((keep_ref, 0), (send_ref, half)):
            begin = pl.multiple_of(src_ref[offset + slot] * piece, 8)
            ref[slot] = acc_ref[pl.ds(begin, piece), :].astype(BF)


def plain_weight_kernel(left_ref, right_ref, out_ref, *refs):
    right = right_ref[0] if len(right_ref.shape) == 3 else right_ref[...]
    out_ref[...] = dot(left_ref[...], right, TN).astype(BF)
    if refs:
        refs[0][0] = jnp.broadcast_to(column_sum(right.astype(F32)), refs[0].shape[1:])


def weight_gradient(left, right, source, sums=False):
    rows, tall = left.shape
    devices = source.shape[0]
    piece = tall // devices
    if right.ndim == 3:
        steps, _, tile = right.shape
        right_block = pl.BlockSpec((1, rows, tile), lambda j, *s: (j, 0, 0))
    else:
        tile = min(right.shape[1], 768)
        steps = right.shape[1] // tile
        right_block = pl.BlockSpec((rows, tile), lambda j, *s: (0, j))
    left_block = pl.BlockSpec((rows, tall), lambda j, *s: (0, 0))
    extra_specs = [pl.BlockSpec((1, 8, tile), lambda j, *s: (j, 0, 0))] if sums else []
    extra_shapes = [jax.ShapeDtypeStruct((steps, 8, tile), F32)] if sums else []
    estimate = cost(
        2 * rows * tall * tile * steps,
        2 * tall * tile * steps + 2 * rows * (tall + tile * steps),
        longer=64,
    )
    if piece % 8:
        whole, *rest = pl.pallas_call(
            plain_weight_kernel,
            grid=(steps,),
            in_specs=[left_block, right_block],
            out_specs=[pl.BlockSpec((tall, tile), lambda j: (0, j))] + extra_specs,
            out_shape=[jax.ShapeDtypeStruct((tall, steps * tile), BF)] + extra_shapes,
            compiler_params=params(1),
            cost_estimate=estimate,
            name="weight_gradient",
        )(left, right)
        ordered = jnp.take(whole.reshape(devices, piece, steps * tile), source, axis=0)
        return (ordered[: devices // 2], ordered[devices // 2 :], *rest)
    block = pl.BlockSpec((devices // 2, piece, tile), lambda j, s: (0, 0, j))
    shape = jax.ShapeDtypeStruct((devices // 2, piece, steps * tile), BF)
    grid_spec = pltpu.PrefetchScalarGridSpec(
        num_scalar_prefetch=1,
        grid=(steps,),
        in_specs=[left_block, right_block],
        out_specs=[block, block] + extra_specs,
        scratch_shapes=[pltpu.VMEM((tall, tile), F32), pltpu.VMEM((tall, rows), BF)],
    )
    return pl.pallas_call(
        functools.partial(weight_kernel, sums=sums),
        grid_spec=grid_spec,
        out_shape=[shape, shape] + extra_shapes,
        compiler_params=params(1),
        cost_estimate=estimate,
        name="weight_gradient",
    )(source, left, right)


def joint_kernel(
    src_ref,
    left_ref,
    last_left_ref,
    right_ref,
    last_right_ref,
    keep_ref,
    send_ref,
    acc_ref,
    turned_ref,
):
    half, piece, _ = keep_ref.shape
    last = pl.num_programs(0) - 1

    @pl.when(pl.program_id(0) == 0)
    def _():
        turned_ref[...] = left_ref[...].T

    @pl.when(pl.program_id(0) < last)
    def _():
        acc_ref[...] = dot(turned_ref[...], right_ref[...])

    @pl.when(pl.program_id(0) == last)
    def _():
        acc_ref[...] = dot(last_left_ref[...], last_right_ref[...], TN)

    for slot in range(half):
        for ref, offset in ((keep_ref, 0), (send_ref, half)):
            begin = pl.multiple_of(src_ref[offset + slot] * piece, 8)
            ref[slot] = acc_ref[pl.ds(begin, piece), :].astype(BF)


def joint_gradient(left, right, last_left, last_right, source):
    rows, tall = left.shape
    devices = source.shape[0]
    piece = tall // devices
    tile = last_right.shape[1]
    wide = right.shape[1] // tile
    if piece % 8:
        one = weight_gradient(left, right, source)
        two = weight_gradient(last_left, last_right, source)
        return [jnp.concatenate(both, axis=2) for both in zip(one, two)]
    full = pl.BlockSpec((rows, tall), lambda j, s: (0, 0))
    block = pl.BlockSpec((devices // 2, piece, tile), lambda j, s: (0, 0, j))
    shape = jax.ShapeDtypeStruct((devices // 2, piece, (wide + 1) * tile), BF)
    grid_spec = pltpu.PrefetchScalarGridSpec(
        num_scalar_prefetch=1,
        grid=(wide + 1,),
        in_specs=[
            full,
            full,
            pl.BlockSpec((rows, tile), lambda j, s: (0, jnp.minimum(j, wide - 1))),
            pl.BlockSpec((rows, tile), lambda j, s: (0, 0)),
        ],
        out_specs=[block, block],
        scratch_shapes=[pltpu.VMEM((tall, tile), F32), pltpu.VMEM((tall, rows), BF)],
    )
    return pl.pallas_call(
        joint_kernel,
        grid_spec=grid_spec,
        out_shape=[shape, shape],
        compiler_params=params(1),
        cost_estimate=cost(
            2 * rows * tall * tile * (wide + 1),
            2 * (tall + rows) * tile * (wide + 1) + 4 * rows * tall,
            longer=8,
        ),
        name="joint_gradient",
    )(source, left, last_left, right, last_right)


def tall_kernel(slot_ref, left_ref, right_ref, keep_ref, send_ref, acc_ref):
    step = pl.program_id(0)
    half, piece, _ = keep_ref.shape
    here = left_ref.shape[1] // piece
    acc_ref[...] = dot(left_ref[...], right_ref[...], TN)
    for index in range(here):
        slot = slot_ref[step * here + index]
        part = acc_ref[index * piece : (index + 1) * piece, :].astype(BF)

        @pl.when(slot < half)
        def _():
            keep_ref[jnp.minimum(slot, half - 1)] = part

        @pl.when(slot >= half)
        def _():
            send_ref[jnp.maximum(slot - half, 0)] = part


def plain_tall_kernel(left_ref, right_ref, out_ref):
    out_ref[...] = dot(left_ref[...], right_ref[...], TN).astype(BF)


def tall_gradient(left, right, source, slot_of):
    rows, tall = left.shape
    width = right.shape[1]
    devices = source.shape[0]
    piece = tall // devices
    steps = tall // width
    left_block = pl.BlockSpec((rows, width), lambda j, *s: (0, j))
    right_block = pl.BlockSpec((rows, width), lambda j, *s: (0, 0))
    estimate = cost(2 * rows * tall * width, 2 * tall * width + 2 * rows * (tall + width))
    if piece % 16:
        whole = pl.pallas_call(
            plain_tall_kernel,
            grid=(steps,),
            in_specs=[left_block, right_block],
            out_specs=pl.BlockSpec((width, width), lambda j: (j, 0)),
            out_shape=jax.ShapeDtypeStruct((tall, width), BF),
            compiler_params=params(1),
            cost_estimate=estimate,
            name="tall_gradient",
        )(left, right)
        ordered = jnp.take(whole.reshape(devices, piece, width), source, axis=0)
        return (ordered[: devices // 2], ordered[devices // 2 :])
    block = pl.BlockSpec((devices // 2, piece, width), lambda j, s: (0, 0, 0))
    shape = jax.ShapeDtypeStruct((devices // 2, piece, width), BF)
    grid_spec = pltpu.PrefetchScalarGridSpec(
        num_scalar_prefetch=1,
        grid=(steps,),
        in_specs=[left_block, right_block],
        out_specs=[block, block],
        scratch_shapes=[pltpu.VMEM((width, width), F32)],
    )
    return pl.pallas_call(
        tall_kernel,
        grid_spec=grid_spec,
        out_shape=[shape, shape],
        compiler_params=params(1),
        cost_estimate=estimate,
        name="tall_gradient",
    )(slot_of, left, right)


def input_kernel(resid_ref, w_ref, *refs, groups):
    out_ref = refs[-1]
    width = resid_ref.shape[1]
    total = resid_ref[...]
    base = 0
    for grad_ref in refs[:groups]:
        here = grad_ref.shape[2]
        for part in range(3):
            total = total + dot(grad_ref[part], w_ref[:, pl.ds(part * width + base, here)], NT)
        base += here
    out_ref[...] = total.astype(BF)


def input_gradient(resid, gathered, grads, which, batch, filled):
    rows, width = resid.shape
    steps = rows // batch // ROWS
    base = which * steps
    return pl.pallas_call(
        functools.partial(input_kernel, groups=len(grads)),
        grid=(steps,),
        in_specs=[
            pl.BlockSpec((ROWS, width), lambda i: (base + i, 0)),
            pl.BlockSpec((width, 3 * width), lambda i: (0, 0), pipeline_mode=pl.Buffered(1)),
        ]
        + [pl.BlockSpec((3, ROWS, grad.shape[2]), lambda i: (0, base + i, 0)) for grad in grads]
        + [pl.BlockSpec(memory_space=pl.ANY)] * len(filled),
        out_specs=pl.BlockSpec((ROWS, width), lambda i: (base + i, 0)),
        out_shape=jax.ShapeDtypeStruct((rows, width), BF),
        input_output_aliases={2 + len(grads): 0} if filled else {},
        compiler_params=params(1),
        cost_estimate=cost(
            6 * rows * width * width // batch,
            (12 * rows * width + 6 * width * width) // batch,
            longer=64,
        ),
        name="input_gradient",
    )(resid, gathered, *grads, *filled)


def swap(value, mask, devices):
    return lax.ppermute(value, "dp", [(index, index ^ mask) for index in range(devices)])


def hold(value, *others):
    return lax.optimization_barrier((value, others))[0]


def masks_of(bits):
    found = [0]
    for bit in bits:
        found = found + [mask | (1 << bit) for mask in found]
    return found


def relative_order(order):
    relative = [0]
    for bits in order:
        relative = [base | mask for base in relative for mask in masks_of(bits)]
    return relative


def stage_orders(devices):
    bits = devices.bit_length() - 1
    rest = [(bit,) for bit in range(3, bits)]
    low = [(bit,) for bit in range(min(3, bits))]
    by_x = low + rest
    by_y = low[:1] + low[1:][::-1] + rest
    middle_bits = [tuple(range(1, min(3, bits)))] if bits > 1 else []
    outward = (low[:1] + middle_bits + rest)[::-1]
    high = range(3, bits)
    pairs = [tuple(high[at : at + 2]) for at in range(0, len(high), 2)]
    return by_x, by_y, low[:1] + middle_bits + pairs, outward


class Reduce:
    def __init__(self, keep, send, order, devices):
        self.order, self.devices, self.at = order, devices, 0
        self.parts = [keep, send]
        self.terms = None

    def send(self):
        masks = masks_of(self.order[self.at])
        self.terms = [self.parts[0]] + [
            swap(part, mask, self.devices) for part, mask in zip(self.parts[1:], masks[1:])
        ]
        self.at += 1
        return self

    def total(self, begin, size):
        result = self.terms[0][begin : begin + size].astype(F32)
        for term in self.terms[1:]:
            result = result + term[begin : begin + size].astype(F32)
        return result

    def join(self):
        ways = len(masks_of(self.order[self.at]))
        size = self.terms[0].shape[0] // ways
        self.parts = [self.total(way * size, size).astype(BF) for way in range(ways)]
        return self

    def after(self, *values):
        self.terms = list(lax.optimization_barrier((tuple(self.terms), values))[0])
        return self

    def finish(self):
        if self.terms is None:
            self.send()
        while self.at < len(self.order):
            self.join().send()
        return self.total(0, 1)[0]


class Gather:
    def __init__(self, shard, order, devices):
        self.order, self.devices, self.at = order, devices, 0
        self.held = shard[None]
        self.taken = None

    def send(self):
        masks = masks_of(self.order[self.at])
        self.taken = [swap(self.held, mask, self.devices) for mask in masks[1:]]
        self.at += 1
        return self

    def join(self):
        self.held = jnp.concatenate([self.held] + self.taken, axis=0)
        return self


def lay_pairs_kernel(index_ref, odd_ref, held_ref, taken_ref, out_ref):
    half, piece, _ = held_ref.shape
    odd = odd_ref[0] == 1
    for slot in range(half):
        mine = held_ref[slot].astype(F32)
        other = taken_ref[slot].astype(F32)
        both = jnp.concatenate(
            [jnp.where(odd, other, mine), jnp.where(odd, mine, other)], axis=0
        ).astype(BF)
        begin = pl.multiple_of((index_ref[slot] // 2) * (2 * piece), 16)
        out_ref[pl.ds(begin, 2 * piece), :] = both


def lay_out(gather, me):
    held, taken = gather.held, gather.taken[0]
    half, piece, columns = held.shape
    devices = 2 * half
    relative = [0]
    for bits in gather.order[:-1]:
        relative = [base | mask for mask in masks_of(bits) for base in relative]
    index = jnp.asarray(relative, jnp.int32) ^ me
    if piece % 8:
        where = [0] * devices
        for slot, value in enumerate(relative):
            where[value], where[value ^ 1] = slot, half + slot
        natural = jnp.take(jnp.asarray(where, jnp.int32), jnp.arange(devices, dtype=jnp.int32) ^ me)
        both = jnp.concatenate([held, taken], axis=0)
        return jnp.take(both, natural, axis=0).reshape(devices * piece, columns)
    tile = columns // 5 if columns % (5 * LANES) == 0 else columns
    block = pl.BlockSpec((half, piece, tile), lambda i, *s: (0, 0, i))
    grid_spec = pltpu.PrefetchScalarGridSpec(
        num_scalar_prefetch=2,
        grid=(columns // tile,),
        in_specs=[block, block],
        out_specs=pl.BlockSpec((devices * piece, tile), lambda i, *s: (0, i)),
    )
    return pl.pallas_call(
        lay_pairs_kernel,
        grid_spec=grid_spec,
        out_shape=jax.ShapeDtypeStruct((devices * piece, columns), BF),
        compiler_params=params(1),
        cost_estimate=cost(devices * piece * columns, 4 * devices * piece * columns),
        name="lay_out",
    )(index, (me & 1).reshape(1), held, taken)


def adamw(weight, grad, first, second, decay, rate):
    new_first = BETA_ONE * first + (1.0 - BETA_ONE) * grad
    new_second = BETA_TWO * second + (1.0 - BETA_TWO) * grad * grad
    corrected = new_first / (1.0 - BETA_ONE**STEP)
    scale_sq = new_second / (1.0 - BETA_TWO**STEP)
    new_weight = weight - rate * (corrected / (jnp.sqrt(scale_sq) + EPSILON_ADAM) + decay * weight)
    return (new_first, new_second, new_weight)


def on_device(
    hidden_in,
    lengths,
    cotangent,
    proj_qkv,
    proj_attn,
    proj_up,
    proj_down,
    vectors,
    first_qkv,
    first_attn,
    first_up,
    first_down,
    first_vectors,
    second_qkv,
    second_attn,
    second_up,
    second_down,
    second_vectors,
):
    devices = lax.axis_size("dp")
    me = lax.axis_index("dp")
    width = hidden_in.shape[1]
    piece = proj_qkv.shape[0]
    inner = proj_up.shape[1]
    batch = lengths.shape[0]
    by_x, by_y, both, outward = stage_orders(devices)

    def source_of(order):
        return jnp.asarray(relative_order(order), jnp.int32) ^ me

    slots = [0] * devices
    for slot, value in enumerate(relative_order(by_x)):
        slots[value] = slot
    slot_of = jnp.take(jnp.asarray(slots, jnp.int32), jnp.arange(devices, dtype=jnp.int32) ^ me)

    entries = vectors.shape[0] // piece
    ratio = inner // width
    down_columns = proj_down.astype(BF).reshape(ratio, piece, width).transpose(1, 0, 2)
    wide = lax.all_gather(
        jnp.concatenate(
            [proj_up.astype(BF), down_columns.reshape(piece, inner), proj_attn.astype(BF)], axis=1
        ),
        "dp",
        axis=0,
        tiled=True,
    )
    shard = jnp.concatenate(
        [
            proj_qkv.astype(BF),
            jnp.pad(vectors.astype(BF).reshape(piece, entries), ((0, 0), (0, 2 * LANES - entries))),
        ],
        axis=1,
    )
    qkv = Gather(shard, outward, devices)
    for _ in range(len(outward) - 1):
        qkv.send().join()
    qkv.send()
    gathered = lay_out(qkv, me)
    vec = gathered[:, 3 * width : 3 * width + entries].astype(F32).reshape(-1, width)

    packed = project_qkv(hidden_in, gathered, vec)
    filled = ()
    for which in range(batch):
        filled = attend_forward(packed, lengths, width, which, filled)
    mixed, lse = filled
    output, first_low, active, grad_upper, grad_branch, grad_attn, grad_mixed, grad_one, sums = middle(
        hidden_in, mixed, cotangent, lengths, wide, vec, piece
    )

    total = Reduce(*tall_gradient(active, grad_branch, source_of(by_x), slot_of), by_x, devices)
    total.send()
    grad_upper = hold(grad_upper, total.parts)
    joint = Reduce(
        *joint_gradient(first_low, grad_upper, mixed, grad_attn, source_of(by_y)), by_y, devices
    )
    total.after(joint.parts)
    joint.parts = list(hold(tuple(joint.parts), *total.terms))
    joint.send()
    total.join()
    joint.join()
    grad_mixed = hold(grad_mixed, total.parts, joint.parts)
    total.send()
    joint.send()
    part = ()
    for which in range(batch):
        part = (attend_backward(packed, lengths, lse, grad_mixed, which, part),)
    for chain in (joint, total):
        chain.after(part).join()
    left = hold(hidden_in, joint.parts, total.parts)
    for chain in (joint, total):
        chain.send()
    keep, send, part_sums = weight_gradient(left, part[0], source_of(both), sums=True)
    vector_sums = jnp.concatenate([part_sums[0, :1], part_sums[2, :1], sums[2:]], axis=0)
    ordered = jnp.take(vector_sums.reshape(devices, piece, entries), source_of(both), axis=0)
    ordered = jnp.pad(ordered.astype(BF), ((0, 0), (0, 0), (0, LANES - entries)))
    keep = jnp.concatenate([keep, ordered[: devices // 2]], axis=2)
    send = jnp.concatenate([send, ordered[devices // 2 :]], axis=2)
    narrow = Reduce(keep, send, both, devices).send()
    grad_one = hold(grad_one, send)
    filled = ()
    for which in range(batch):
        if which == batch - 1:
            for chain in (narrow, joint, total):
                chain.after(filled).join()
            grad_one = hold(grad_one, *(chain.parts for chain in (narrow, joint, total)))
            for chain in (narrow, joint, total):
                chain.send()
        filled = (input_gradient(grad_one, gathered, part, which, batch, filled),)
    input_grad = filled[0]
    for chain in (joint, total, narrow):
        chain.after(filled)

    total_narrow = narrow.finish()
    total_qkv = total_narrow[:, : 3 * width]
    total_vectors = total_narrow[:, 3 * width : 3 * width + entries].reshape(-1)
    total_wide = joint.finish()
    total_up, total_attn = total_wide[:, :inner], total_wide[:, inner:]
    total_down = total.finish()

    m_qkv, v_qkv, w_qkv = adamw(proj_qkv, total_qkv, first_qkv, second_qkv, WEIGHT_DECAY, LEARN_RATE)
    m_attn, v_attn, w_attn = adamw(
        proj_attn, total_attn, first_attn, second_attn, WEIGHT_DECAY, LEARN_RATE
    )
    m_up, v_up, w_up = adamw(proj_up, total_up, first_up, second_up, WEIGHT_DECAY, LEARN_RATE)
    m_down, v_down, w_down = adamw(
        proj_down, total_down, first_down, second_down, WEIGHT_DECAY, LEARN_RATE
    )
    m_vec, v_vec, w_vec = adamw(
        vectors, total_vectors, first_vectors, second_vectors, 0.0, LEARN_RATE_VECTOR
    )
    return (
        output,
        input_grad,
        m_qkv,
        v_qkv,
        w_qkv,
        m_attn,
        v_attn,
        w_attn,
        m_up,
        v_up,
        w_up,
        m_down,
        v_down,
        w_down,
        m_vec,
        v_vec,
        w_vec,
    )


def solution(mesh):
    rows, flat = P("dp", None), P("dp")
    return jax.shard_map(
        on_device,
        mesh=mesh,
        in_specs=(rows, flat, rows) + (rows, rows, rows, rows, flat) * 3,
        out_specs=(rows, rows) + (rows,) * 12 + (flat,) * 3,
        check_vma=False,
    )
```

```python
import functools
import math

import jax
import jax.numpy as jnp
from jax import lax
from jax.experimental import pallas as pl
from jax.experimental.pallas import tpu as pltpu
from jax.sharding import PartitionSpec as P

HEAD = 64
STEP = 10

EPSILON_NORM = 1e-05
BETA_ONE = 0.9
BETA_TWO = 0.999
LEARN_RATE = 0.1
LEARN_RATE_VECTOR = 0.4
WEIGHT_DECAY = 0.01
EPSILON_ADAM = 1e-08

LANES = 128
ROWS = 256
VMEM_BYTES = 56 * 1024 * 1024
BF = jnp.bfloat16
F32 = jnp.float32

NN = (((1,), (0,)), ((), ()))
NT = (((1,), (1,)), ((), ()))
TN = (((0,), (0,)), ((), ()))


def dot(left, right, dims=NN):
    return lax.dot_general(left, right, dims, preferred_element_type=F32)


def params(grid_rank):
    return pltpu.CompilerParams(
        dimension_semantics=("arbitrary",) * grid_rank, vmem_limit_bytes=VMEM_BYTES
    )


def cost(flops, moved, exps=0, longer=1):
    return pl.CostEstimate(
        flops=longer * int(flops), bytes_accessed=int(moved), transcendentals=int(exps)
    )


def qkv_kernel(x_ref, w_ref, vec_ref, out_ref):
    width = x_ref.shape[1]
    x = x_ref[...]
    for part in range(3):
        cols = pl.ds(part * width, width)
        value = dot(x, w_ref[:, cols])
        if part == 0:
            value = value + vec_ref[0:1, :]
        if part == 2:
            value = value + vec_ref[1:2, :]
        out_ref[:, cols] = value.astype(BF)


def project_qkv(x, gathered, vec):
    rows, width = x.shape
    return pl.pallas_call(
        qkv_kernel,
        grid=(rows // ROWS,),
        in_specs=[
            pl.BlockSpec((ROWS, width), lambda i: (i, 0)),
            pl.BlockSpec((width, 3 * width), lambda i: (0, 0), pipeline_mode=pl.Buffered(1)),
            pl.BlockSpec(vec.shape, lambda i: (0, 0)),
        ],
        out_specs=pl.BlockSpec((ROWS, 3 * width), lambda i: (i, 0)),
        out_shape=jax.ShapeDtypeStruct((rows, 3 * width), BF),
        compiler_params=params(1),
        cost_estimate=cost(6 * rows * width * width, 2 * (4 * rows * width + 3 * width * width)),
        name="project_qkv",
    )(x, gathered, vec)


def masked_scores(query, keyset, length, head):
    lane = lax.broadcasted_iota(jnp.int32, query.shape, 1)
    alive = lax.broadcasted_iota(jnp.int32, query.shape, 0) < length
    mine = (lane < HEAD) if head == 0 else (lane >= HEAD)
    spare = lane == (HEAD if head == 0 else 0)
    zeros = jnp.zeros(query.shape, F32)
    adding = jnp.where(alive, zeros, -1e30)
    key_side = jnp.where(mine, keyset.astype(F32), jnp.where(spare, adding, zeros)).astype(BF)
    query_side = jnp.where(mine, query.astype(F32), jnp.where(spare, 1.0, 0.0)).astype(BF)
    return dot(key_side, query_side, NT)


def attend_kernel(len_ref, q_ref, k_ref, v_ref, *refs, which):
    out_ref, lse_ref = refs[-2:]
    length = len_ref[which]
    seq = q_ref.shape[0]
    query = q_ref[...] * jnp.asarray(1.0 / math.sqrt(HEAD), BF)
    keyset = k_ref[...]
    val_t = v_ref[...].T
    mixed = []
    for head in range(2):
        scores = masked_scores(query, keyset, length, head)
        highest = jnp.max(scores, axis=0, keepdims=True)
        expo = jnp.exp(scores - highest)
        summed = jnp.sum(expo, axis=0, keepdims=True)
        probs = (expo * (1.0 / summed)).astype(BF)
        mixed.append(dot(val_t[head * HEAD : (head + 1) * HEAD], probs))
        lse_ref[0, head : head + 1, :] = highest + jnp.log(summed)
    out_ref[...] = jnp.concatenate(mixed, axis=0).T.astype(BF)


def attend_forward(packed, lengths, width, which, filled):
    rows = packed.shape[0]
    batch = lengths.shape[0]
    seq = rows // batch
    pairs = width // LANES
    grid_spec = pltpu.PrefetchScalarGridSpec(
        num_scalar_prefetch=1,
        grid=(pairs,),
        in_specs=[
            pl.BlockSpec((seq, LANES), lambda h, ln: (which, h)),
            pl.BlockSpec((seq, LANES), lambda h, ln: (which, pairs + h)),
            pl.BlockSpec((seq, LANES), lambda h, ln: (which, 2 * pairs + h)),
        ]
        + [pl.BlockSpec(memory_space=pl.ANY)] * len(filled),
        out_specs=[
            pl.BlockSpec((seq, LANES), lambda h, ln: (which, h)),
            pl.BlockSpec((1, 2, seq), lambda h, ln: (which * pairs + h, 0, 0)),
        ],
    )
    return pl.pallas_call(
        functools.partial(attend_kernel, which=which),
        grid_spec=grid_spec,
        out_shape=[
            jax.ShapeDtypeStruct((rows, width), BF),
            jax.ShapeDtypeStruct((batch * pairs, 2, seq), F32),
        ],
        input_output_aliases={4 + index: index for index in range(len(filled))},
        compiler_params=params(1),
        cost_estimate=cost(16 * seq * seq * width, 8 * seq * width, seq * seq * width // HEAD),
        name="attend_forward",
    )(lengths, packed, packed, packed, *filled)


def attend_back_kernel(len_ref, q_ref, k_ref, v_ref, g_ref, lse_ref, *refs, which):
    out_ref = refs[-1]
    length = len_ref[which]
    seq = q_ref.shape[0]
    factor = 1.0 / math.sqrt(HEAD)
    query = q_ref[...] * jnp.asarray(factor, BF)
    keyset = k_ref[...]
    valset = v_ref[...]
    grad = g_ref[...]
    key_t = keyset.T
    lane = lax.broadcasted_iota(jnp.int32, (seq, LANES), 1)
    grad_q = []
    grad_k = 0.0
    grad_v = 0.0
    for head in range(2):
        mine = (lane < HEAD) if head == 0 else (lane >= HEAD)
        query_h = jnp.where(mine, query, jnp.zeros_like(query))
        grad_h = jnp.where(mine, grad, jnp.zeros_like(grad))
        scores = masked_scores(query, keyset, length, head)
        probs = jnp.exp(scores - lse_ref[0, head : head + 1, :])
        grad_probs = dot(valset, grad_h, NT)
        total = jnp.sum(probs * grad_probs, axis=0, keepdims=True)
        grad_scores = (probs * (grad_probs - total)).astype(BF)
        grad_v = grad_v + dot(probs.astype(BF), grad_h)
        grad_k = grad_k + dot(grad_scores, query_h)
        grad_q.append(dot(key_t[head * HEAD : (head + 1) * HEAD], grad_scores))
    out_ref[0] = (jnp.concatenate(grad_q, axis=0).T * factor).astype(BF)
    out_ref[1] = grad_k.astype(BF)
    out_ref[2] = grad_v.astype(BF)


def attend_backward(packed, lengths, lse, grad_mixed, which, filled):
    rows, width = grad_mixed.shape
    batch = lengths.shape[0]
    seq = rows // batch
    pairs = width // LANES
    base, here = 0, pairs
    grid_spec = pltpu.PrefetchScalarGridSpec(
        num_scalar_prefetch=1,
        grid=(here,),
        in_specs=[
            pl.BlockSpec((seq, LANES), lambda h, ln: (which, base + h)),
            pl.BlockSpec((seq, LANES), lambda h, ln: (which, pairs + base + h)),
            pl.BlockSpec((seq, LANES), lambda h, ln: (which, 2 * pairs + base + h)),
            pl.BlockSpec((seq, LANES), lambda h, ln: (which, base + h)),
            pl.BlockSpec((1, 2, seq), lambda h, ln: (which * pairs + base + h, 0, 0)),
        ]
        + [pl.BlockSpec(memory_space=pl.ANY)] * len(filled),
        out_specs=pl.BlockSpec((3, seq, LANES), lambda h, ln: (0, which, h)),
    )
    return pl.pallas_call(
        functools.partial(attend_back_kernel, which=which),
        grid_spec=grid_spec,
        out_shape=jax.ShapeDtypeStruct((3, rows, here * LANES), BF),
        input_output_aliases={6 + index: index for index in range(len(filled))},
        compiler_params=params(1),
        cost_estimate=cost(
            40 * seq * seq * here * LANES, 14 * seq * here * LANES, seq * seq * here * 2, 8
        ),
        name="attend_backward",
    )(lengths, packed, packed, packed, grad_mixed, lse, *filled)


def norm_forward(resid, gain, shift):
    centred = resid - jnp.mean(resid, axis=-1, keepdims=True)
    inverse = lax.rsqrt(jnp.mean(centred * centred, axis=-1, keepdims=True) + EPSILON_NORM)
    scaled = centred * inverse
    return (scaled * gain + shift, scaled, inverse)


def norm_backward(grad, scaled, inverse, gain):
    grad_scaled = grad * gain
    return inverse * (
        grad_scaled
        - jnp.mean(grad_scaled, axis=-1, keepdims=True)
        - scaled * jnp.mean(grad_scaled * scaled, axis=-1, keepdims=True)
    )


def column_sum(value):
    return jnp.sum(value, axis=0, keepdims=True)


def middle_kernel(
    len_ref,
    x_ref,
    mixed_ref,
    cot_ref,
    w_attn,
    w_up,
    w_down,
    vec_ref,
    out_ref,
    first_ref,
    active_ref,
    upper_ref,
    branch_ref,
    attn_ref,
    gmix_ref,
    resid_ref,
    sum_ref,
    slope_ref,
    *down_refs,
    seq,
    piece,
):
    step = pl.program_id(0)
    rows, width = x_ref.shape
    chunks = w_up.shape[1] // width
    if down_refs:
        columns_ref, w_down = w_down, down_refs[0]

        @pl.when(step == 0)
        def _():
            def lay(pair, carry):
                begin = pl.multiple_of(pair * 2 * piece, 16)
                strips = [
                    columns_ref[pl.ds(begin, 2 * piece), pl.ds(j * width, width)].astype(F32)
                    for j in range(chunks)
                ]
                both = [strip[:piece] for strip in strips] + [strip[piece:] for strip in strips]
                there = pl.multiple_of(pair * 2 * chunks * piece, 16)
                w_down[pl.ds(there, 2 * chunks * piece), :] = jnp.concatenate(both, axis=0).astype(BF)
                return carry

            lax.fori_loop(0, width // (2 * piece), lay, 0)

    start = (step * rows) % seq
    length = len_ref[(step * rows) // seq]

    def vec(index):
        return vec_ref[index : index + 1, :]

    gain_one, shift_one, gain_two, shift_two = vec(8), vec(9), vec(10), vec(11)

    @pl.when(step == 0)
    def _():
        sum_ref[...] = jnp.zeros_like(sum_ref)

    resid_one = x_ref[...].astype(F32) + dot(mixed_ref[...], w_attn[...]) + vec(2)
    first, scaled_one, inverse_one = norm_forward(resid_one, gain_one, shift_one)
    first_low = first.astype(BF)
    first_ref[...] = first_low
    total = first + vec(7)
    for j in range(chunks):
        cols = pl.ds(j * width, width)
        upper = dot(first_low, w_up[:, cols]) + vec(3 + j)
        half = 0.5 + 0.5 * lax.erf(upper * (1.0 / math.sqrt(2.0)))
        active = (upper * half).astype(BF)
        active_ref[:, cols] = active
        slope_ref[:, cols] = half + upper * jnp.exp(-0.5 * upper * upper) * (
            1.0 / math.sqrt(2.0 * math.pi)
        )
        total = total + dot(active, w_down[cols, :])
    output, scaled_two, inverse_two = norm_forward(total, gain_two, shift_two)
    out_ref[...] = output.astype(BF)

    @pl.when(start < length)
    def _():
        alive = lax.broadcasted_iota(jnp.int32, (rows, 1), 0) + start < length
        grad_out = jnp.where(alive, cot_ref[...].astype(F32), 0.0)
        grad_two = norm_backward(grad_out, scaled_two, inverse_two, gain_two)
        branch = grad_two.astype(BF)
        branch_ref[...] = branch
        grad_first = grad_two
        for j in range(chunks):
            cols = pl.ds(j * width, width)
            grad_upper = (dot(branch, w_down[cols, :], NT) * slope_ref[:, cols]).astype(BF)
            upper_ref[:, cols] = grad_upper
            sum_ref[3 + j : 4 + j, :] += column_sum(grad_upper.astype(F32))
            grad_first = grad_first + dot(grad_upper, w_up[:, cols], NT)
        grad_one = norm_backward(grad_first, scaled_one, inverse_one, gain_one)
        resid_ref[...] = grad_one
        grad_attn = grad_one.astype(BF)
        attn_ref[...] = grad_attn
        gmix_ref[...] = dot(grad_attn, w_attn[...], NT).astype(BF)
        sum_ref[2:3, :] += column_sum(grad_attn.astype(F32))
        sum_ref[7:8, :] += column_sum(branch.astype(F32))
        sum_ref[8:9, :] += column_sum(grad_first * scaled_one)
        sum_ref[9:10, :] += column_sum(grad_first)
        sum_ref[10:11, :] += column_sum(grad_out * scaled_two)
        sum_ref[11:12, :] += column_sum(grad_out)

    @pl.when(start >= length)
    def _():
        upper_ref[...] = jnp.zeros_like(upper_ref)
        branch_ref[...] = jnp.zeros_like(branch_ref)
        attn_ref[...] = jnp.zeros_like(attn_ref)
        gmix_ref[...] = jnp.zeros_like(gmix_ref)
        resid_ref[...] = jnp.zeros_like(resid_ref)


def middle(x, mixed, cotangent, lengths, gathered, vec, piece):
    rows, width = x.shape
    inner = (gathered.shape[1] - width) // 2
    ratio = inner // width
    if piece % 8:
        w_down = gathered[:, inner + width :].reshape(width // piece, piece, ratio, width)
        w_down = w_down.transpose(0, 2, 1, 3).reshape(inner, width)
        down_block = (inner, width), 0
    else:
        w_down = gathered
        down_block = (width, inner), 1
    seq = rows // lengths.shape[0]
    once = pl.Buffered(1)
    thin = pl.BlockSpec((ROWS, width), lambda i, ln: (i, 0))
    wide = pl.BlockSpec((ROWS, inner), lambda i, ln: (i, 0))
    grid_spec = pltpu.PrefetchScalarGridSpec(
        num_scalar_prefetch=1,
        grid=(rows // ROWS,),
        in_specs=[
            thin,
            thin,
            thin,
            pl.BlockSpec((width, width), lambda i, ln: (0, 2 * ratio), pipeline_mode=once),
            pl.BlockSpec((width, inner), lambda i, ln: (0, 0), pipeline_mode=once),
            pl.BlockSpec(down_block[0], lambda i, ln: (0, down_block[1]), pipeline_mode=once),
            pl.BlockSpec(vec.shape, lambda i, ln: (0, 0)),
        ],
        out_specs=[
            thin,
            thin,
            wide,
            wide,
            thin,
            thin,
            thin,
            thin,
            pl.BlockSpec(vec.shape, lambda i, ln: (0, 0)),
        ],
        scratch_shapes=[pltpu.VMEM((ROWS, inner), F32)]
        + ([] if piece % 8 else [pltpu.VMEM((inner, width), BF)]),
    )
    low = jax.ShapeDtypeStruct((rows, width), BF)
    low_wide = jax.ShapeDtypeStruct((rows, inner), BF)
    return pl.pallas_call(
        functools.partial(middle_kernel, seq=seq, piece=piece),
        grid_spec=grid_spec,
        out_shape=[
            low,
            low,
            low_wide,
            low_wide,
            low,
            low,
            low,
            jax.ShapeDtypeStruct((rows, width), F32),
            jax.ShapeDtypeStruct(vec.shape, F32),
        ],
        compiler_params=params(1),
        cost_estimate=cost(
            8 * rows * width * inner + 4 * rows * width * width,
            rows * (4 * inner + 20 * width) + 4 * width * inner,
            2 * rows * inner,
        ),
        name="middle",
    )(lengths, x, mixed, cotangent, gathered, gathered, w_down, vec)


def weight_kernel(src_ref, left_ref, right_ref, *refs, sums):
    keep_ref, send_ref, acc_ref, turned_ref = refs[0], refs[1], refs[-2], refs[-1]
    half, piece, _ = keep_ref.shape
    right = right_ref[0] if len(right_ref.shape) == 3 else right_ref[...]

    @pl.when(pl.program_id(0) == 0)
    def _():
        turned_ref[...] = left_ref[...].T

    acc_ref[...] = dot(turned_ref[...], right)
    if sums:
        refs[2][0] = jnp.broadcast_to(column_sum(right.astype(F32)), refs[2].shape[1:])
    for slot in range(half):
        for ref, offset in ((keep_ref, 0), (send_ref, half)):
            begin = pl.multiple_of(src_ref[offset + slot] * piece, 8)
            ref[slot] = acc_ref[pl.ds(begin, piece), :].astype(BF)


def plain_weight_kernel(left_ref, right_ref, out_ref, *refs):
    right = right_ref[0] if len(right_ref.shape) == 3 else right_ref[...]
    out_ref[...] = dot(left_ref[...], right, TN).astype(BF)
    if refs:
        refs[0][0] = jnp.broadcast_to(column_sum(right.astype(F32)), refs[0].shape[1:])


def weight_gradient(left, right, source, sums=False):
    rows, tall = left.shape
    devices = source.shape[0]
    piece = tall // devices
    if right.ndim == 3:
        steps, _, tile = right.shape
        right_block = pl.BlockSpec((1, rows, tile), lambda j, *s: (j, 0, 0))
    else:
        tile = min(right.shape[1], 768)
        steps = right.shape[1] // tile
        right_block = pl.BlockSpec((rows, tile), lambda j, *s: (0, j))
    left_block = pl.BlockSpec((rows, tall), lambda j, *s: (0, 0))
    extra_specs = [pl.BlockSpec((1, 8, tile), lambda j, *s: (j, 0, 0))] if sums else []
    extra_shapes = [jax.ShapeDtypeStruct((steps, 8, tile), F32)] if sums else []
    estimate = cost(
        2 * rows * tall * tile * steps,
        2 * tall * tile * steps + 2 * rows * (tall + tile * steps),
        longer=64,
    )
    if piece % 8:
        whole, *rest = pl.pallas_call(
            plain_weight_kernel,
            grid=(steps,),
            in_specs=[left_block, right_block],
            out_specs=[pl.BlockSpec((tall, tile), lambda j: (0, j))] + extra_specs,
            out_shape=[jax.ShapeDtypeStruct((tall, steps * tile), BF)] + extra_shapes,
            compiler_params=params(1),
            cost_estimate=estimate,
            name="weight_gradient",
        )(left, right)
        ordered = jnp.take(whole.reshape(devices, piece, steps * tile), source, axis=0)
        return (ordered[: devices // 2], ordered[devices // 2 :], *rest)
    block = pl.BlockSpec((devices // 2, piece, tile), lambda j, s: (0, 0, j))
    shape = jax.ShapeDtypeStruct((devices // 2, piece, steps * tile), BF)
    grid_spec = pltpu.PrefetchScalarGridSpec(
        num_scalar_prefetch=1,
        grid=(steps,),
        in_specs=[left_block, right_block],
        out_specs=[block, block] + extra_specs,
        scratch_shapes=[pltpu.VMEM((tall, tile), F32), pltpu.VMEM((tall, rows), BF)],
    )
    return pl.pallas_call(
        functools.partial(weight_kernel, sums=sums),
        grid_spec=grid_spec,
        out_shape=[shape, shape] + extra_shapes,
        compiler_params=params(1),
        cost_estimate=estimate,
        name="weight_gradient",
    )(source, left, right)


def joint_kernel(
    src_ref,
    left_ref,
    last_left_ref,
    right_ref,
    last_right_ref,
    keep_ref,
    send_ref,
    acc_ref,
    turned_ref,
):
    half, piece, _ = keep_ref.shape
    last = pl.num_programs(0) - 1

    @pl.when(pl.program_id(0) == 0)
    def _():
        turned_ref[...] = left_ref[...].T

    @pl.when(pl.program_id(0) < last)
    def _():
        acc_ref[...] = dot(turned_ref[...], right_ref[...])

    @pl.when(pl.program_id(0) == last)
    def _():
        acc_ref[...] = dot(last_left_ref[...], last_right_ref[...], TN)

    for slot in range(half):
        for ref, offset in ((keep_ref, 0), (send_ref, half)):
            begin = pl.multiple_of(src_ref[offset + slot] * piece, 8)
            ref[slot] = acc_ref[pl.ds(begin, piece), :].astype(BF)


def joint_gradient(left, right, last_left, last_right, source):
    rows, tall = left.shape
    devices = source.shape[0]
    piece = tall // devices
    tile = last_right.shape[1]
    wide = right.shape[1] // tile
    if piece % 8:
        one = weight_gradient(left, right, source)
        two = weight_gradient(last_left, last_right, source)
        return [jnp.concatenate(both, axis=2) for both in zip(one, two)]
    full = pl.BlockSpec((rows, tall), lambda j, s: (0, 0))
    block = pl.BlockSpec((devices // 2, piece, tile), lambda j, s: (0, 0, j))
    shape = jax.ShapeDtypeStruct((devices // 2, piece, (wide + 1) * tile), BF)
    grid_spec = pltpu.PrefetchScalarGridSpec(
        num_scalar_prefetch=1,
        grid=(wide + 1,),
        in_specs=[
            full,
            full,
            pl.BlockSpec((rows, tile), lambda j, s: (0, jnp.minimum(j, wide - 1))),
            pl.BlockSpec((rows, tile), lambda j, s: (0, 0)),
        ],
        out_specs=[block, block],
        scratch_shapes=[pltpu.VMEM((tall, tile), F32), pltpu.VMEM((tall, rows), BF)],
    )
    return pl.pallas_call(
        joint_kernel,
        grid_spec=grid_spec,
        out_shape=[shape, shape],
        compiler_params=params(1),
        cost_estimate=cost(
            2 * rows * tall * tile * (wide + 1),
            2 * (tall + rows) * tile * (wide + 1) + 4 * rows * tall,
            longer=8,
        ),
        name="joint_gradient",
    )(source, left, last_left, right, last_right)


def tall_kernel(slot_ref, left_ref, right_ref, keep_ref, send_ref, acc_ref):
    step = pl.program_id(0)
    half, piece, _ = keep_ref.shape
    here = left_ref.shape[1] // piece
    acc_ref[...] = dot(left_ref[...], right_ref[...], TN)
    for index in range(here):
        slot = slot_ref[step * here + index]
        part = acc_ref[index * piece : (index + 1) * piece, :].astype(BF)

        @pl.when(slot < half)
        def _():
            keep_ref[jnp.minimum(slot, half - 1)] = part

        @pl.when(slot >= half)
        def _():
            send_ref[jnp.maximum(slot - half, 0)] = part


def plain_tall_kernel(left_ref, right_ref, out_ref):
    out_ref[...] = dot(left_ref[...], right_ref[...], TN).astype(BF)


def tall_gradient(left, right, source, slot_of):
    rows, tall = left.shape
    width = right.shape[1]
    devices = source.shape[0]
    piece = tall // devices
    steps = tall // width
    left_block = pl.BlockSpec((rows, width), lambda j, *s: (0, j))
    right_block = pl.BlockSpec((rows, width), lambda j, *s: (0, 0))
    estimate = cost(2 * rows * tall * width, 2 * tall * width + 2 * rows * (tall + width))
    if piece % 16:
        whole = pl.pallas_call(
            plain_tall_kernel,
            grid=(steps,),
            in_specs=[left_block, right_block],
            out_specs=pl.BlockSpec((width, width), lambda j: (j, 0)),
            out_shape=jax.ShapeDtypeStruct((tall, width), BF),
            compiler_params=params(1),
            cost_estimate=estimate,
            name="tall_gradient",
        )(left, right)
        ordered = jnp.take(whole.reshape(devices, piece, width), source, axis=0)
        return (ordered[: devices // 2], ordered[devices // 2 :])
    block = pl.BlockSpec((devices // 2, piece, width), lambda j, s: (0, 0, 0))
    shape = jax.ShapeDtypeStruct((devices // 2, piece, width), BF)
    grid_spec = pltpu.PrefetchScalarGridSpec(
        num_scalar_prefetch=1,
        grid=(steps,),
        in_specs=[left_block, right_block],
        out_specs=[block, block],
        scratch_shapes=[pltpu.VMEM((width, width), F32)],
    )
    return pl.pallas_call(
        tall_kernel,
        grid_spec=grid_spec,
        out_shape=[shape, shape],
        compiler_params=params(1),
        cost_estimate=estimate,
        name="tall_gradient",
    )(slot_of, left, right)


def input_kernel(resid_ref, w_ref, *refs, groups):
    out_ref = refs[-1]
    width = resid_ref.shape[1]
    total = resid_ref[...]
    base = 0
    for grad_ref in refs[:groups]:
        here = grad_ref.shape[2]
        for part in range(3):
            total = total + dot(grad_ref[part], w_ref[:, pl.ds(part * width + base, here)], NT)
        base += here
    out_ref[...] = total.astype(BF)


def input_gradient(resid, gathered, grads, which, batch, filled):
    rows, width = resid.shape
    steps = rows // batch // ROWS
    base = which * steps
    return pl.pallas_call(
        functools.partial(input_kernel, groups=len(grads)),
        grid=(steps,),
        in_specs=[
            pl.BlockSpec((ROWS, width), lambda i: (base + i, 0)),
            pl.BlockSpec((width, 3 * width), lambda i: (0, 0), pipeline_mode=pl.Buffered(1)),
        ]
        + [pl.BlockSpec((3, ROWS, grad.shape[2]), lambda i: (0, base + i, 0)) for grad in grads]
        + [pl.BlockSpec(memory_space=pl.ANY)] * len(filled),
        out_specs=pl.BlockSpec((ROWS, width), lambda i: (base + i, 0)),
        out_shape=jax.ShapeDtypeStruct((rows, width), BF),
        input_output_aliases={2 + len(grads): 0} if filled else {},
        compiler_params=params(1),
        cost_estimate=cost(
            6 * rows * width * width // batch,
            (12 * rows * width + 6 * width * width) // batch,
            longer=64,
        ),
        name="input_gradient",
    )(resid, gathered, *grads, *filled)


def swap(value, mask, devices):
    return lax.ppermute(value, "dp", [(index, index ^ mask) for index in range(devices)])


def hold(value, *others):
    return lax.optimization_barrier((value, others))[0]


def masks_of(bits):
    found = [0]
    for bit in bits:
        found = found + [mask | (1 << bit) for mask in found]
    return found


def relative_order(order):
    relative = [0]
    for bits in order:
        relative = [base | mask for base in relative for mask in masks_of(bits)]
    return relative


def stage_orders(devices):
    bits = devices.bit_length() - 1
    rest = [(bit,) for bit in range(3, bits)]
    low = [(bit,) for bit in range(min(3, bits))]
    by_x = low + rest
    by_y = low[:1] + low[1:][::-1] + rest
    middle_bits = [tuple(range(1, min(3, bits)))] if bits > 1 else []
    outward = (low[:1] + middle_bits + rest)[::-1]
    high = range(3, bits)
    pairs = [tuple(high[at : at + 2]) for at in range(0, len(high), 2)]
    return by_x, by_y, low[:1] + middle_bits + pairs, outward


class Reduce:
    def __init__(self, keep, send, order, devices):
        self.order, self.devices, self.at = order, devices, 0
        self.parts = [keep, send]
        self.terms = None

    def send(self):
        masks = masks_of(self.order[self.at])
        self.terms = [self.parts[0]] + [
            swap(part, mask, self.devices) for part, mask in zip(self.parts[1:], masks[1:])
        ]
        self.at += 1
        return self

    def total(self, begin, size):
        result = self.terms[0][begin : begin + size].astype(F32)
        for term in self.terms[1:]:
            result = result + term[begin : begin + size].astype(F32)
        return result

    def join(self):
        ways = len(masks_of(self.order[self.at]))
        size = self.terms[0].shape[0] // ways
        self.parts = [self.total(way * size, size).astype(BF) for way in range(ways)]
        return self

    def after(self, *values):
        self.terms = list(lax.optimization_barrier((tuple(self.terms), values))[0])
        return self

    def finish(self):
        if self.terms is None:
            self.send()
        while self.at < len(self.order):
            self.join().send()
        return self.total(0, 1)[0]


class Gather:
    def __init__(self, shard, order, devices):
        self.order, self.devices, self.at = order, devices, 0
        self.held = shard[None]
        self.taken = None

    def send(self):
        masks = masks_of(self.order[self.at])
        self.taken = [swap(self.held, mask, self.devices) for mask in masks[1:]]
        self.at += 1
        return self

    def join(self):
        self.held = jnp.concatenate([self.held] + self.taken, axis=0)
        return self


def lay_pairs_kernel(index_ref, odd_ref, held_ref, taken_ref, out_ref):
    half, piece, _ = held_ref.shape
    odd = odd_ref[0] == 1
    for slot in range(half):
        mine = held_ref[slot].astype(F32)
        other = taken_ref[slot].astype(F32)
        both = jnp.concatenate(
            [jnp.where(odd, other, mine), jnp.where(odd, mine, other)], axis=0
        ).astype(BF)
        begin = pl.multiple_of((index_ref[slot] // 2) * (2 * piece), 16)
        out_ref[pl.ds(begin, 2 * piece), :] = both


def lay_out(gather, me):
    held, taken = gather.held, gather.taken[0]
    half, piece, columns = held.shape
    devices = 2 * half
    relative = [0]
    for bits in gather.order[:-1]:
        relative = [base | mask for mask in masks_of(bits) for base in relative]
    index = jnp.asarray(relative, jnp.int32) ^ me
    if piece % 8:
        where = [0] * devices
        for slot, value in enumerate(relative):
            where[value], where[value ^ 1] = slot, half + slot
        natural = jnp.take(jnp.asarray(where, jnp.int32), jnp.arange(devices, dtype=jnp.int32) ^ me)
        both = jnp.concatenate([held, taken], axis=0)
        return jnp.take(both, natural, axis=0).reshape(devices * piece, columns)
    tile = columns // 5 if columns % (5 * LANES) == 0 else columns
    block = pl.BlockSpec((half, piece, tile), lambda i, *s: (0, 0, i))
    grid_spec = pltpu.PrefetchScalarGridSpec(
        num_scalar_prefetch=2,
        grid=(columns // tile,),
        in_specs=[block, block],
        out_specs=pl.BlockSpec((devices * piece, tile), lambda i, *s: (0, i)),
    )
    return pl.pallas_call(
        lay_pairs_kernel,
        grid_spec=grid_spec,
        out_shape=jax.ShapeDtypeStruct((devices * piece, columns), BF),
        compiler_params=params(1),
        cost_estimate=cost(devices * piece * columns, 4 * devices * piece * columns),
        name="lay_out",
    )(index, (me & 1).reshape(1), held, taken)


def adamw(weight, grad, first, second, decay, rate):
    new_first = BETA_ONE * first + (1.0 - BETA_ONE) * grad
    new_second = BETA_TWO * second + (1.0 - BETA_TWO) * grad * grad
    corrected = new_first / (1.0 - BETA_ONE**STEP)
    scale_sq = new_second / (1.0 - BETA_TWO**STEP)
    new_weight = weight - rate * (corrected / (jnp.sqrt(scale_sq) + EPSILON_ADAM) + decay * weight)
    return (new_first, new_second, new_weight)


def on_device(
    hidden_in,
    lengths,
    cotangent,
    proj_qkv,
    proj_attn,
    proj_up,
    proj_down,
    vectors,
    first_qkv,
    first_attn,
    first_up,
    first_down,
    first_vectors,
    second_qkv,
    second_attn,
    second_up,
    second_down,
    second_vectors,
):
    devices = lax.axis_size("dp")
    me = lax.axis_index("dp")
    width = hidden_in.shape[1]
    piece = proj_qkv.shape[0]
    inner = proj_up.shape[1]
    batch = lengths.shape[0]
    by_x, by_y, both, outward = stage_orders(devices)

    def source_of(order):
        return jnp.asarray(relative_order(order), jnp.int32) ^ me

    slots = [0] * devices
    for slot, value in enumerate(relative_order(by_x)):
        slots[value] = slot
    slot_of = jnp.take(jnp.asarray(slots, jnp.int32), jnp.arange(devices, dtype=jnp.int32) ^ me)

    entries = vectors.shape[0] // piece
    ratio = inner // width
    down_columns = proj_down.astype(BF).reshape(ratio, piece, width).transpose(1, 0, 2)
    wide = lax.all_gather(
        jnp.concatenate(
            [proj_up.astype(BF), down_columns.reshape(piece, inner), proj_attn.astype(BF)], axis=1
        ),
        "dp",
        axis=0,
        tiled=True,
    )
    shard = jnp.concatenate(
        [
            proj_qkv.astype(BF),
            jnp.pad(vectors.astype(BF).reshape(piece, entries), ((0, 0), (0, 2 * LANES - entries))),
        ],
        axis=1,
    )
    qkv = Gather(shard, outward, devices)
    for _ in range(len(outward) - 1):
        qkv.send().join()
    qkv.send()
    gathered = lay_out(qkv, me)
    vec = gathered[:, 3 * width : 3 * width + entries].astype(F32).reshape(-1, width)

    packed = project_qkv(hidden_in, gathered, vec)
    filled = ()
    for which in range(batch):
        filled = attend_forward(packed, lengths, width, which, filled)
    mixed, lse = filled
    output, first_low, active, grad_upper, grad_branch, grad_attn, grad_mixed, grad_one, sums = middle(
        hidden_in, mixed, cotangent, lengths, wide, vec, piece
    )

    total = Reduce(*tall_gradient(active, grad_branch, source_of(by_x), slot_of), by_x, devices)
    total.send()
    grad_upper = hold(grad_upper, total.parts)
    joint = Reduce(
        *joint_gradient(first_low, grad_upper, mixed, grad_attn, source_of(by_y)), by_y, devices
    )
    total.after(joint.parts)
    joint.parts = list(hold(tuple(joint.parts), *total.terms))
    joint.send()
    total.join()
    joint.join()
    grad_mixed = hold(grad_mixed, total.parts, joint.parts)
    total.send()
    joint.send()
    part = ()
    for which in range(batch):
        part = (attend_backward(packed, lengths, lse, grad_mixed, which, part),)
    for chain in (joint, total):
        chain.after(part).join()
    left = hold(hidden_in, joint.parts, total.parts)
    for chain in (joint, total):
        chain.send()
    keep, send, part_sums = weight_gradient(left, part[0], source_of(both), sums=True)
    vector_sums = jnp.concatenate([part_sums[0, :1], part_sums[2, :1], sums[2:]], axis=0)
    ordered = jnp.take(vector_sums.reshape(devices, piece, entries), source_of(both), axis=0)
    ordered = jnp.pad(ordered.astype(BF), ((0, 0), (0, 0), (0, LANES - entries)))
    keep = jnp.concatenate([keep, ordered[: devices // 2]], axis=2)
    send = jnp.concatenate([send, ordered[devices // 2 :]], axis=2)
    send = hold(send, joint.terms, total.terms)
    narrow = Reduce(keep, send, both, devices).send().join()
    grad_one = hold(grad_one, narrow.parts)
    narrow.send()
    filled = ()
    for which in range(batch):
        if which == batch - 1:
            for chain in (joint, total):
                chain.after(filled).join()
            grad_one = hold(grad_one, joint.parts, total.parts)
            for chain in (joint, total):
                chain.send()
        filled = (input_gradient(grad_one, gathered, part, which, batch, filled),)
    input_grad = filled[0]
    for chain in (joint, total, narrow):
        chain.after(filled)

    total_narrow = narrow.finish()
    total_qkv = total_narrow[:, : 3 * width]
    total_vectors = total_narrow[:, 3 * width : 3 * width + entries].reshape(-1)
    total_wide = joint.finish()
    total_up, total_attn = total_wide[:, :inner], total_wide[:, inner:]
    total_down = total.finish()

    m_qkv, v_qkv, w_qkv = adamw(proj_qkv, total_qkv, first_qkv, second_qkv, WEIGHT_DECAY, LEARN_RATE)
    m_attn, v_attn, w_attn = adamw(
        proj_attn, total_attn, first_attn, second_attn, WEIGHT_DECAY, LEARN_RATE
    )
    m_up, v_up, w_up = adamw(proj_up, total_up, first_up, second_up, WEIGHT_DECAY, LEARN_RATE)
    m_down, v_down, w_down = adamw(
        proj_down, total_down, first_down, second_down, WEIGHT_DECAY, LEARN_RATE
    )
    m_vec, v_vec, w_vec = adamw(
        vectors, total_vectors, first_vectors, second_vectors, 0.0, LEARN_RATE_VECTOR
    )
    return (
        output,
        input_grad,
        m_qkv,
        v_qkv,
        w_qkv,
        m_attn,
        v_attn,
        w_attn,
        m_up,
        v_up,
        w_up,
        m_down,
        v_down,
        w_down,
        m_vec,
        v_vec,
        w_vec,
    )


def solution(mesh):
    rows, flat = P("dp", None), P("dp")
    return jax.shard_map(
        on_device,
        mesh=mesh,
        in_specs=(rows, flat, rows) + (rows, rows, rows, rows, flat) * 3,
        out_specs=(rows, rows) + (rows,) * 12 + (flat,) * 3,
        check_vma=False,
    )
```
